32 devices in a mesh: seq: 8 (over z, y), batch: 4 (over x, core).
Axes of the slice: x: 2, y: 2, z: 4, core: 2. Of those that a mesh axis runs over, the one named last changes fastest.
Arguments:
- inputs: bfloat16 [16, 1024, 768], P('batch', 'seq'), may hold values from -6 to 6
- gain_one: bfloat16 [768], replicated, may hold values from 0.5 to 1.5
- bias_one: bfloat16 [768], replicated, may hold values from -1.25 to 1.25
- project_weight: bfloat16 [768, 2304], replicated, may hold values from -0.21875 to 0.21875
- project_bias: bfloat16 [2304], replicated, may hold values from -0.3125 to 0.3125
- query_map: bfloat16 [12, 64, 64], replicated, may hold values from -0.75 to 0.75
- key_map: bfloat16 [12, 64, 64], replicated, may hold values from -0.75 to 0.75
- output_weight: bfloat16 [768, 768], replicated, may hold values from -0.875 to 0.875
- output_bias: bfloat16 [768], replicated, may hold values from -1.25 to 1.25
- gain_two: bfloat16 [768], replicated, may hold values from 0.5 to 1.5
- bias_two: bfloat16 [768], replicated, may hold values from -1.25 to 1.25
- expand_weight: bfloat16 [768, 3072], replicated, may hold values from -0.21875 to 0.21875
- expand_bias: bfloat16 [3072], replicated, may hold values from -1.25 to 1.25
- contract_weight: bfloat16 [3072, 768], replicated, may hold values from -0.109375 to 0.109375
- contract_bias: bfloat16 [768], replicated, may hold values from -1.25 to 1.25
- bounds: int32 [16, 2], P('batch'), may hold values from 1 to 1023, as said below
- cotangent: bfloat16 [16, 1024, 768], P('batch', 'seq'), may hold values from -6 to 6
Outputs:
- block_output: bfloat16 [16, 1024, 768], P('batch', 'seq')
- input_grad: bfloat16 [16, 1024, 768], P('batch', 'seq')
- gain_one_grad: float32 [768], replicated
- bias_one_grad: float32 [768], replicated
- project_weight_grad: float32 [768, 2304], P('seq')
- project_bias_grad: float32 [2304], replicated
- query_map_grad: float32 [12, 64, 64], replicated
- key_map_grad: float32 [12, 64, 64], replicated
- output_weight_grad: float32 [768, 768], P('seq')
- output_bias_grad: float32 [768], replicated
- gain_two_grad: float32 [768], replicated
- bias_two_grad: float32 [768], replicated
- expand_weight_grad: float32 [768, 3072], P('seq')
- expand_bias_grad: float32 [3072], replicated
- contract_weight_grad: float32 [3072, 768], P('seq')
- contract_bias_grad: float32 [768], replicated
The draws below stay inside these ranges and needn't reach their ends.
Inputs may be any that keep to these rules, and one draw needn't show every extreme that they name: bounds[i, 0] < bounds[i, 1]; among the 4 sequences of each index of batch, at least at least one, which one drawn from the seed, has bounds[i, 0] < 128 and bounds[i, 1] >= 896.
All inputs are finite; a program needn't handle non-finite values.
Results may differ from the reference program's by a relative error of at most 0.011.
Values sent between devices are 32-bit elements; how exact they have to be, the bound alone decides.
A program may use at most 320 MiB of HBM per device.

```python
import math
import jax
import jax.numpy as jnp
from jax import lax

D = 768
HEADS = 12
HEAD = 64
FF = 3072
FEAT = 128
TOK_DEV = 128
MICRO = 4
SEQS = 16
LENGTH = 1024


def draw_bounds(key, part):
    key = jax.random.fold_in(key, 7)
    pick_key, first_key, second_key, early_key, later_key = jax.random.split(key, 5)
    groups = SEQS // MICRO
    chosen = jax.random.randint(pick_key, (groups, 1), 0, MICRO, dtype=jnp.int32)
    spanning = (jnp.arange(MICRO, dtype=jnp.int32)[None, :] == chosen).reshape(SEQS)
    span_first = jax.random.randint(early_key, (SEQS,), 1, TOK_DEV, dtype=jnp.int32)
    span_second = jax.random.randint(later_key, (SEQS,), LENGTH - TOK_DEV, LENGTH, dtype=jnp.int32)
    free_first = jax.random.randint(first_key, (SEQS,), 1, LENGTH - 1, dtype=jnp.int32)
    free_second = jax.random.randint(second_key, (SEQS,), free_first + 1, LENGTH, dtype=jnp.int32)
    first_bound = jnp.where(spanning, span_first, free_first)
    second_bound = jnp.where(spanning, span_second, free_second)
    return jnp.stack([first_bound, second_bound], axis=1)


def shard_levels(own_key, extent, shards, least, top_value):
    level = 1.0
    for position, parts in shards:
        heights = jax.random.uniform(jax.random.fold_in(jax.random.fold_in(own_key, 6), position), (parts,), jnp.float32, least / len(shards), top_value / len(shards))
        level = level * jnp.repeat(jnp.exp(heights), extent[position] // parts).reshape((-1,) + (1,) * (len(extent) - 1 - position))
    return level


def scatter_about(rng, dims, scale, reach, cuts=(), kind=jnp.bfloat16):
    values = jax.random.normal(rng, dims, jnp.float32) * scale
    if len(cuts) > 0:
        values = shard_levels(rng, dims, cuts, -0.22, 0.18) * values
    return jnp.clip(values, min=-reach, max=reach).astype(kind)


def setup_inputs(seed: int = 0) -> dict:
    key_of = jax.random.split(jax.random.key(seed), 18)
    return {
        "inputs": scatter_about(key_of[0], (SEQS, LENGTH, D), 1.0, 6.0, ((0, 4), (1, 8))),
        "gain_one": jnp.clip(1.0 + 0.1 * jax.random.normal(key_of[1], (D,), jnp.float32), 0.5, 1.5).astype(jnp.bfloat16),
        "bias_one": scatter_about(key_of[2], (D,), 0.2, 1.25),
        "project_weight": scatter_about(key_of[3], (D, 3 * D), D ** -0.5, 0.21875),
        "project_bias": scatter_about(key_of[4], (3 * D,), 0.05, 0.3125),
        "query_map": scatter_about(key_of[5], (HEADS, HEAD, HEAD), HEAD ** -0.5, 0.75),
        "key_map": scatter_about(key_of[6], (HEADS, HEAD, HEAD), HEAD ** -0.5, 0.75),
        "output_weight": scatter_about(key_of[7], (D, D), (D // 16) ** -0.5, 0.875),
        "output_bias": scatter_about(key_of[8], (D,), 0.2, 1.25),
        "gain_two": jnp.clip(1.0 + 0.1 * jax.random.normal(key_of[9], (D,), jnp.float32), 0.5, 1.5).astype(jnp.bfloat16),
        "bias_two": scatter_about(key_of[10], (D,), 0.2, 1.25),
        "expand_weight": scatter_about(key_of[11], (D, FF), D ** -0.5, 0.21875),
        "expand_bias": scatter_about(key_of[12], (FF,), 0.2, 1.25),
        "contract_weight": scatter_about(key_of[13], (FF, D), FF ** -0.5, 0.109375),
        "contract_bias": scatter_about(key_of[14], (D,), 0.2, 1.25),
        "bounds": draw_bounds(jax.random.fold_in(key_of[17], 71), 0),
        "cotangent": scatter_about(key_of[16], (SEQS, LENGTH, D), 1.0, 6.0, ((0, 4), (1, 8))),
    }


epsilon = 1e-05
precise = lax.Precision.HIGHEST

@jax.custom_vjp
def low(v):
    return lax.optimization_barrier(v.astype(jnp.bfloat16)).astype(jnp.float32)

@jax.custom_vjp
def low_back(v):
    return v

def low_keep(v):
    return (low(v), None)

def low_pass(kept, grad):
    return (grad,)

def back_keep(v):
    return (v, None)

def back_low(kept, grad):
    return (low(grad),)
low.defvjp(low_keep, low_pass)
low_back.defvjp(back_keep, back_low)

def layer_norm(values, gain_vector, shift_vector):
    centered = values - lax.optimization_barrier(jnp.mean(values, axis=-1, keepdims=True))
    spread = lax.optimization_barrier(jnp.mean(centered * centered, axis=-1, keepdims=True))
    return centered * lax.rsqrt(spread + epsilon) * gain_vector + shift_vector

def feature_map(vectors, weights):
    mapped = low_back(jnp.einsum('thd,hde->the', vectors, weights, precision=precise))
    return low(jnp.concatenate([jax.nn.softmax(mapped, axis=-1), jax.nn.softmax(-mapped, axis=-1)], axis=-1))

def doc_index(positions, bounds_row):
    return (positions >= bounds_row[0]).astype(jnp.int32) + (positions >= bounds_row[1]).astype(jnp.int32)

def linear_attention(feat_query, feat_key, value_rows, bounds_row):
    length = feat_query.shape[0]
    block_rows = math.gcd(length, 512)
    block_count = length // block_rows
    query_blocks = feat_query.reshape(block_count, block_rows, HEADS, FEAT)
    key_blocks = feat_key.reshape(block_count, block_rows, HEADS, FEAT)
    value_blocks = value_rows.reshape(block_count, block_rows, HEADS, HEAD)
    starts = jnp.arange(block_count, dtype=jnp.int32) * block_rows

    def block_step(carry_in, pieces):
        state_now, key_sum = carry_in
        query_block, key_block, value_block, block_start = pieces
        positions = block_start + jnp.arange(block_rows, dtype=jnp.int32)
        doc_ids = doc_index(positions, bounds_row)
        doc_prev = doc_index(block_start - 1, bounds_row)
        doc_last = doc_index(block_start + block_rows - 1, bounds_row)
        use_in = (doc_ids == doc_prev).astype(jnp.float32)
        in_last = (doc_ids == doc_last).astype(jnp.float32)
        keep_state = (doc_prev == doc_last).astype(jnp.float32)
        causal = positions[:, None] >= positions[None, :]
        attend_mask = (causal & (doc_ids[:, None] == doc_ids[None, :])).astype(jnp.float32)
        scores = jnp.einsum('thf,shf->hts', query_block, key_block, precision=precise) * attend_mask[None]
        numerator = jnp.einsum('hts,she->the', scores, value_block, precision=precise)
        numerator = numerator + use_in[:, None, None] * jnp.einsum('thf,hfe->the', query_block, state_now, precision=precise)
        denominator = jnp.transpose(lax.optimization_barrier(jnp.sum(scores, axis=-1))) + use_in[:, None] * jnp.einsum('thf,hf->th', query_block, key_sum, precision=precise)
        attended = numerator / denominator[:, :, None]
        weighted = key_block * in_last[:, None, None]
        new_state = jnp.einsum('thf,the->hfe', weighted, value_block, precision=precise) + keep_state * state_now
        new_sum = lax.optimization_barrier(jnp.sum(weighted, axis=0)) + keep_state * key_sum
        return ((new_state, new_sum), attended)
    start_carry = (jnp.zeros((HEADS, FEAT, HEAD), jnp.float32), jnp.zeros((HEADS, FEAT), jnp.float32))
    final_carry, outputs = lax.scan(jax.checkpoint(block_step), start_carry, (query_blocks, key_blocks, value_blocks, starts))
    return outputs.reshape(length, HEADS, HEAD)

def layer_forward(sequence_in, param_list, bounds_row):
    gain_one, bias_one, project_weight, project_bias, query_map, key_map, output_weight, output_bias, gain_two, bias_two, expand_weight, expand_bias, contract_weight, contract_bias = param_list
    length = sequence_in.shape[0]
    normed = low(layer_norm(sequence_in, gain_one, bias_one))
    projected = low(low_back(jnp.dot(normed, project_weight, precision=precise) + project_bias))
    queries = projected[:, :D].reshape(length, HEADS, HEAD)
    key_rows = projected[:, D:2 * D].reshape(length, HEADS, HEAD)
    value_rows = projected[:, 2 * D:].reshape(length, HEADS, HEAD)
    feat_query = feature_map(queries, query_map)
    feat_key = feature_map(key_rows, key_map)
    attended = low(linear_attention(feat_query, feat_key, value_rows, bounds_row).reshape(length, D))
    branch = low_back(jnp.dot(attended, output_weight, precision=precise) + output_bias)
    middle = sequence_in + branch
    normed_two = low(layer_norm(middle, gain_two, bias_two))
    expanded = low_back(jnp.dot(normed_two, expand_weight, precision=precise) + expand_bias)
    hidden = low(jax.nn.gelu(expanded, approximate=True))
    return middle + low_back(jnp.dot(hidden, contract_weight, precision=precise) + contract_bias)

def reference(inputs, gain_one, bias_one, project_weight, project_bias, query_map, key_map, output_weight, output_bias, gain_two, bias_two, expand_weight, expand_bias, contract_weight, contract_bias, bounds, cotangent):
    params = tuple((weight_array.astype(jnp.float32) for weight_array in (gain_one, bias_one, project_weight, project_bias, query_map, key_map, output_weight, output_bias, gain_two, bias_two, expand_weight, expand_bias, contract_weight, contract_bias)))

    def per_sequence(totals, pieces):
        sequence, grad_out, bounds_row = pieces

        def wrapped(sequence_in, param_list):
            return layer_forward(sequence_in, param_list, bounds_row)
        result, pullback = jax.vjp(wrapped, sequence.astype(jnp.float32), params)
        input_grad, param_grads = pullback(grad_out.astype(jnp.float32))
        return (jax.tree.map(jnp.add, totals, param_grads), (result.astype(jnp.bfloat16), input_grad.astype(jnp.bfloat16)))
    zeros_start = jax.tree.map(jnp.zeros_like, params)
    totals, (outputs, input_grads) = lax.scan(per_sequence, zeros_start, (inputs, cotangent, bounds))
    return (outputs, input_grads, totals[0], totals[1], totals[2], totals[3], totals[4], totals[5], totals[6], totals[7], totals[8], totals[9], totals[10], totals[11], totals[12], totals[13])
```

```python
from functools import partial

import jax
import jax.numpy as jnp
from jax import lax
from jax.experimental import pallas as pl
from jax.experimental.pallas import tpu as pltpu
from jax.sharding import PartitionSpec as P

epsilon = 1e-05
bfloat = jnp.bfloat16
single = jnp.float32
MESH = pl.DeviceIdType.MESH
VMEM_LIMIT = 56 * 1024 * 1024


def matmul(a, b, contract):
    return lax.dot_general(
        a, b, (((contract[0],), (contract[1],)), ((), ())), preferred_element_type=single
    )


def norm_forward(values, gain_vector, shift_vector):
    centered = values - jnp.mean(values, axis=-1, keepdims=True)
    inverse = lax.rsqrt(jnp.mean(centered * centered, axis=-1, keepdims=True) + epsilon)
    unit_rows = centered * inverse
    return (unit_rows * gain_vector + shift_vector, unit_rows, inverse)


def norm_backward(gradient, unit_rows, inverse, gain_vector):
    inner = gradient * gain_vector
    result = inverse * (
        inner
        - jnp.mean(inner, axis=-1, keepdims=True)
        - unit_rows * jnp.mean(inner * unit_rows, axis=-1, keepdims=True)
    )
    return (result, jnp.sum(gradient * unit_rows, axis=0), jnp.sum(gradient, axis=0))


def doc_number(positions, first_bound, second_bound):
    return (positions >= first_bound).astype(jnp.int32) + (positions >= second_bound).astype(
        jnp.int32
    )


def two_softmaxes(mapped):
    up = jnp.exp(mapped - jnp.max(mapped, axis=0, keepdims=True))
    down = jnp.exp(jnp.min(mapped, axis=0, keepdims=True) - mapped)
    return (
        up / jnp.sum(up, axis=0, keepdims=True),
        down / jnp.sum(down, axis=0, keepdims=True),
    )


def with_ones(rows):
    return jnp.concatenate([rows, jnp.ones((16, rows.shape[1]), rows.dtype)], axis=0)


def state_rows(state, micro, head_width):
    low = state[micro * head_width : (micro + 1) * head_width, :]
    count = state.shape[0] // (head_width + 2)
    total = state[count * head_width + micro : count * head_width + micro + 1, :]
    return jnp.concatenate([low, jnp.broadcast_to(total, (16, low.shape[1]))], axis=0)


def feature_kernel(micro_count, q_ref, k_ref, v_ref, qm_ref, km_ref, last_ref, fq_ref, fk_ref, state_ref):
    head_width = q_ref.shape[0]
    rows = q_ref.shape[1] // micro_count
    for source, weights, target in ((q_ref, qm_ref, fq_ref), (k_ref, km_ref, fk_ref)):
        mapped = matmul(weights[0], source[...], (0, 0))
        up, down = two_softmaxes(mapped)
        target[...] = jnp.concatenate([up, down], axis=0).astype(bfloat)
    wide = with_ones(v_ref[...]) * last_ref[...]
    sums = []
    for m in range(micro_count):
        part = slice(m * rows, (m + 1) * rows)
        local = matmul(wide[:, part], fk_ref[:, part], (1, 1))
        state_ref[0, m * head_width : (m + 1) * head_width, :] = local[:head_width]
        sums.append(local[head_width : head_width + 1])
    sums = jnp.concatenate(sums + sums, axis=0)
    state_ref[0, micro_count * head_width :, :] = sums


def attend_kernel(micro_count, fq_ref, fk_ref, v_ref, state_ref, mask_ref, use_ref, att_ref, low_ref, den_ref):
    head_width = v_ref.shape[0]
    rows = v_ref.shape[1] // micro_count
    wide = with_ones(v_ref[...])
    used = fq_ref[...] * use_ref[...]
    for m in range(micro_count):
        part = slice(m * rows, (m + 1) * rows)
        scores = matmul(fk_ref[:, part], fq_ref[:, part], (0, 0)) * mask_ref[m]
        state = state_rows(state_ref[0], m, head_width).astype(bfloat)
        numer = matmul(wide[:, part], scores.astype(bfloat), (1, 0)) + matmul(
            state, used[:, part], (1, 0)
        )
        denom = numer[head_width : head_width + 1]
        attended = numer[:head_width] / denom
        att_ref[:, part] = attended
        low_ref[:, part] = attended.astype(bfloat)
        den_ref[0, :, part] = denom


def score_grads(grad, attended, denom):
    inverse = 1.0 / denom
    numer_grad = grad * inverse
    denom_grad = -jnp.sum(grad * attended, axis=0, keepdims=True) * inverse
    pad = jnp.zeros((15, grad.shape[1]), single)
    return jnp.concatenate([numer_grad, denom_grad, pad], axis=0)


def state_grad_kernel(micro_count, grad_ref, att_ref, den_ref, fq_ref, use_ref, state_ref):
    head_width = grad_ref.shape[0]
    rows = grad_ref.shape[1] // micro_count
    wide = (score_grads(grad_ref[...], att_ref[...], den_ref[0]) * use_ref[...]).astype(bfloat)
    sums = []
    for m in range(micro_count):
        part = slice(m * rows, (m + 1) * rows)
        local = matmul(wide[:, part], fq_ref[:, part], (1, 1))
        state_ref[0, m * head_width : (m + 1) * head_width, :] = local[:head_width]
        sums.append(local[head_width : head_width + 1])
    sums = jnp.concatenate(sums + sums, axis=0)
    state_ref[0, micro_count * head_width :, :] = sums


def feature_backward(feat_grad, source, weights):
    head_width = source.shape[0]
    up, down = two_softmaxes(matmul(weights, source, (0, 0)))
    grad_up, grad_down = (feat_grad[:head_width], feat_grad[head_width:])
    mapped = up * (grad_up - jnp.sum(up * grad_up, axis=0, keepdims=True)) - down * (
        grad_down - jnp.sum(down * grad_down, axis=0, keepdims=True)
    )
    low = mapped.astype(bfloat)
    return (matmul(weights, low, (1, 0)), matmul(source, low, (1, 1)))


def backward_kernel(
    micro_count, q_ref, k_ref, v_ref, qm_ref, km_ref, fq_ref, fk_ref, grad_ref, att_ref, den_ref,
    state_ref, out_grad_ref, mask_ref, use_ref, last_ref, proj_ref, qmg_ref, kmg_ref, fqg, fkg,
):
    head_width = q_ref.shape[0]
    rows = q_ref.shape[1] // micro_count
    grads = score_grads(grad_ref[...], att_ref[...], den_ref[0])
    low_grads = grads.astype(bfloat)
    used_grads = (grads * use_ref[...]).astype(bfloat)
    wide = with_ones(v_ref[...])
    wide_last = wide * last_ref[...]
    for m in range(micro_count):
        part = slice(m * rows, (m + 1) * rows)
        fq, fk = (fq_ref[:, part], fk_ref[:, part])
        mask = mask_ref[m]
        scores = (matmul(fk, fq, (0, 0)) * mask).astype(bfloat)
        grad_scores = (matmul(wide[:, part], low_grads[:, part], (0, 0)) * mask).astype(bfloat)
        state = state_rows(state_ref[0], m, head_width).astype(bfloat)
        out_grad = state_rows(out_grad_ref[0], m, head_width)
        row = lax.broadcasted_iota(jnp.int32, out_grad.shape, 0)
        out_grad = jnp.where(row <= head_width, out_grad, 0.0).astype(bfloat)
        fqg[:, part] = matmul(fk, grad_scores, (1, 0)) + matmul(state, used_grads[:, part], (0, 0))
        fkg[:, part] = matmul(fq, grad_scores, (1, 1)) + matmul(out_grad, wide_last[:, part], (0, 0))
        value_grad = matmul(low_grads[:head_width, part], scores, (1, 1)) + matmul(
            out_grad[:head_width], fk * last_ref[:, part], (1, 0)
        )
        proj_ref[2, :, part] = value_grad.astype(bfloat)
    q_grad, qmg = feature_backward(fqg[...], q_ref[...], qm_ref[0])
    proj_ref[0] = q_grad.astype(bfloat)
    qmg_ref[0] = qmg
    k_grad, kmg = feature_backward(fkg[...], k_ref[...], km_ref[0])
    proj_ref[1] = k_grad.astype(bfloat)
    kmg_ref[0] = kmg


def scan_kernel(
    reverse, count, local_ref, mask_ref, out_ref, carry, onward, aside, beside,
    carry_send, carry_recv, side_send, side_recv,
):
    place, column = (lax.axis_index("seq"), lax.axis_index("batch"))
    high, low = (place // 2, lax.rem(place, 2))
    length = count // 2
    if reverse:
        lap = length - 1 - high
        ahead, behind = (place - 2, place + 2)
    else:
        lap = high
        ahead, behind = (place + 2, place - 2)
    partner = place + 1 - 2 * low
    first = lap == 0
    final = lap == length - 1
    chunks = local_ref.shape[0]
    barrier = pltpu.get_barrier_semaphore()

    @pl.when(jnp.logical_not(final))
    def _():
        pl.semaphore_signal(barrier, inc=1, device_id=(ahead, column), device_id_type=MESH)

    @pl.when(jnp.logical_not(first))
    def _():
        pl.semaphore_signal(barrier, inc=1, device_id=(behind, column), device_id_type=MESH)

    pl.semaphore_signal(barrier, inc=1, device_id=(partner, column), device_id_type=MESH)
    pl.semaphore_wait(
        barrier, 1 + jnp.where(first, 0, 1) + jnp.where(final, 0, 1)
    )

    def along(i):
        return pltpu.make_async_remote_copy(
            src_ref=onward.at[i], dst_ref=carry.at[i], send_sem=carry_send.at[i],
            recv_sem=carry_recv.at[i], device_id=(ahead, column), device_id_type=MESH,
        )

    def across(i):
        return pltpu.make_async_remote_copy(
            src_ref=aside.at[i], dst_ref=beside.at[i], send_sem=side_send.at[i],
            recv_sem=side_recv.at[i], device_id=(partner, column), device_id_type=MESH,
        )

    @pl.when(first)
    def _():
        carry[...] = jnp.zeros_like(carry)

    def one(i, _):
        @pl.when(jnp.logical_not(first))
        def _():
            along(i).wait_recv()

        state, local = (carry[i], local_ref[i])
        aside[i] = mask_ref[2] * state + mask_ref[3] * local
        across(i).start()

        @pl.when(jnp.logical_not(final))
        def _():
            onward[i] = mask_ref[0] * state + mask_ref[1] * local
            along(i).start()

        return 0

    lax.fori_loop(0, chunks, one, 0)

    def two(i, _):
        across(i).wait_recv()
        out_ref[i] = mask_ref[4] * carry[i] + beside[i]
        return 0

    lax.fori_loop(0, chunks, two, 0)

    def three(i, _):
        across(i).wait_send()

        @pl.when(jnp.logical_not(final))
        def _():
            along(i).wait_send()

        return 0

    lax.fori_loop(0, chunks, three, 0)


def scan_states(local, masks, count, reverse, identity):
    chunks = local.shape[0]
    whole = pl.BlockSpec(memory_space=pltpu.VMEM)
    return pl.pallas_call(
        partial(scan_kernel, reverse, count),
        out_shape=jax.ShapeDtypeStruct(local.shape, single),
        in_specs=[whole, whole],
        out_specs=whole,
        scratch_shapes=[pltpu.VMEM(local.shape, single)] * 4
        + [pltpu.SemaphoreType.DMA((chunks,))] * 4,
        compiler_params=pltpu.CompilerParams(
            collective_id=identity, has_side_effects=True, vmem_limit_bytes=VMEM_LIMIT
        ),
    )(local, masks)


def scan_masks(bounds, first_row, row_count, place, micro_count, head_width, reverse):
    def doc(position):
        return doc_number(position, bounds[:, 0], bounds[:, 1])

    low = lax.rem(place, 2)
    base = first_row - low * row_count
    step = 2 * row_count
    if reverse:
        low = 1 - low
        own_edge = doc(first_row)
        pair = doc(base + step - 1)
        ahead = doc(base - 1)
        inner = doc(base + row_count - 1)
    else:
        own_edge = doc(first_row + row_count - 1)
        pair = doc(base - 1)
        ahead = doc(base + step - 1)
        inner = doc(base + row_count - 1)
    if reverse:
        own_edge = doc(first_row - 1)
    one = jnp.ones((micro_count,), single)
    keep = (pair == inner).astype(single)
    masks = jnp.stack(
        [
            (pair == ahead).astype(single),
            (own_edge == ahead).astype(single),
            jnp.where(low == 0, keep, one),
            jnp.where(low == 0, one, 0 * one),
            jnp.where(low == 0, one, keep),
        ]
    )
    wide = jnp.concatenate([jnp.repeat(masks, head_width, axis=1), masks, masks], axis=1)
    return jnp.broadcast_to(wide[:, :, None], wide.shape + (2 * head_width,))


def per_device(
    inputs, gain_one, bias_one, project_weight, project_bias, query_map, key_map, output_weight,
    output_bias, gain_two, bias_two, expand_weight, expand_bias, contract_weight, contract_bias,
    bounds, cotangent,
):
    micro_count, row_count, model_width = inputs.shape
    head_count, head_width = (query_map.shape[0], query_map.shape[1])
    feat_width = 2 * head_width
    total_rows = micro_count * row_count
    count = lax.axis_size("seq")
    place = lax.axis_index("seq")
    first_row = place * row_count
    positions = first_row + jnp.arange(row_count, dtype=jnp.int32)
    first_bound, second_bound = (bounds[:, 0:1], bounds[:, 1:2])
    doc_ids = doc_number(positions[None, :], first_bound, second_bound)
    doc_prev = doc_number(first_row - 1, first_bound, second_bound)
    doc_last = doc_number(first_row + row_count - 1, first_bound, second_bound)
    use_in = (doc_ids == doc_prev).astype(single).reshape(1, total_rows)
    in_last = (doc_ids == doc_last).astype(single).reshape(1, total_rows)
    use_low, last_low = (use_in.astype(bfloat), in_last.astype(bfloat))
    causal = positions[:, None] <= positions[None, :]
    mask = (causal[None] & (doc_ids[:, :, None] == doc_ids[:, None, :])).astype(single)
    masks_forward = scan_masks(bounds, first_row, row_count, place, micro_count, head_width, False)
    masks_reverse = scan_masks(bounds, first_row, row_count, place, micro_count, head_width, True)

    flat_input = inputs.reshape(total_rows, model_width).astype(single)
    normed, unit_one, inverse_one = norm_forward(
        flat_input, gain_one.astype(single), bias_one.astype(single)
    )
    normed_low = normed.astype(bfloat)
    projected = (
        jnp.einsum("dc,rd->cr", project_weight, normed_low, preferred_element_type=single)
        + project_bias.astype(single)[:, None]
    ).astype(bfloat)

    head_rows = lambda offset: pl.BlockSpec((head_width, total_rows), lambda h: (h + offset, 0))
    map_spec = pl.BlockSpec((1, head_width, head_width), lambda h: (h, 0, 0))
    feat_spec = pl.BlockSpec((feat_width, total_rows), lambda h: (h, 0))
    line_spec = pl.BlockSpec((1, total_rows), lambda h: (0, 0))
    den_spec = pl.BlockSpec((1, 1, total_rows), lambda h: (h, 0, 0))
    state_height = micro_count * (head_width + 2)
    state_spec = pl.BlockSpec((1, state_height, feat_width), lambda h: (h, 0, 0))
    mask_spec = pl.BlockSpec((micro_count, row_count, row_count), lambda h: (0, 0, 0))
    q_spec, k_spec, v_spec = (head_rows(0), head_rows(head_count), head_rows(2 * head_count))
    feat_shape = jax.ShapeDtypeStruct((head_count * feat_width, total_rows), bfloat)
    state_shape = jax.ShapeDtypeStruct((head_count, state_height, feat_width), single)
    params = pltpu.CompilerParams(vmem_limit_bytes=VMEM_LIMIT)

    feat_query, feat_key, local_state = pl.pallas_call(
        partial(feature_kernel, micro_count),
        grid=(head_count,),
        in_specs=[q_spec, k_spec, v_spec, map_spec, map_spec, line_spec],
        out_specs=[feat_spec, feat_spec, state_spec],
        out_shape=[feat_shape, feat_shape, state_shape],
        compiler_params=params,
    )(projected, projected, projected, query_map, key_map, last_low)
    state_in = scan_states(local_state, masks_forward, count, False, 1)
    attended, attended_low, denominator = pl.pallas_call(
        partial(attend_kernel, micro_count),
        grid=(head_count,),
        in_specs=[feat_spec, feat_spec, v_spec, state_spec, mask_spec, line_spec],
        out_specs=[head_rows(0), head_rows(0), den_spec],
        out_shape=[
            jax.ShapeDtypeStruct((model_width, total_rows), single),
            jax.ShapeDtypeStruct((model_width, total_rows), bfloat),
            jax.ShapeDtypeStruct((head_count, 1, total_rows), single),
        ],
        compiler_params=params,
    )(feat_query, feat_key, projected, state_in, mask, use_low)

    branch = jnp.einsum(
        "er,ed->rd", attended_low, output_weight, preferred_element_type=single
    ) + output_bias.astype(single)
    middle = flat_input + branch
    normed_two, unit_two, inverse_two = norm_forward(
        middle, gain_two.astype(single), bias_two.astype(single)
    )
    normed_two_low = normed_two.astype(bfloat)
    expanded = jnp.dot(
        normed_two_low, expand_weight, preferred_element_type=single
    ) + expand_bias.astype(single)
    gelu_value, gelu_pull = jax.vjp(partial(jax.nn.gelu, approximate=True), expanded)
    hidden_low = gelu_value.astype(bfloat)
    result = (
        middle
        + jnp.dot(hidden_low, contract_weight, preferred_element_type=single)
        + contract_bias.astype(single)
    )
    block_output = result.astype(bfloat).reshape(micro_count, row_count, model_width)
    grad_contract = cotangent.reshape(total_rows, model_width)
    grad_wide = grad_contract.astype(single)
    hidden_grad = jnp.einsum(
        "rd,fd->rf", grad_contract, contract_weight, preferred_element_type=single
    )
    expanded_grad = gelu_pull(hidden_grad)[0].astype(bfloat)
    normed_two_grad = jnp.einsum(
        "rf,df->rd", expanded_grad, expand_weight, preferred_element_type=single
    )
    middle_norm_grad, gain_two_grad, bias_two_grad = norm_backward(
        normed_two_grad, unit_two, inverse_two, gain_two.astype(single)
    )
    middle_grad = grad_wide + middle_norm_grad
    branch_low = middle_grad.astype(bfloat)
    attended_grad = jnp.einsum(
        "rd,ed->er", branch_low, output_weight, preferred_element_type=single
    )
    local_grad = pl.pallas_call(
        partial(state_grad_kernel, micro_count),
        grid=(head_count,),
        in_specs=[head_rows(0), head_rows(0), den_spec, feat_spec, line_spec],
        out_specs=state_spec,
        out_shape=state_shape,
        compiler_params=params,
    )(attended_grad, attended, denominator, feat_query, use_in)
    out_grad = scan_states(local_grad, masks_reverse, count, True, 2)
    proj_spec = pl.BlockSpec((3, head_width, total_rows), lambda h: (0, h, 0))
    projected_grad, query_map_grad, key_map_grad = pl.pallas_call(
        partial(backward_kernel, micro_count),
        grid=(head_count,),
        in_specs=[
            q_spec, k_spec, v_spec, map_spec, map_spec, feat_spec, feat_spec, head_rows(0),
            head_rows(0), den_spec, state_spec, state_spec, mask_spec, line_spec, line_spec,
        ],
        out_specs=[proj_spec, map_spec, map_spec],
        out_shape=[
            jax.ShapeDtypeStruct((3, model_width, total_rows), bfloat),
            jax.ShapeDtypeStruct(query_map.shape, single),
            jax.ShapeDtypeStruct(key_map.shape, single),
        ],
        scratch_shapes=[pltpu.VMEM((feat_width, total_rows), single)] * 2,
        compiler_params=params,
    )(
        projected, projected, projected, query_map, key_map, feat_query, feat_key, attended_grad,
        attended, denominator, state_in, out_grad, mask, use_in, last_low,
    )
    projected_grad = projected_grad.reshape(3 * model_width, total_rows)
    normed_grad = jnp.einsum(
        "cr,dc->rd", projected_grad, project_weight, preferred_element_type=single
    )
    input_norm_grad, gain_one_grad, bias_one_grad = norm_backward(
        normed_grad, unit_one, inverse_one, gain_one.astype(single)
    )
    input_grad = (
        (middle_grad + input_norm_grad).astype(bfloat).reshape(micro_count, row_count, model_width)
    )

    def scatter(value):
        return lax.psum_scatter(value, "seq", scatter_dimension=0, tiled=True)

    shares = (
        scatter(jnp.einsum("rd,cr->dc", normed_low, projected_grad, preferred_element_type=single)),
        scatter(jnp.einsum("er,rd->ed", attended_low, branch_low, preferred_element_type=single)),
        scatter(
            jnp.einsum("rd,rf->df", normed_two_low, expanded_grad, preferred_element_type=single)
        ),
        scatter(jnp.einsum("rf,rd->fd", hidden_low, grad_contract, preferred_element_type=single)),
    )
    totals = lax.psum(shares, "batch")
    project_bias_grad = jnp.sum(projected_grad.astype(single), axis=1)
    output_bias_grad = jnp.sum(branch_low.astype(single), axis=0)
    expand_bias_grad = jnp.sum(expanded_grad.astype(single), axis=0)
    contract_bias_grad = jnp.sum(grad_wide, axis=0)
    small_sums = lax.psum(
        (
            gain_one_grad, bias_one_grad, project_bias_grad, query_map_grad, key_map_grad,
            output_bias_grad, gain_two_grad, bias_two_grad, expand_bias_grad, contract_bias_grad,
        ),
        ("seq", "batch"),
    )
    return (
        block_output, input_grad, small_sums[0], small_sums[1], totals[0], small_sums[2],
        small_sums[3], small_sums[4], totals[1], small_sums[5], small_sums[6], small_sums[7],
        totals[2], small_sums[8], totals[3], small_sums[9],
    )


def solution(mesh):
    rows = P("batch", "seq", None)
    placed = (rows,) + (P(),) * 14 + (P("batch", None), rows)
    shard = P("seq", None)
    return jax.shard_map(
        per_device,
        mesh=mesh,
        in_specs=placed,
        out_specs=(
            rows, rows, P(), P(), shard, P(), P(), P(), shard, P(), P(), P(), shard, P(), shard, P(),
        ),
        check_vma=False,
    )
```

```python
from functools import partial

import jax
import jax.numpy as jnp
from jax import lax
from jax.experimental import pallas as pl
from jax.experimental.pallas import tpu as pltpu
from jax.sharding import PartitionSpec as P

epsilon = 1e-05
bfloat = jnp.bfloat16
single = jnp.float32
MESH = pl.DeviceIdType.MESH
VMEM_LIMIT = 56 * 1024 * 1024
REDUCE_LIMIT = 60 * 1024 * 1024


def matmul(a, b, contract):
    return lax.dot_general(
        a, b, (((contract[0],), (contract[1],)), ((), ())), preferred_element_type=single
    )


def norm_forward(values, gain_vector, shift_vector):
    centered = values - jnp.mean(values, axis=-1, keepdims=True)
    inverse = lax.rsqrt(jnp.mean(centered * centered, axis=-1, keepdims=True) + epsilon)
    unit_rows = centered * inverse
    return (unit_rows * gain_vector + shift_vector, unit_rows, inverse)


def norm_backward(gradient, unit_rows, inverse, gain_vector):
    inner = gradient * gain_vector
    result = inverse * (
        inner
        - jnp.mean(inner, axis=-1, keepdims=True)
        - unit_rows * jnp.mean(inner * unit_rows, axis=-1, keepdims=True)
    )
    return (result, jnp.sum(gradient * unit_rows, axis=0), jnp.sum(gradient, axis=0))


def doc_number(positions, first_bound, second_bound):
    return (positions >= first_bound).astype(jnp.int32) + (positions >= second_bound).astype(
        jnp.int32
    )


def two_softmaxes(mapped):
    up = jnp.exp(mapped - jnp.max(mapped, axis=0, keepdims=True))
    down = jnp.exp(jnp.min(mapped, axis=0, keepdims=True) - mapped)
    return (
        up / jnp.sum(up, axis=0, keepdims=True),
        down / jnp.sum(down, axis=0, keepdims=True),
    )


def with_ones(rows):
    return jnp.concatenate([rows, jnp.ones((16, rows.shape[1]), rows.dtype)], axis=0)


def state_rows(state, micro, head_width):
    low = state[micro * head_width : (micro + 1) * head_width, :]
    count = state.shape[0] // (head_width + 2)
    total = state[count * head_width + micro : count * head_width + micro + 1, :]
    return jnp.concatenate([low, jnp.broadcast_to(total, (16, low.shape[1]))], axis=0)


def feature_kernel(micro_count, q_ref, k_ref, v_ref, qm_ref, km_ref, last_ref, fq_ref, fk_ref, state_ref):
    head_width = q_ref.shape[0]
    rows = q_ref.shape[1] // micro_count
    for source, weights, target in ((q_ref, qm_ref, fq_ref), (k_ref, km_ref, fk_ref)):
        mapped = matmul(weights[0], source[...], (0, 0))
        up, down = two_softmaxes(mapped)
        target[...] = jnp.concatenate([up, down], axis=0).astype(bfloat)
    wide = with_ones(v_ref[...]) * last_ref[...]
    sums = []
    for m in range(micro_count):
        part = slice(m * rows, (m + 1) * rows)
        local = matmul(wide[:, part], fk_ref[:, part], (1, 1))
        state_ref[0, m * head_width : (m + 1) * head_width, :] = local[:head_width]
        sums.append(local[head_width : head_width + 1])
    sums = jnp.concatenate(sums + sums, axis=0)
    state_ref[0, micro_count * head_width :, :] = sums


def attend_kernel(micro_count, fq_ref, fk_ref, v_ref, state_ref, mask_ref, use_ref, att_ref, low_ref, den_ref):
    head_width = v_ref.shape[0]
    rows = v_ref.shape[1] // micro_count
    wide = with_ones(v_ref[...])
    used = fq_ref[...] * use_ref[...]
    for m in range(micro_count):
        part = slice(m * rows, (m + 1) * rows)
        scores = matmul(fk_ref[:, part], fq_ref[:, part], (0, 0)) * mask_ref[m]
        state = state_rows(state_ref[0], m, head_width).astype(bfloat)
        numer = matmul(wide[:, part], scores.astype(bfloat), (1, 0)) + matmul(
            state, used[:, part], (1, 0)
        )
        denom = numer[head_width : head_width + 1]
        attended = numer[:head_width] / denom
        att_ref[:, part] = attended
        low_ref[:, part] = attended.astype(bfloat)
        den_ref[0, :, part] = denom


def score_grads(grad, attended, denom):
    inverse = 1.0 / denom
    numer_grad = grad * inverse
    denom_grad = -jnp.sum(grad * attended, axis=0, keepdims=True) * inverse
    pad = jnp.zeros((15, grad.shape[1]), single)
    return jnp.concatenate([numer_grad, denom_grad, pad], axis=0)


def state_grad_kernel(micro_count, grad_ref, att_ref, den_ref, fq_ref, use_ref, state_ref):
    head_width = grad_ref.shape[0]
    rows = grad_ref.shape[1] // micro_count
    wide = (score_grads(grad_ref[...], att_ref[...], den_ref[0]) * use_ref[...]).astype(bfloat)
    sums = []
    for m in range(micro_count):
        part = slice(m * rows, (m + 1) * rows)
        local = matmul(wide[:, part], fq_ref[:, part], (1, 1))
        state_ref[0, m * head_width : (m + 1) * head_width, :] = local[:head_width]
        sums.append(local[head_width : head_width + 1])
    sums = jnp.concatenate(sums + sums, axis=0)
    state_ref[0, micro_count * head_width :, :] = sums


def feature_backward(feat_grad, source, weights):
    head_width = source.shape[0]
    up, down = two_softmaxes(matmul(weights, source, (0, 0)))
    grad_up, grad_down = (feat_grad[:head_width], feat_grad[head_width:])
    mapped = up * (grad_up - jnp.sum(up * grad_up, axis=0, keepdims=True)) - down * (
        grad_down - jnp.sum(down * grad_down, axis=0, keepdims=True)
    )
    low = mapped.astype(bfloat)
    return (matmul(weights, low, (1, 0)), matmul(source, low, (1, 1)))


def backward_kernel(
    micro_count, q_ref, k_ref, v_ref, qm_ref, km_ref, fq_ref, fk_ref, grad_ref, att_ref, den_ref,
    state_ref, out_grad_ref, mask_ref, use_ref, last_ref, proj_ref, qmg_ref, kmg_ref, fqg, fkg,
):
    head_width = q_ref.shape[0]
    rows = q_ref.shape[1] // micro_count
    grads = score_grads(grad_ref[...], att_ref[...], den_ref[0])
    low_grads = grads.astype(bfloat)
    used_grads = (grads * use_ref[...]).astype(bfloat)
    wide = with_ones(v_ref[...])
    wide_last = wide * last_ref[...]
    for m in range(micro_count):
        part = slice(m * rows, (m + 1) * rows)
        fq, fk = (fq_ref[:, part], fk_ref[:, part])
        mask = mask_ref[m]
        scores = (matmul(fk, fq, (0, 0)) * mask).astype(bfloat)
        grad_scores = (matmul(wide[:, part], low_grads[:, part], (0, 0)) * mask).astype(bfloat)
        state = state_rows(state_ref[0], m, head_width).astype(bfloat)
        out_grad = state_rows(out_grad_ref[0], m, head_width)
        row = lax.broadcasted_iota(jnp.int32, out_grad.shape, 0)
        out_grad = jnp.where(row <= head_width, out_grad, 0.0).astype(bfloat)
        fqg[:, part] = matmul(fk, grad_scores, (1, 0)) + matmul(state, used_grads[:, part], (0, 0))
        fkg[:, part] = matmul(fq, grad_scores, (1, 1)) + matmul(out_grad, wide_last[:, part], (0, 0))
        value_grad = matmul(low_grads[:head_width, part], scores, (1, 1)) + matmul(
            out_grad[:head_width], fk * last_ref[:, part], (1, 0)
        )
        proj_ref[2, :, part] = value_grad.astype(bfloat)
    q_grad, qmg = feature_backward(fqg[...], q_ref[...], qm_ref[0])
    proj_ref[0] = q_grad.astype(bfloat)
    qmg_ref[0] = qmg
    k_grad, kmg = feature_backward(fkg[...], k_ref[...], km_ref[0])
    proj_ref[1] = k_grad.astype(bfloat)
    kmg_ref[0] = kmg


def scan_kernel(
    reverse, count, local_ref, mask_ref, out_ref, carry, onward, aside, beside,
    carry_send, carry_recv, side_send, side_recv,
):
    place, column = (lax.axis_index("seq"), lax.axis_index("batch"))
    high, low = (place // 2, lax.rem(place, 2))
    length = count // 2
    if reverse:
        lap = length - 1 - high
        ahead, behind = (place - 2, place + 2)
    else:
        lap = high
        ahead, behind = (place + 2, place - 2)
    partner = place + 1 - 2 * low
    first = lap == 0
    final = lap == length - 1
    chunks = local_ref.shape[0]
    barrier = pltpu.get_barrier_semaphore()

    @pl.when(jnp.logical_not(final))
    def _():
        pl.semaphore_signal(barrier, inc=1, device_id=(ahead, column), device_id_type=MESH)

    @pl.when(jnp.logical_not(first))
    def _():
        pl.semaphore_signal(barrier, inc=1, device_id=(behind, column), device_id_type=MESH)

    pl.semaphore_signal(barrier, inc=1, device_id=(partner, column), device_id_type=MESH)
    pl.semaphore_wait(
        barrier, 1 + jnp.where(first, 0, 1) + jnp.where(final, 0, 1)
    )

    def along(i):
        return pltpu.make_async_remote_copy(
            src_ref=onward.at[i], dst_ref=carry.at[i], send_sem=carry_send.at[i],
            recv_sem=carry_recv.at[i], device_id=(ahead, column), device_id_type=MESH,
        )

    def across(i):
        return pltpu.make_async_remote_copy(
            src_ref=aside.at[i], dst_ref=beside.at[i], send_sem=side_send.at[i],
            recv_sem=side_recv.at[i], device_id=(partner, column), device_id_type=MESH,
        )

    @pl.when(first)
    def _():
        carry[...] = jnp.zeros_like(carry)

    def one(i, _):
        @pl.when(jnp.logical_not(first))
        def _():
            along(i).wait_recv()

        state, local = (carry[i], local_ref[i])
        aside[i] = mask_ref[2] * state + mask_ref[3] * local
        across(i).start()

        @pl.when(jnp.logical_not(final))
        def _():
            onward[i] = mask_ref[0] * state + mask_ref[1] * local
            along(i).start()

        return 0

    lax.fori_loop(0, chunks, one, 0)

    def two(i, _):
        across(i).wait_recv()
        out_ref[i] = mask_ref[4] * carry[i] + beside[i]
        return 0

    lax.fori_loop(0, chunks, two, 0)

    def three(i, _):
        across(i).wait_send()

        @pl.when(jnp.logical_not(final))
        def _():
            along(i).wait_send()

        return 0

    lax.fori_loop(0, chunks, three, 0)


def scan_states(local, masks, count, reverse, identity):
    chunks = local.shape[0]
    whole = pl.BlockSpec(memory_space=pltpu.VMEM)
    return pl.pallas_call(
        partial(scan_kernel, reverse, count),
        out_shape=jax.ShapeDtypeStruct(local.shape, single),
        in_specs=[whole, whole],
        out_specs=whole,
        scratch_shapes=[pltpu.VMEM(local.shape, single)] * 4
        + [pltpu.SemaphoreType.DMA((chunks,))] * 4,
        compiler_params=pltpu.CompilerParams(
            collective_id=identity, has_side_effects=True, vmem_limit_bytes=VMEM_LIMIT
        ),
    )(local, masks)


def reduce_kernel(count, lines, plans, sources, *refs):
    direct, halved = plans
    total = direct + halved
    arrays = len({s[0] for s in sources})
    inputs, outputs = (refs[:arrays], refs[arrays : 2 * arrays])
    refs = refs[2 * arrays :]
    out, own, got, y_got, zr_got, zl_got, x_got = refs[:7]
    hx_got, hy_got, hzr_got, hzl_got = refs[7:11]
    sems = refs[11:]
    own_sem, core_send, core_recv, y_send, y_recv, zr_send, zr_recv, zl_send, zl_recv = sems[:9]
    x_send, x_recv, hx_send, hx_recv, back_send, back_recv = sems[9:]
    length = count // 2
    rows, wide = out.shape[1:]
    half = wide // 2
    part = rows // lines
    place, column = (lax.axis_index("seq"), lax.axis_index("batch"))
    high, low = (place // 2, lax.rem(place, 2))
    across, core = (column // 2, lax.rem(column, 2))
    mine = pl.ds(pl.multiple_of(core * half, 128), half)
    strip = pl.ds(pl.multiple_of(across * part, 8), part)
    at_core = (place, column + 1 - 2 * core)
    at_y = (place + 1 - 2 * low, column)
    at_right, at_left = ((place + 2, column), (place - 2, column))
    not_first, not_last = (high > 0, high < length - 1)

    def line(d):
        other = lax.rem(across + d, lines)
        return other, (place, other * 2 + core)

    def remote(src, dst, send, recv, device):
        return pltpu.make_async_remote_copy(
            src_ref=src, dst_ref=dst, send_sem=send, recv_sem=recv, device_id=device, device_id_type=MESH
        )

    barrier = pltpu.get_barrier_semaphore()
    for device in [at_core, at_y] + [line(d)[1] for d in range(1, lines)]:
        pl.semaphore_signal(barrier, inc=1, device_id=device, device_id_type=MESH)

    @pl.when(not_last)
    def _():
        pl.semaphore_signal(barrier, inc=1, device_id=at_right, device_id_type=MESH)

    @pl.when(not_first)
    def _():
        pl.semaphore_signal(barrier, inc=1, device_id=at_left, device_id_type=MESH)

    pl.semaphore_wait(barrier, 1 + lines + jnp.where(not_first, 1, 0) + jnp.where(not_last, 1, 0))

    def source(u, column_half):
        array, lead, row, col = sources[u]
        window = (pl.ds(row, rows), pl.ds(pl.multiple_of(col + column_half * half, 128), half))
        if lead is None:
            return inputs[array].at[(slice(None), slice(None)) + window]
        return inputs[array].at[(slice(None), slice(None), lead) + window]

    def load(u):
        return pltpu.make_async_copy(source(u, core), own.at[u], own_sem.at[u])

    def give(u):
        return remote(source(u, 1 - core), got.at[u], core_send.at[u], core_recv.at[u], at_core)

    for u in range(total):
        give(u).start()
        load(u).start()

    def settle(u):
        pltpu.make_async_copy(own.at[u], own.at[u], own_sem.at[u]).wait()
        remote(own.at[u], got.at[u], core_send.at[u], core_recv.at[u], at_core).wait_recv()
        own[u] = own[u] + got[u]

    def give_back(u):
        block = out.at[u, :, mine]
        return remote(block, block, back_send.at[u], back_recv.at[u], at_core)

    class Grid:
        def __init__(self, base, window, y, zr, zl):
            self.base, self.window, self.y, self.zr, self.zl = base, window, y, zr, zl

        def block(self, i, h, l):
            return own.at[(self.base + i, h, l) + self.window]

        def y_copy(self, i):
            return remote(
                own.at[(self.base + i, slice(None), 1 - low) + self.window], self.y.at[i],
                y_send.at[self.base + i], y_recv.at[self.base + i], at_y,
            )

        def right(self, i, k):
            return remote(
                self.block(i, k, low), self.zr.at[i, k], zr_send.at[self.base + i, k],
                zr_recv.at[self.base + i, k], at_right,
            )

        def left(self, i, k):
            return remote(
                self.block(i, k, low), self.zl.at[i, k], zl_send.at[self.base + i, k],
                zl_recv.at[self.base + i, k], at_left,
            )

        def from_y(self, i):
            self.y_copy(i).wait_recv()
            target = own.at[(self.base + i, slice(None), low) + self.window]
            target[...] = target[...] + self.y[i]
            self.z_step(i, 1)

        def take_right(self, i, k):
            self.right(i, k).wait_recv()
            target = self.block(i, k, low)
            target[...] = target[...] + self.zr[i, k]

        def take_left(self, i, k):
            self.left(i, k).wait_recv()
            target = self.block(i, k, low)
            target[...] = target[...] + self.zl[i, k]

        def z_step(self, i, t):
            k = high + length - t

            @pl.when(high <= t - 1)
            def _():
                if t > 1:
                    @pl.when(not_first)
                    def _():
                        self.take_right(i, k)

                self.right(i, k).start()

            j = high - length + t

            @pl.when(high >= length - t)
            def _():
                if t > 1:
                    @pl.when(not_last)
                    def _():
                        self.take_left(i, j)

                self.left(i, j).start()

        def z_end(self, i):
            @pl.when(not_first)
            def _():
                self.take_right(i, high)

            @pl.when(not_last)
            def _():
                self.take_left(i, high)

        def drain(self, i):
            self.y_copy(i).wait_send()

            def right_one(k, _):
                self.right(i, k).wait_send()
                return 0

            def left_one(k, _):
                self.left(i, k).wait_send()
                return 0

            lax.fori_loop(high + 1, length, right_one, 0)
            lax.fori_loop(0, high, left_one, 0)

    full = Grid(0, (), y_got, zr_got, zl_got)
    thin = Grid(direct, (strip,), hy_got, hzr_got, hzl_got)

    def x_copy(i, d):
        return remote(
            full.block(i, high, low), x_got.at[i, d - 1], x_send.at[i, d - 1], x_recv.at[i, d - 1], line(d)[1]
        )

    def direct_first(i):
        settle(i)
        full.y_copy(i).start()

    def direct_reduced(i):
        full.z_end(i)
        for d in range(1, lines):
            x_copy(i, d).start()

    def direct_done(i):
        for d in range(1, lines):
            x_copy(i, d).wait_recv()
        value = full.block(i, high, low)[...]
        if lines == 2:
            value = value + x_got[i, 0]
        else:
            parts = []
            for x in range(lines):
                slot = lax.rem(across - x + lines - 1, lines)
                parts.append(jnp.where(x == across, value, x_got[i, jnp.minimum(slot, lines - 2)]))
            value = sum(parts[1:], parts[0])
        out[i, :, mine] = value
        give_back(i).start()

    def strip_copy(i, d):
        other, device = line(d)
        theirs = pl.ds(pl.multiple_of(other * part, 8), part)
        return remote(
            own.at[direct + i, :, :, theirs], hx_got.at[i, d - 1], hx_send.at[i, 0, d - 1],
            hx_recv.at[i, 0, d - 1], device,
        )

    def strip_back(i, d):
        block = out.at[direct + i, strip, mine]
        return remote(block, block, hx_send.at[i, 1, d - 1], hx_recv.at[i, 1, d - 1], line(d)[1])

    def halved_first(i):
        settle(direct + i)
        for d in range(1, lines):
            strip_copy(i, d).start()

    def halved_next(i):
        for d in range(1, lines):
            strip_copy(i, d).wait_recv()
            target = own.at[direct + i, :, :, strip]
            target[...] = target[...] + hx_got[i, d - 1]
        thin.y_copy(i).start()

    def halved_reduced(i):
        thin.z_end(i)
        out[direct + i, strip, mine] = thin.block(i, high, low)[...]
        for d in range(1, lines):
            strip_back(i, d).start()

    def halved_done(i):
        for d in range(1, lines):
            strip_back(i, d).wait_recv()
        give_back(direct + i).start()

    def z_steps(grid):
        return [partial(grid.z_step, t=t) for t in range(2, length)]

    stages = []
    if direct:
        steps = [direct_first, full.from_y] + z_steps(full) + [direct_reduced, direct_done]
        stages += [(s, f, direct) for s, f in enumerate(steps)]
    if halved:
        steps = [halved_first, halved_next, thin.from_y] + z_steps(thin) + [halved_reduced, halved_done]
        stages += [(s, f, halved) for s, f in enumerate(steps)]
    stages.sort(key=lambda s: -s[0])
    rounds = max(direct, halved) + stages[0][0]

    def one_round(r, _):
        for lag, step, size in stages:
            @pl.when((r >= lag) & (r < lag + size))
            def _(lag=lag, step=step):
                step(r - lag)

        return 0

    lax.fori_loop(0, rounds, one_round, 0)

    def finish(u, _):
        remote(own.at[u], got.at[u], core_send.at[u], core_recv.at[u], at_core).wait_send()
        give_back(u).wait()
        return 0

    lax.fori_loop(0, total, finish, 0)

    def store(u):
        array, lead, row, col = sources[u]
        window = (pl.ds(row, rows), pl.ds(col, wide))
        window = window if lead is None else (lead,) + window
        return pltpu.make_async_copy(out.at[u], outputs[array].at[window], own_sem.at[u])

    for u in range(total):
        store(u).start()

    def drain_direct(i, _):
        full.drain(i)
        for d in range(1, lines):
            x_copy(i, d).wait_send()
        return 0

    def drain_halved(i, _):
        thin.drain(i)
        for d in range(1, lines):
            strip_copy(i, d).wait_send()
            strip_back(i, d).wait_send()
        return 0

    if direct:
        lax.fori_loop(0, direct, drain_direct, 0)
    if halved:
        lax.fori_loop(0, halved, drain_halved, 0)
    for u in range(total):
        store(u).wait()


def reduce_all(arrays, sources, plans, rows, count, lines, identity):
    direct, halved = plans
    total = direct + halved
    length = count // 2
    wide = 768
    half = wide // 2
    part = max(rows // lines, 8)
    spare = max(halved, 1)
    DMA = pltpu.SemaphoreType.DMA
    others = max(lines - 1, 1)
    return pl.pallas_call(
        partial(reduce_kernel, count, lines, plans, sources),
        out_shape=[jax.ShapeDtypeStruct(a.shape[2:], single) for a in arrays],
        in_specs=[pl.BlockSpec(memory_space=pl.ANY)] * len(arrays),
        out_specs=[pl.BlockSpec(memory_space=pl.ANY)] * len(arrays),
        scratch_shapes=[
            pltpu.VMEM((total, rows, wide), single),
            pltpu.VMEM((total, length, 2, rows, half), single),
            pltpu.VMEM((total, length, 2, rows, half), single),
            pltpu.VMEM((max(direct, 1), length, rows, half), single),
            pltpu.VMEM((max(direct, 1), length, rows, half), single),
            pltpu.VMEM((max(direct, 1), length, rows, half), single),
            pltpu.VMEM((max(direct, 1), others, rows, half), single),
            pltpu.VMEM((spare, others, length, 2, part, half), single),
            pltpu.VMEM((spare, length, part, half), single),
            pltpu.VMEM((spare, length, part, half), single),
            pltpu.VMEM((spare, length, part, half), single),
            DMA((total,)), DMA((total,)), DMA((total,)), DMA((total,)), DMA((total,)),
            DMA((total, length)), DMA((total, length)), DMA((total, length)), DMA((total, length)),
            DMA((max(direct, 1), others)), DMA((max(direct, 1), others)),
            DMA((spare, 2, others)), DMA((spare, 2, others)),
            DMA((total,)), DMA((total,)),
        ],
        compiler_params=pltpu.CompilerParams(
            collective_id=identity, has_side_effects=True, vmem_limit_bytes=REDUCE_LIMIT
        ),
    )(*arrays)


def scan_masks(bounds, first_row, row_count, place, micro_count, head_width, reverse):
    def doc(position):
        return doc_number(position, bounds[:, 0], bounds[:, 1])

    low = lax.rem(place, 2)
    base = first_row - low * row_count
    step = 2 * row_count
    if reverse:
        low = 1 - low
        own_edge = doc(first_row)
        pair = doc(base + step - 1)
        ahead = doc(base - 1)
        inner = doc(base + row_count - 1)
    else:
        own_edge = doc(first_row + row_count - 1)
        pair = doc(base - 1)
        ahead = doc(base + step - 1)
        inner = doc(base + row_count - 1)
    if reverse:
        own_edge = doc(first_row - 1)
    one = jnp.ones((micro_count,), single)
    keep = (pair == inner).astype(single)
    masks = jnp.stack(
        [
            (pair == ahead).astype(single),
            (own_edge == ahead).astype(single),
            jnp.where(low == 0, keep, one),
            jnp.where(low == 0, one, 0 * one),
            jnp.where(low == 0, one, keep),
        ]
    )
    wide = jnp.concatenate([jnp.repeat(masks, head_width, axis=1), masks, masks], axis=1)
    return jnp.broadcast_to(wide[:, :, None], wide.shape + (2 * head_width,))


def per_device(
    inputs, gain_one, bias_one, project_weight, project_bias, query_map, key_map, output_weight,
    output_bias, gain_two, bias_two, expand_weight, expand_bias, contract_weight, contract_bias,
    bounds, cotangent,
):
    micro_count, row_count, model_width = inputs.shape
    head_count, head_width = (query_map.shape[0], query_map.shape[1])
    feat_width = 2 * head_width
    total_rows = micro_count * row_count
    count = lax.axis_size("seq")
    place = lax.axis_index("seq")
    first_row = place * row_count
    positions = first_row + jnp.arange(row_count, dtype=jnp.int32)
    first_bound, second_bound = (bounds[:, 0:1], bounds[:, 1:2])
    doc_ids = doc_number(positions[None, :], first_bound, second_bound)
    doc_prev = doc_number(first_row - 1, first_bound, second_bound)
    doc_last = doc_number(first_row + row_count - 1, first_bound, second_bound)
    use_in = (doc_ids == doc_prev).astype(single).reshape(1, total_rows)
    in_last = (doc_ids == doc_last).astype(single).reshape(1, total_rows)
    use_low, last_low = (use_in.astype(bfloat), in_last.astype(bfloat))
    causal = positions[:, None] <= positions[None, :]
    mask = (causal[None] & (doc_ids[:, :, None] == doc_ids[:, None, :])).astype(single)
    masks_forward = scan_masks(bounds, first_row, row_count, place, micro_count, head_width, False)
    masks_reverse = scan_masks(bounds, first_row, row_count, place, micro_count, head_width, True)

    flat_input = inputs.reshape(total_rows, model_width).astype(single)
    normed, unit_one, inverse_one = norm_forward(
        flat_input, gain_one.astype(single), bias_one.astype(single)
    )
    normed_low = normed.astype(bfloat)
    projected = (
        jnp.einsum("dc,rd->cr", project_weight, normed_low, preferred_element_type=single)
        + project_bias.astype(single)[:, None]
    ).astype(bfloat)

    head_rows = lambda offset: pl.BlockSpec((head_width, total_rows), lambda h: (h + offset, 0))
    map_spec = pl.BlockSpec((1, head_width, head_width), lambda h: (h, 0, 0))
    feat_spec = pl.BlockSpec((feat_width, total_rows), lambda h: (h, 0))
    line_spec = pl.BlockSpec((1, total_rows), lambda h: (0, 0))
    den_spec = pl.BlockSpec((1, 1, total_rows), lambda h: (h, 0, 0))
    state_height = micro_count * (head_width + 2)
    state_spec = pl.BlockSpec((1, state_height, feat_width), lambda h: (h, 0, 0))
    mask_spec = pl.BlockSpec((micro_count, row_count, row_count), lambda h: (0, 0, 0))
    q_spec, k_spec, v_spec = (head_rows(0), head_rows(head_count), head_rows(2 * head_count))
    feat_shape = jax.ShapeDtypeStruct((head_count * feat_width, total_rows), bfloat)
    state_shape = jax.ShapeDtypeStruct((head_count, state_height, feat_width), single)
    params = pltpu.CompilerParams(vmem_limit_bytes=VMEM_LIMIT)

    feat_query, feat_key, local_state = pl.pallas_call(
        partial(feature_kernel, micro_count),
        grid=(head_count,),
        in_specs=[q_spec, k_spec, v_spec, map_spec, map_spec, line_spec],
        out_specs=[feat_spec, feat_spec, state_spec],
        out_shape=[feat_shape, feat_shape, state_shape],
        compiler_params=params,
    )(projected, projected, projected, query_map, key_map, last_low)
    state_in = scan_states(local_state, masks_forward, count, False, 1)
    attended, attended_low, denominator = pl.pallas_call(
        partial(attend_kernel, micro_count),
        grid=(head_count,),
        in_specs=[feat_spec, feat_spec, v_spec, state_spec, mask_spec, line_spec],
        out_specs=[head_rows(0), head_rows(0), den_spec],
        out_shape=[
            jax.ShapeDtypeStruct((model_width, total_rows), single),
            jax.ShapeDtypeStruct((model_width, total_rows), bfloat),
            jax.ShapeDtypeStruct((head_count, 1, total_rows), single),
        ],
        compiler_params=params,
    )(feat_query, feat_key, projected, state_in, mask, use_low)

    branch = jnp.einsum(
        "er,ed->rd", attended_low, output_weight, preferred_element_type=single
    ) + output_bias.astype(single)
    middle = flat_input + branch
    normed_two, unit_two, inverse_two = norm_forward(
        middle, gain_two.astype(single), bias_two.astype(single)
    )
    normed_two_low = normed_two.astype(bfloat)
    expanded = jnp.dot(
        normed_two_low, expand_weight, preferred_element_type=single
    ) + expand_bias.astype(single)
    gelu_value, gelu_pull = jax.vjp(partial(jax.nn.gelu, approximate=True), expanded)
    hidden_low = gelu_value.astype(bfloat)
    result = (
        middle
        + jnp.dot(hidden_low, contract_weight, preferred_element_type=single)
        + contract_bias.astype(single)
    )
    block_output = result.astype(bfloat).reshape(micro_count, row_count, model_width)
    grad_contract = cotangent.reshape(total_rows, model_width)
    grad_wide = grad_contract.astype(single)
    hidden_grad = jnp.einsum(
        "rd,fd->rf", grad_contract, contract_weight, preferred_element_type=single
    )
    expanded_grad = gelu_pull(hidden_grad)[0].astype(bfloat)
    normed_two_grad = jnp.einsum(
        "rf,df->rd", expanded_grad, expand_weight, preferred_element_type=single
    )
    middle_norm_grad, gain_two_grad, bias_two_grad = norm_backward(
        normed_two_grad, unit_two, inverse_two, gain_two.astype(single)
    )
    middle_grad = grad_wide + middle_norm_grad
    branch_low = middle_grad.astype(bfloat)
    attended_grad = jnp.einsum(
        "rd,ed->er", branch_low, output_weight, preferred_element_type=single
    )
    local_grad = pl.pallas_call(
        partial(state_grad_kernel, micro_count),
        grid=(head_count,),
        in_specs=[head_rows(0), head_rows(0), den_spec, feat_spec, line_spec],
        out_specs=state_spec,
        out_shape=state_shape,
        compiler_params=params,
    )(attended_grad, attended, denominator, feat_query, use_in)
    out_grad = scan_states(local_grad, masks_reverse, count, True, 2)
    proj_spec = pl.BlockSpec((3, head_width, total_rows), lambda h: (0, h, 0))
    projected_grad, query_map_grad, key_map_grad = pl.pallas_call(
        partial(backward_kernel, micro_count),
        grid=(head_count,),
        in_specs=[
            q_spec, k_spec, v_spec, map_spec, map_spec, feat_spec, feat_spec, head_rows(0),
            head_rows(0), den_spec, state_spec, state_spec, mask_spec, line_spec, line_spec,
        ],
        out_specs=[proj_spec, map_spec, map_spec],
        out_shape=[
            jax.ShapeDtypeStruct((3, model_width, total_rows), bfloat),
            jax.ShapeDtypeStruct(query_map.shape, single),
            jax.ShapeDtypeStruct(key_map.shape, single),
        ],
        scratch_shapes=[pltpu.VMEM((feat_width, total_rows), single)] * 2,
        compiler_params=params,
    )(
        projected, projected, projected, query_map, key_map, feat_query, feat_key, attended_grad,
        attended, denominator, state_in, out_grad, mask, use_in, last_low,
    )
    projected_grad = projected_grad.reshape(3 * model_width, total_rows)
    normed_grad = jnp.einsum(
        "cr,dc->rd", projected_grad, project_weight, preferred_element_type=single
    )
    input_norm_grad, gain_one_grad, bias_one_grad = norm_backward(
        normed_grad, unit_one, inverse_one, gain_one.astype(single)
    )
    input_grad = (
        (middle_grad + input_norm_grad).astype(bfloat).reshape(micro_count, row_count, model_width)
    )

    lines = lax.axis_size("batch") // 2
    share = model_width // count
    rows = share // 2 if share // 2 % (8 * lines) == 0 else share
    tiles = (count // 2, 2)
    arrays = [
        jnp.einsum("rf,rd->fd", hidden_low, grad_contract, preferred_element_type=single).reshape(
            tiles + (expand_weight.shape[1] // model_width, share, model_width)
        ),
        jnp.einsum("rd,rf->df", normed_two_low, expanded_grad, preferred_element_type=single),
        jnp.einsum("er,rd->ed", attended_low, branch_low, preferred_element_type=single),
        jnp.einsum("rd,cr->dc", normed_low, projected_grad, preferred_element_type=single),
    ]
    arrays[1:] = [a.reshape(tiles + (share, a.shape[1])) for a in arrays[1:]]
    units = [(0, u, 0) for u in range(arrays[0].shape[2])]
    for a in (1, 2, 3):
        units += [(a, None, c) for c in range(0, arrays[a].shape[3], model_width)]
    chunks = [(a, lead, row, col) for a, lead, col in units for row in range(0, share, rows)]
    if rows % (8 * lines) == 0:
        direct, halved = (chunks[0::2], chunks[1::2])
    else:
        direct, halved = (chunks, [])
    totals = reduce_all(
        arrays, direct + halved, (len(direct), len(halved)), rows, count, lines, 3
    )
    totals = [totals[3], totals[2], totals[1], totals[0].reshape(-1, model_width)]
    project_bias_grad = jnp.sum(projected_grad.astype(single), axis=1)
    output_bias_grad = jnp.sum(branch_low.astype(single), axis=0)
    expand_bias_grad = jnp.sum(expanded_grad.astype(single), axis=0)
    contract_bias_grad = jnp.sum(grad_wide, axis=0)
    small_sums = lax.psum(
        (
            gain_one_grad, bias_one_grad, project_bias_grad, query_map_grad, key_map_grad,
            output_bias_grad, gain_two_grad, bias_two_grad, expand_bias_grad, contract_bias_grad,
        ),
        ("seq", "batch"),
    )
    return (
        block_output, input_grad, small_sums[0], small_sums[1], totals[0], small_sums[2],
        small_sums[3], small_sums[4], totals[1], small_sums[5], small_sums[6], small_sums[7],
        totals[2], small_sums[8], totals[3], small_sums[9],
    )


def solution(mesh):
    rows = P("batch", "seq", None)
    placed = (rows,) + (P(),) * 14 + (P("batch", None), rows)
    shard = P("seq", None)
    return jax.shard_map(
        per_device,
        mesh=mesh,
        in_specs=placed,
        out_specs=(
            rows, rows, P(), P(), shard, P(), P(), P(), shard, P(), P(), P(), shard, P(), shard, P(),
        ),
        check_vma=False,
    )
```

```python
from functools import partial

import jax
import jax.numpy as jnp
from jax import lax
from jax.experimental import pallas as pl
from jax.experimental.pallas import tpu as pltpu
from jax.sharding import PartitionSpec as P

epsilon = 1e-05
bfloat = jnp.bfloat16
single = jnp.float32
MESH = pl.DeviceIdType.MESH
VMEM_LIMIT = 56 * 1024 * 1024
REDUCE_LIMIT = 60 * 1024 * 1024


def matmul(a, b, contract):
    return lax.dot_general(
        a, b, (((contract[0],), (contract[1],)), ((), ())), preferred_element_type=single
    )


def norm_forward(values, gain_vector, shift_vector):
    centered = values - jnp.mean(values, axis=-1, keepdims=True)
    inverse = lax.rsqrt(jnp.mean(centered * centered, axis=-1, keepdims=True) + epsilon)
    unit_rows = centered * inverse
    return (unit_rows * gain_vector + shift_vector, unit_rows, inverse)


def norm_backward(gradient, unit_rows, inverse, gain_vector):
    inner = gradient * gain_vector
    result = inverse * (
        inner
        - jnp.mean(inner, axis=-1, keepdims=True)
        - unit_rows * jnp.mean(inner * unit_rows, axis=-1, keepdims=True)
    )
    return (result, jnp.sum(gradient * unit_rows, axis=0), jnp.sum(gradient, axis=0))


def doc_number(positions, first_bound, second_bound):
    return (positions >= first_bound).astype(jnp.int32) + (positions >= second_bound).astype(
        jnp.int32
    )


def two_softmaxes(mapped):
    up = jnp.exp(mapped - jnp.max(mapped, axis=0, keepdims=True))
    down = jnp.exp(jnp.min(mapped, axis=0, keepdims=True) - mapped)
    return (
        up / jnp.sum(up, axis=0, keepdims=True),
        down / jnp.sum(down, axis=0, keepdims=True),
    )


def with_ones(rows):
    return jnp.concatenate([rows, jnp.ones((16, rows.shape[1]), rows.dtype)], axis=0)


def state_rows(state, micro, micro_count, head_width):
    low = state[micro * head_width : (micro + 1) * head_width, :]
    row = micro_count * head_width + micro
    total = state[row : row + 1, :]
    return jnp.concatenate([low, jnp.broadcast_to(total, (16, low.shape[1]))], axis=0)


def score_grads(grad, attended, denom):
    inverse = 1.0 / denom
    numer_grad = grad * inverse
    denom_grad = -jnp.sum(grad * attended, axis=0, keepdims=True) * inverse
    pad = jnp.zeros((15, grad.shape[1]), single)
    return jnp.concatenate([numer_grad, denom_grad, pad], axis=0)


def state_grad_kernel(micro_count, grad_ref, att_ref, den_ref, fq_ref, use_ref, state_ref):
    head_width = grad_ref.shape[0]
    rows = grad_ref.shape[1] // micro_count
    wide = (score_grads(grad_ref[...], att_ref[...], den_ref[0]) * use_ref[...]).astype(bfloat)
    sums = []
    for m in range(micro_count):
        part = slice(m * rows, (m + 1) * rows)
        local = matmul(wide[:, part], fq_ref[:, part], (1, 1))
        state_ref[0, m * head_width : (m + 1) * head_width, :] = local[:head_width]
        sums.append(local[head_width : head_width + 1])
    sums = jnp.concatenate(sums + sums, axis=0)
    state_ref[0, micro_count * head_width :, :] = sums


def feature_backward(feat_grad, source, weights):
    head_width = source.shape[0]
    up, down = two_softmaxes(matmul(weights, source, (0, 0)))
    grad_up, grad_down = (feat_grad[:head_width], feat_grad[head_width:])
    mapped = up * (grad_up - jnp.sum(up * grad_up, axis=0, keepdims=True)) - down * (
        grad_down - jnp.sum(down * grad_down, axis=0, keepdims=True)
    )
    low = mapped.astype(bfloat)
    return (matmul(weights, low, (1, 0)), matmul(source, low, (1, 1)))


def backward_kernel(
    micro_count, q_ref, k_ref, v_ref, qm_ref, km_ref, fq_ref, fk_ref, grad_ref, att_ref, den_ref,
    state_ref, out_grad_ref, mask_ref, use_ref, last_ref, proj_ref, qmg_ref, kmg_ref, fqg, fkg,
):
    head_width = q_ref.shape[0]
    rows = q_ref.shape[1] // micro_count
    grads = score_grads(grad_ref[...], att_ref[...], den_ref[0])
    low_grads = grads.astype(bfloat)
    used_grads = (grads * use_ref[...]).astype(bfloat)
    wide = with_ones(v_ref[...])
    wide_last = wide * last_ref[...]
    for m in range(micro_count):
        part = slice(m * rows, (m + 1) * rows)
        fq, fk = (fq_ref[:, part], fk_ref[:, part])
        mask = mask_ref[m]
        scores = (matmul(fk, fq, (0, 0)) * mask).astype(bfloat)
        grad_scores = (matmul(wide[:, part], low_grads[:, part], (0, 0)) * mask).astype(bfloat)
        state = state_rows(state_ref.at[0], m, micro_count, head_width).astype(bfloat)
        out_grad = state_rows(out_grad_ref.at[0], m, micro_count, head_width)
        row = lax.broadcasted_iota(jnp.int32, out_grad.shape, 0)
        out_grad = jnp.where(row <= head_width, out_grad, 0.0).astype(bfloat)
        fqg[:, part] = matmul(fk, grad_scores, (1, 0)) + matmul(state, used_grads[:, part], (0, 0))
        fkg[:, part] = matmul(fq, grad_scores, (1, 1)) + matmul(out_grad, wide_last[:, part], (0, 0))
        value_grad = matmul(low_grads[:head_width, part], scores, (1, 1)) + matmul(
            out_grad[:head_width], fk * last_ref[:, part], (1, 0)
        )
        proj_ref[2, :, part] = value_grad.astype(bfloat)
    q_grad, qmg = feature_backward(fqg[...], q_ref[...], qm_ref[0])
    proj_ref[0] = q_grad.astype(bfloat)
    qmg_ref[0] = qmg
    k_grad, kmg = feature_backward(fkg[...], k_ref[...], km_ref[0])
    proj_ref[1] = k_grad.astype(bfloat)
    kmg_ref[0] = kmg


def scan_kernel(
    reverse, count, local_ref, mask_ref, out_ref, carry, onward, aside, beside,
    carry_send, carry_recv, side_send, side_recv,
):
    place, column = (lax.axis_index("seq"), lax.axis_index("batch"))
    high, low = (place // 2, lax.rem(place, 2))
    length = count // 2
    if reverse:
        lap = length - 1 - high
        ahead, behind = (place - 2, place + 2)
    else:
        lap = high
        ahead, behind = (place + 2, place - 2)
    partner = place + 1 - 2 * low
    first = lap == 0
    final = lap == length - 1
    chunks = local_ref.shape[0]
    barrier = pltpu.get_barrier_semaphore()

    @pl.when(jnp.logical_not(final))
    def _():
        pl.semaphore_signal(barrier, inc=1, device_id=(ahead, column), device_id_type=MESH)

    @pl.when(jnp.logical_not(first))
    def _():
        pl.semaphore_signal(barrier, inc=1, device_id=(behind, column), device_id_type=MESH)

    pl.semaphore_signal(barrier, inc=1, device_id=(partner, column), device_id_type=MESH)
    pl.semaphore_wait(
        barrier, 1 + jnp.where(first, 0, 1) + jnp.where(final, 0, 1)
    )

    def along(i):
        return pltpu.make_async_remote_copy(
            src_ref=onward.at[i], dst_ref=carry.at[i], send_sem=carry_send.at[i],
            recv_sem=carry_recv.at[i], device_id=(ahead, column), device_id_type=MESH,
        )

    def across(i):
        return pltpu.make_async_remote_copy(
            src_ref=aside.at[i], dst_ref=beside.at[i], send_sem=side_send.at[i],
            recv_sem=side_recv.at[i], device_id=(partner, column), device_id_type=MESH,
        )

    @pl.when(first)
    def _():
        carry[...] = jnp.zeros_like(carry)

    def one(i, _):
        @pl.when(jnp.logical_not(first))
        def _():
            along(i).wait_recv()

        state, local = (carry[i], local_ref[i])
        aside[i] = mask_ref[2] * state + mask_ref[3] * local
        across(i).start()

        @pl.when(jnp.logical_not(final))
        def _():
            onward[i] = mask_ref[0] * state + mask_ref[1] * local
            along(i).start()

        return 0

    lax.fori_loop(0, chunks, one, 0)

    def two(i, _):
        across(i).wait_recv()
        out_ref[i] = mask_ref[4] * carry[i] + beside[i]
        return 0

    lax.fori_loop(0, chunks, two, 0)

    def three(i, _):
        across(i).wait_send()

        @pl.when(jnp.logical_not(final))
        def _():
            along(i).wait_send()

        return 0

    lax.fori_loop(0, chunks, three, 0)


def scan_states(local, masks, count, reverse, identity):
    chunks = local.shape[0]
    whole = pl.BlockSpec(memory_space=pltpu.VMEM)
    return pl.pallas_call(
        partial(scan_kernel, reverse, count),
        out_shape=jax.ShapeDtypeStruct(local.shape, single),
        in_specs=[whole, whole],
        out_specs=whole,
        scratch_shapes=[pltpu.VMEM(local.shape, single)] * 4
        + [pltpu.SemaphoreType.DMA((chunks,))] * 4,
        compiler_params=pltpu.CompilerParams(
            collective_id=identity, has_side_effects=True, vmem_limit_bytes=VMEM_LIMIT
        ),
    )(local, masks)


def document(position, bounds_ref, m):
    return jnp.where(position >= bounds_ref[m, 0], 1, 0) + jnp.where(
        position >= bounds_ref[m, 1], 1, 0
    )


def token_masks(bounds_ref, first_row, rows, micro_count, mask_ref, use_ref, last_ref):
    low_shape, line_shape = ((rows, rows), (1, rows))
    source = first_row + lax.broadcasted_iota(jnp.int32, low_shape, 0)
    target = first_row + lax.broadcasted_iota(jnp.int32, low_shape, 1)
    line = first_row + lax.broadcasted_iota(jnp.int32, line_shape, 1)
    for m in range(micro_count):
        part = slice(m * rows, (m + 1) * rows)
        same = document(source, bounds_ref, m) == document(target, bounds_ref, m)
        mask_ref[m] = jnp.where((source <= target) & same, 1.0, 0.0)
        own = document(line, bounds_ref, m)
        use_ref[:, part] = jnp.where(own == document(first_row - 1, bounds_ref, m), 1.0, 0.0)
        last_ref[:, part] = jnp.where(
            own == document(first_row + rows - 1, bounds_ref, m), 1.0, 0.0
        )


def chain_masks(bounds_ref, first_row, low, rows, micro_count, head_width, reverse, mask_ref):
    base = first_row - low * rows
    step = 2 * rows
    height, wide = mask_ref.shape[1:]
    for m in range(micro_count):
        def doc(position, m=m):
            return document(position, bounds_ref, m)

        inner = doc(base + rows - 1)
        if reverse:
            lead = 1 - low
            own_edge, pair, ahead = (doc(first_row - 1), doc(base + step - 1), doc(base - 1))
        else:
            lead = low
            own_edge, pair, ahead = (
                doc(first_row + rows - 1), doc(base - 1), doc(base + step - 1),
            )
        keep = jnp.where(pair == inner, 1.0, 0.0)
        values = [
            jnp.where(pair == ahead, 1.0, 0.0),
            jnp.where(own_edge == ahead, 1.0, 0.0),
            jnp.where(lead == 0, keep, 1.0),
            jnp.where(lead == 0, 1.0, 0.0),
            jnp.where(lead == 0, 1.0, keep),
        ]
        for i, value in enumerate(values):
            mask_ref[i, m * head_width : (m + 1) * head_width, :] = jnp.full(
                (head_width, wide), value
            )
            tail = slice(micro_count * head_width, height)
            row = lax.broadcasted_iota(jnp.int32, (height - tail.start, wide), 0)
            before = jnp.zeros(row.shape, single) if m == 0 else mask_ref[i, tail, :]
            mask_ref[i, tail, :] = jnp.where(lax.rem(row, micro_count) == m, value, before)


class Chain:
    def __init__(self, reverse, count, carry, onward, aside, beside, mask, sems):
        self.carry, self.onward, self.aside, self.beside = carry, onward, aside, beside
        self.mask, self.sems = mask, sems
        place, self.column = (lax.axis_index("seq"), lax.axis_index("batch"))
        high, low = (place // 2, lax.rem(place, 2))
        length = count // 2
        self.lap = length - 1 - high if reverse else high
        self.ahead, self.behind = (place - 2, place + 2) if reverse else (place + 2, place - 2)
        self.partner = place + 1 - 2 * low
        self.first, self.final = (self.lap == 0, self.lap == length - 1)

    def greet(self, barrier):
        def signal(place):
            pl.semaphore_signal(
                barrier, inc=1, device_id=(place, self.column), device_id_type=MESH
            )

        signal(self.partner)

        @pl.when(jnp.logical_not(self.final))
        def _():
            signal(self.ahead)

        @pl.when(jnp.logical_not(self.first))
        def _():
            signal(self.behind)

        return 1 + jnp.where(self.first, 0, 1) + jnp.where(self.final, 0, 1)

    def along(self, i):
        return pltpu.make_async_remote_copy(
            src_ref=self.onward.at[i], dst_ref=self.carry.at[i], send_sem=self.sems[0].at[i],
            recv_sem=self.sems[1].at[i], device_id=(self.ahead, self.column), device_id_type=MESH,
        )

    def across(self, i):
        return pltpu.make_async_remote_copy(
            src_ref=self.aside.at[i], dst_ref=self.beside.at[i], send_sem=self.sems[2].at[i],
            recv_sem=self.sems[3].at[i], device_id=(self.partner, self.column),
            device_id_type=MESH,
        )

    def start(self):
        @pl.when(self.first)
        def _():
            self.carry[...] = jnp.zeros_like(self.carry)

    def step(self, i, local):
        @pl.when(jnp.logical_not(self.first))
        def _():
            self.along(i).wait_recv()

        state = self.carry[i]

        @pl.when(jnp.logical_not(self.final))
        def _():
            self.onward[i] = self.mask[0] * state + self.mask[1] * local
            self.along(i).start()

        self.aside[i] = self.mask[2] * state + self.mask[3] * local
        self.across(i).start()

    def result(self, i):
        self.across(i).wait_recv()
        return self.mask[4] * self.carry[i] + self.beside[i]

    def drain(self, chunks):
        def one(i, _):
            self.across(i).wait_send()

            @pl.when(jnp.logical_not(self.final))
            def _():
                self.along(i).wait_send()

            return 0

        lax.fori_loop(0, chunks, one, 0)


def local_state(wide, other, micro_count, head_width, target):
    rows = wide.shape[1] // micro_count
    sums = []
    for m in range(micro_count):
        part = slice(m * rows, (m + 1) * rows)
        local = matmul(wide[:, part], other[:, part], (1, 1))
        target[m * head_width : (m + 1) * head_width, :] = local[:head_width]
        sums.append(local[head_width : head_width + 1])
    target[micro_count * head_width :, :] = jnp.concatenate(sums + sums, axis=0)


def forward_kernel(
    count, micro_count, x_ref, gain_ref, shift_ref, weight_ref, bias_ref, qm_ref, km_ref,
    bounds_ref, proj_ref, fq_ref, fk_ref, state_ref, att_ref, low_ref, den_ref,
    normed, mask, use, last, chain_mask, local, carry, onward, aside, beside, *sems,
):
    heads, head_width = qm_ref.shape[:2]
    total_rows = x_ref.shape[0]
    rows = total_rows // micro_count
    model_width = x_ref.shape[1]
    pair = 2 * head_width
    place = lax.axis_index("seq")
    first_row = place * rows
    chain = Chain(False, count, carry, onward, aside, beside, chain_mask, sems)
    barrier = pltpu.get_barrier_semaphore()
    greeted = chain.greet(barrier)
    token_masks(bounds_ref, first_row, rows, micro_count, mask, use, last)
    chain_masks(
        bounds_ref, first_row, lax.rem(place, 2), rows, micro_count, head_width, False, chain_mask
    )
    chain.start()
    normed[...] = norm_forward(
        x_ref[...].astype(single), gain_ref[...].astype(single), shift_ref[...].astype(single)
    )[0].astype(bfloat)
    pl.semaphore_wait(barrier, greeted)

    def project(p):
        for part in range(3):
            columns = pl.ds(pl.multiple_of(part * model_width + p * pair, pair), pair)
            value = matmul(normed[...], weight_ref[:, columns], (1, 0))
            value = (value + bias_ref[:, columns].astype(single)).astype(bfloat).T
            proj_ref[part * heads + 2 * p] = value[:head_width]
            proj_ref[part * heads + 2 * p + 1] = value[head_width:]

    def features(h):
        for offset, weights, target in ((0, qm_ref, fq_ref), (heads, km_ref, fk_ref)):
            mapped = matmul(weights[h], proj_ref[offset + h], (0, 0))
            up, down = two_softmaxes(mapped)
            target[h] = jnp.concatenate([up, down], axis=0).astype(bfloat)
        wide = with_ones(proj_ref[2 * heads + h]) * last[...].astype(bfloat)
        local_state(wide, fk_ref.at[h], micro_count, head_width, local.at[h])

    def attend(h):
        state_ref[h] = chain.result(h)
        wide = with_ones(proj_ref[2 * heads + h])
        used = fq_ref[h] * use[...].astype(bfloat)
        for m in range(micro_count):
            part = slice(m * rows, (m + 1) * rows)
            scores = matmul(fk_ref[h, :, part], fq_ref[h, :, part], (0, 0)) * mask[m]
            state = state_rows(state_ref.at[h], m, micro_count, head_width).astype(bfloat)
            numer = matmul(wide[:, part], scores.astype(bfloat), (1, 0)) + matmul(
                state, used[:, part], (1, 0)
            )
            denom = numer[head_width : head_width + 1]
            attended = numer[:head_width] / denom
            att_ref[h, :, part] = attended
            low_ref[h, :, part] = attended.astype(bfloat)
            den_ref[h, :, part] = denom

    def one_round(r, _):
        @pl.when((r < heads) & (lax.rem(r, 2) == 0))
        def _():
            project(r // 2)

        @pl.when(r < heads)
        def _():
            features(r)

        @pl.when((r >= chain.lap) & (r < heads + chain.lap))
        def _():
            chain.step(r - chain.lap, local[r - chain.lap])

        @pl.when(r >= chain.lap + 1)
        def _():
            attend(r - chain.lap - 1)

        return 0

    lax.fori_loop(0, heads + chain.lap + 1, one_round, 0)
    chain.drain(heads)


def forward_attention(x, gain, shift, weight, bias, query_map, key_map, bounds, count):
    total_rows, model_width = x.shape
    heads, head_width = query_map.shape[:2]
    micro_count = bounds.shape[0]
    rows = total_rows // micro_count
    height = micro_count * (head_width + 2)
    chunk = (heads, height, 2 * head_width)
    whole = pl.BlockSpec(memory_space=pltpu.VMEM)
    head = (heads, head_width, total_rows)
    feat = (heads, 2 * head_width, total_rows)
    shape = jax.ShapeDtypeStruct
    return pl.pallas_call(
        partial(forward_kernel, count, micro_count),
        out_shape=[
            shape((3 * heads,) + head[1:], bfloat), shape(feat, bfloat), shape(feat, bfloat),
            shape(chunk, single), shape(head, single), shape(head, bfloat),
            shape((heads, 1, total_rows), single),
        ],
        in_specs=[whole] * 7 + [pl.BlockSpec(memory_space=pltpu.SMEM)],
        out_specs=[whole] * 7,
        scratch_shapes=[
            pltpu.VMEM((total_rows, model_width), bfloat),
            pltpu.VMEM((micro_count, rows, rows), single),
            pltpu.VMEM((1, total_rows), single),
            pltpu.VMEM((1, total_rows), single),
            pltpu.VMEM((5,) + chunk[1:], single),
        ]
        + [pltpu.VMEM(chunk, single)] * 5
        + [pltpu.SemaphoreType.DMA((heads,))] * 4,
        compiler_params=pltpu.CompilerParams(
            collective_id=1, has_side_effects=True, vmem_limit_bytes=VMEM_LIMIT
        ),
    )(
        x, gain.reshape(1, -1), shift.reshape(1, -1), weight, bias.reshape(1, -1), query_map,
        key_map, bounds,
    )


def reduce_kernel(count, lines, plans, sources, *refs, ahead=2):
    direct, halved = plans
    total = direct + halved
    arrays = len({s[0] for s in sources})
    inputs, outputs = (refs[:arrays], refs[arrays : 2 * arrays])
    refs = refs[2 * arrays :]
    out, own, got, y_got, zr_got, zl_got, x_got = refs[:7]
    hx_got, hy_got, hzr_got, hzl_got = refs[7:11]
    sems = refs[11:]
    own_sem, core_send, core_recv, y_send, y_recv, zr_send, zr_recv, zl_send, zl_recv = sems[:9]
    x_send, x_recv, hx_send, hx_recv, back_send, back_recv = sems[9:]
    length = count // 2
    rows, wide = out.shape[1:]
    half = wide // 2
    part = rows // lines
    place, column = (lax.axis_index("seq"), lax.axis_index("batch"))
    high, low = (place // 2, lax.rem(place, 2))
    across, core = (column // 2, lax.rem(column, 2))
    mine = pl.ds(pl.multiple_of(core * half, 128), half)
    strip = pl.ds(pl.multiple_of(across * part, 8), part)
    at_core = (place, column + 1 - 2 * core)
    at_y = (place + 1 - 2 * low, column)
    at_right, at_left = ((place + 2, column), (place - 2, column))
    not_first, not_last = (high > 0, high < length - 1)

    def line(d):
        other = lax.rem(across + d, lines)
        return other, (place, other * 2 + core)

    def remote(src, dst, send, recv, device):
        return pltpu.make_async_remote_copy(
            src_ref=src, dst_ref=dst, send_sem=send, recv_sem=recv, device_id=device, device_id_type=MESH
        )

    barrier = pltpu.get_barrier_semaphore()
    for device in [at_core, at_y] + [line(d)[1] for d in range(1, lines)]:
        pl.semaphore_signal(barrier, inc=1, device_id=device, device_id_type=MESH)

    @pl.when(not_last)
    def _():
        pl.semaphore_signal(barrier, inc=1, device_id=at_right, device_id_type=MESH)

    @pl.when(not_first)
    def _():
        pl.semaphore_signal(barrier, inc=1, device_id=at_left, device_id_type=MESH)

    pl.semaphore_wait(barrier, 1 + lines + jnp.where(not_first, 1, 0) + jnp.where(not_last, 1, 0))

    def source(u, column_half):
        array, lead, row, col = sources[u]
        window = (pl.ds(row, rows), pl.ds(pl.multiple_of(col + column_half * half, 128), half))
        if lead is None:
            return inputs[array].at[(slice(None), slice(None)) + window]
        return inputs[array].at[(slice(None), slice(None), lead) + window]

    def load(u):
        return pltpu.make_async_copy(source(u, core), own.at[u], own_sem.at[u])

    def give(u):
        return remote(source(u, 1 - core), got.at[u], core_send.at[u], core_recv.at[u], at_core)

    def begin(r):
        for u in ([r] if r < direct else []) + ([direct + r] if r < halved else []):
            give(u).start()
            load(u).start()

    for r in range(ahead):
        begin(r)

    def settle(u):
        pltpu.make_async_copy(own.at[u], own.at[u], own_sem.at[u]).wait()
        remote(own.at[u], got.at[u], core_send.at[u], core_recv.at[u], at_core).wait_recv()
        own[u] = own[u] + got[u]

    def give_back(u):
        block = out.at[u, :, mine]
        return remote(block, block, back_send.at[u], back_recv.at[u], at_core)

    class Grid:
        def __init__(self, base, window, y, zr, zl):
            self.base, self.window, self.y, self.zr, self.zl = base, window, y, zr, zl

        def block(self, i, h, l):
            return own.at[(self.base + i, h, l) + self.window]

        def y_copy(self, i):
            return remote(
                own.at[(self.base + i, slice(None), 1 - low) + self.window], self.y.at[i],
                y_send.at[self.base + i], y_recv.at[self.base + i], at_y,
            )

        def right(self, i, k):
            return remote(
                self.block(i, k, low), self.zr.at[i, k], zr_send.at[self.base + i, k],
                zr_recv.at[self.base + i, k], at_right,
            )

        def left(self, i, k):
            return remote(
                self.block(i, k, low), self.zl.at[i, k], zl_send.at[self.base + i, k],
                zl_recv.at[self.base + i, k], at_left,
            )

        def from_y(self, i):
            self.y_copy(i).wait_recv()
            target = own.at[(self.base + i, slice(None), low) + self.window]
            target[...] = target[...] + self.y[i]
            self.z_step(i, 1)

        def take_right(self, i, k):
            self.right(i, k).wait_recv()
            target = self.block(i, k, low)
            target[...] = target[...] + self.zr[i, k]

        def take_left(self, i, k):
            self.left(i, k).wait_recv()
            target = self.block(i, k, low)
            target[...] = target[...] + self.zl[i, k]

        def z_step(self, i, t):
            k = high + length - t

            @pl.when(high <= t - 1)
            def _():
                if t > 1:
                    @pl.when(not_first)
                    def _():
                        self.take_right(i, k)

                self.right(i, k).start()

            j = high - length + t

            @pl.when(high >= length - t)
            def _():
                if t > 1:
                    @pl.when(not_last)
                    def _():
                        self.take_left(i, j)

                self.left(i, j).start()

        def z_end(self, i):
            @pl.when(not_first)
            def _():
                self.take_right(i, high)

            @pl.when(not_last)
            def _():
                self.take_left(i, high)

        def drain(self, i):
            self.y_copy(i).wait_send()

            def right_one(k, _):
                self.right(i, k).wait_send()
                return 0

            def left_one(k, _):
                self.left(i, k).wait_send()
                return 0

            lax.fori_loop(high + 1, length, right_one, 0)
            lax.fori_loop(0, high, left_one, 0)

    full = Grid(0, (), y_got, zr_got, zl_got)
    thin = Grid(direct, (strip,), hy_got, hzr_got, hzl_got)

    def x_copy(i, d):
        return remote(
            full.block(i, high, low), x_got.at[i, d - 1], x_send.at[i, d - 1], x_recv.at[i, d - 1], line(d)[1]
        )

    def direct_first(i):
        settle(i)
        full.y_copy(i).start()

    def direct_reduced(i):
        full.z_end(i)
        for d in range(1, lines):
            x_copy(i, d).start()

    def direct_done(i):
        for d in range(1, lines):
            x_copy(i, d).wait_recv()
        value = full.block(i, high, low)[...]
        if lines == 2:
            value = value + x_got[i, 0]
        else:
            parts = []
            for x in range(lines):
                slot = lax.rem(across - x + lines - 1, lines)
                parts.append(jnp.where(x == across, value, x_got[i, jnp.minimum(slot, lines - 2)]))
            value = sum(parts[1:], parts[0])
        out[i, :, mine] = value
        give_back(i).start()

    def strip_copy(i, d):
        other, device = line(d)
        theirs = pl.ds(pl.multiple_of(other * part, 8), part)
        return remote(
            own.at[direct + i, :, :, theirs], hx_got.at[i, d - 1], hx_send.at[i, 0, d - 1],
            hx_recv.at[i, 0, d - 1], device,
        )

    def strip_back(i, d):
        block = out.at[direct + i, strip, mine]
        return remote(block, block, hx_send.at[i, 1, d - 1], hx_recv.at[i, 1, d - 1], line(d)[1])

    def halved_first(i):
        settle(direct + i)
        for d in range(1, lines):
            strip_copy(i, d).start()

    def halved_next(i):
        for d in range(1, lines):
            strip_copy(i, d).wait_recv()
            target = own.at[direct + i, :, :, strip]
            target[...] = target[...] + hx_got[i, d - 1]
        thin.y_copy(i).start()

    def halved_reduced(i):
        thin.z_end(i)
        out[direct + i, strip, mine] = thin.block(i, high, low)[...]
        for d in range(1, lines):
            strip_back(i, d).start()

    def halved_done(i):
        for d in range(1, lines):
            strip_back(i, d).wait_recv()
        give_back(direct + i).start()

    def z_steps(grid):
        return [partial(grid.z_step, t=t) for t in range(2, length)]

    stages = []
    if direct:
        steps = [direct_first, full.from_y] + z_steps(full) + [direct_reduced, direct_done]
        stages += [(s, f, direct) for s, f in enumerate(steps)]
    if halved:
        steps = [halved_first, halved_next, thin.from_y] + z_steps(thin) + [halved_reduced, halved_done]
        stages += [(s, f, halved) for s, f in enumerate(steps)]
    stages.sort(key=lambda s: s[0])
    rounds = max(direct, halved) + stages[-1][0]

    def one_round(r, _):
        for later in range(ahead, max(direct, halved)):
            @pl.when(r == later - ahead)
            def _(later=later):
                begin(later)

        for lag, step, size in stages:
            @pl.when((r >= lag) & (r < lag + size))
            def _(lag=lag, step=step):
                step(r - lag)

        return 0

    lax.fori_loop(0, rounds, one_round, 0)

    def finish(u, _):
        remote(own.at[u], got.at[u], core_send.at[u], core_recv.at[u], at_core).wait_send()
        give_back(u).wait()
        return 0

    lax.fori_loop(0, total, finish, 0)

    def store(u):
        array, lead, row, col = sources[u]
        window = (pl.ds(row, rows), pl.ds(col, wide))
        window = window if lead is None else (lead,) + window
        return pltpu.make_async_copy(out.at[u], outputs[array].at[window], own_sem.at[u])

    for u in range(total):
        store(u).start()

    def drain_direct(i, _):
        full.drain(i)
        for d in range(1, lines):
            x_copy(i, d).wait_send()
        return 0

    def drain_halved(i, _):
        thin.drain(i)
        for d in range(1, lines):
            strip_copy(i, d).wait_send()
            strip_back(i, d).wait_send()
        return 0

    if direct:
        lax.fori_loop(0, direct, drain_direct, 0)
    if halved:
        lax.fori_loop(0, halved, drain_halved, 0)
    for u in range(total):
        store(u).wait()


def reduce_all(arrays, sources, plans, rows, count, lines, identity):
    direct, halved = plans
    total = direct + halved
    length = count // 2
    wide = 768
    half = wide // 2
    part = max(rows // lines, 8)
    spare = max(halved, 1)
    DMA = pltpu.SemaphoreType.DMA
    others = max(lines - 1, 1)
    return pl.pallas_call(
        partial(reduce_kernel, count, lines, plans, sources),
        out_shape=[jax.ShapeDtypeStruct(a.shape[2:], single) for a in arrays],
        in_specs=[pl.BlockSpec(memory_space=pl.ANY)] * len(arrays),
        out_specs=[pl.BlockSpec(memory_space=pl.ANY)] * len(arrays),
        scratch_shapes=[
            pltpu.VMEM((total, rows, wide), single),
            pltpu.VMEM((total, length, 2, rows, half), single),
            pltpu.VMEM((total, length, 2, rows, half), single),
            pltpu.VMEM((max(direct, 1), length, rows, half), single),
            pltpu.VMEM((max(direct, 1), length, rows, half), single),
            pltpu.VMEM((max(direct, 1), length, rows, half), single),
            pltpu.VMEM((max(direct, 1), others, rows, half), single),
            pltpu.VMEM((spare, others, length, 2, part, half), single),
            pltpu.VMEM((spare, length, part, half), single),
            pltpu.VMEM((spare, length, part, half), single),
            pltpu.VMEM((spare, length, part, half), single),
            DMA((total,)), DMA((total,)), DMA((total,)), DMA((total,)), DMA((total,)),
            DMA((total, length)), DMA((total, length)), DMA((total, length)), DMA((total, length)),
            DMA((max(direct, 1), others)), DMA((max(direct, 1), others)),
            DMA((spare, 2, others)), DMA((spare, 2, others)),
            DMA((total,)), DMA((total,)),
        ],
        compiler_params=pltpu.CompilerParams(
            collective_id=identity, has_side_effects=True, vmem_limit_bytes=REDUCE_LIMIT
        ),
    )(*arrays)


def scan_masks(bounds, first_row, row_count, place, micro_count, head_width, reverse):
    def doc(position):
        return doc_number(position, bounds[:, 0], bounds[:, 1])

    low = lax.rem(place, 2)
    base = first_row - low * row_count
    step = 2 * row_count
    if reverse:
        low = 1 - low
        own_edge = doc(first_row)
        pair = doc(base + step - 1)
        ahead = doc(base - 1)
        inner = doc(base + row_count - 1)
    else:
        own_edge = doc(first_row + row_count - 1)
        pair = doc(base - 1)
        ahead = doc(base + step - 1)
        inner = doc(base + row_count - 1)
    if reverse:
        own_edge = doc(first_row - 1)
    one = jnp.ones((micro_count,), single)
    keep = (pair == inner).astype(single)
    masks = jnp.stack(
        [
            (pair == ahead).astype(single),
            (own_edge == ahead).astype(single),
            jnp.where(low == 0, keep, one),
            jnp.where(low == 0, one, 0 * one),
            jnp.where(low == 0, one, keep),
        ]
    )
    wide = jnp.concatenate([jnp.repeat(masks, head_width, axis=1), masks, masks], axis=1)
    return jnp.broadcast_to(wide[:, :, None], wide.shape + (2 * head_width,))


def per_device(
    inputs, gain_one, bias_one, project_weight, project_bias, query_map, key_map, output_weight,
    output_bias, gain_two, bias_two, expand_weight, expand_bias, contract_weight, contract_bias,
    bounds, cotangent,
):
    micro_count, row_count, model_width = inputs.shape
    head_count, head_width = (query_map.shape[0], query_map.shape[1])
    feat_width = 2 * head_width
    total_rows = micro_count * row_count
    count = lax.axis_size("seq")
    place = lax.axis_index("seq")
    first_row = place * row_count
    positions = first_row + jnp.arange(row_count, dtype=jnp.int32)
    first_bound, second_bound = (bounds[:, 0:1], bounds[:, 1:2])
    doc_ids = doc_number(positions[None, :], first_bound, second_bound)
    doc_prev = doc_number(first_row - 1, first_bound, second_bound)
    doc_last = doc_number(first_row + row_count - 1, first_bound, second_bound)
    use_in = (doc_ids == doc_prev).astype(single).reshape(1, total_rows)
    in_last = (doc_ids == doc_last).astype(single).reshape(1, total_rows)
    use_low, last_low = (use_in.astype(bfloat), in_last.astype(bfloat))
    causal = positions[:, None] <= positions[None, :]
    mask = (causal[None] & (doc_ids[:, :, None] == doc_ids[:, None, :])).astype(single)
    masks_reverse = scan_masks(bounds, first_row, row_count, place, micro_count, head_width, True)

    flat_input = inputs.reshape(total_rows, model_width).astype(single)
    normed, unit_one, inverse_one = norm_forward(
        flat_input, gain_one.astype(single), bias_one.astype(single)
    )
    normed_low = normed.astype(bfloat)
    head_rows = lambda offset: pl.BlockSpec((head_width, total_rows), lambda h: (h + offset, 0))
    map_spec = pl.BlockSpec((1, head_width, head_width), lambda h: (h, 0, 0))
    feat_spec = pl.BlockSpec((feat_width, total_rows), lambda h: (h, 0))
    line_spec = pl.BlockSpec((1, total_rows), lambda h: (0, 0))
    den_spec = pl.BlockSpec((1, 1, total_rows), lambda h: (h, 0, 0))
    state_height = micro_count * (head_width + 2)
    state_spec = pl.BlockSpec((1, state_height, feat_width), lambda h: (h, 0, 0))
    mask_spec = pl.BlockSpec((micro_count, row_count, row_count), lambda h: (0, 0, 0))
    q_spec, k_spec, v_spec = (head_rows(0), head_rows(head_count), head_rows(2 * head_count))
    state_shape = jax.ShapeDtypeStruct((head_count, state_height, feat_width), single)
    params = pltpu.CompilerParams(vmem_limit_bytes=VMEM_LIMIT)

    projected, feat_query, feat_key, state_in, attended, attended_low, denominator = forward_attention(
        inputs.reshape(total_rows, model_width), gain_one, bias_one, project_weight, project_bias,
        query_map, key_map, bounds, count,
    )
    projected = projected.reshape(3 * model_width, total_rows)
    feat_query = feat_query.reshape(head_count * feat_width, total_rows)
    feat_key = feat_key.reshape(head_count * feat_width, total_rows)
    attended = attended.reshape(model_width, total_rows)
    attended_low = attended_low.reshape(model_width, total_rows)

    branch = jnp.einsum(
        "er,ed->rd", attended_low, output_weight, preferred_element_type=single
    ) + output_bias.astype(single)
    middle = flat_input + branch
    normed_two, unit_two, inverse_two = norm_forward(
        middle, gain_two.astype(single), bias_two.astype(single)
    )
    normed_two_low = normed_two.astype(bfloat)
    expanded = jnp.dot(
        normed_two_low, expand_weight, preferred_element_type=single
    ) + expand_bias.astype(single)
    gelu_value, gelu_pull = jax.vjp(partial(jax.nn.gelu, approximate=True), expanded)
    hidden_low = gelu_value.astype(bfloat)
    result = (
        middle
        + jnp.dot(hidden_low, contract_weight, preferred_element_type=single)
        + contract_bias.astype(single)
    )
    block_output = result.astype(bfloat).reshape(micro_count, row_count, model_width)
    grad_contract = cotangent.reshape(total_rows, model_width)
    grad_wide = grad_contract.astype(single)
    hidden_grad = jnp.einsum(
        "rd,fd->rf", grad_contract, contract_weight, preferred_element_type=single
    )
    expanded_grad = gelu_pull(hidden_grad)[0].astype(bfloat)
    normed_two_grad = jnp.einsum(
        "rf,df->rd", expanded_grad, expand_weight, preferred_element_type=single
    )
    middle_norm_grad, gain_two_grad, bias_two_grad = norm_backward(
        normed_two_grad, unit_two, inverse_two, gain_two.astype(single)
    )
    middle_grad = grad_wide + middle_norm_grad
    branch_low = middle_grad.astype(bfloat)
    attended_grad = jnp.einsum(
        "rd,ed->er", branch_low, output_weight, preferred_element_type=single
    )
    local_grad = pl.pallas_call(
        partial(state_grad_kernel, micro_count),
        grid=(head_count,),
        in_specs=[head_rows(0), head_rows(0), den_spec, feat_spec, line_spec],
        out_specs=state_spec,
        out_shape=state_shape,
        compiler_params=params,
    )(attended_grad, attended, denominator, feat_query, use_in)
    out_grad = scan_states(local_grad, masks_reverse, count, True, 2)
    proj_spec = pl.BlockSpec((3, head_width, total_rows), lambda h: (0, h, 0))
    projected_grad, query_map_grad, key_map_grad = pl.pallas_call(
        partial(backward_kernel, micro_count),
        grid=(head_count,),
        in_specs=[
            q_spec, k_spec, v_spec, map_spec, map_spec, feat_spec, feat_spec, head_rows(0),
            head_rows(0), den_spec, state_spec, state_spec, mask_spec, line_spec, line_spec,
        ],
        out_specs=[proj_spec, map_spec, map_spec],
        out_shape=[
            jax.ShapeDtypeStruct((3, model_width, total_rows), bfloat),
            jax.ShapeDtypeStruct(query_map.shape, single),
            jax.ShapeDtypeStruct(key_map.shape, single),
        ],
        scratch_shapes=[pltpu.VMEM((feat_width, total_rows), single)] * 2,
        compiler_params=params,
    )(
        projected, projected, projected, query_map, key_map, feat_query, feat_key, attended_grad,
        attended, denominator, state_in, out_grad, mask, use_in, last_low,
    )
    projected_grad = projected_grad.reshape(3 * model_width, total_rows)
    normed_grad = jnp.einsum(
        "cr,dc->rd", projected_grad, project_weight, preferred_element_type=single
    )
    input_norm_grad, gain_one_grad, bias_one_grad = norm_backward(
        normed_grad, unit_one, inverse_one, gain_one.astype(single)
    )
    input_grad = (
        (middle_grad + input_norm_grad).astype(bfloat).reshape(micro_count, row_count, model_width)
    )

    lines = lax.axis_size("batch") // 2
    share = model_width // count
    rows = share // 2 if share // 2 % (8 * lines) == 0 else share
    tiles = (count // 2, 2)
    arrays = [
        jnp.einsum("rf,rd->fd", hidden_low, grad_contract, preferred_element_type=single).reshape(
            tiles + (expand_weight.shape[1] // model_width, share, model_width)
        ),
        jnp.einsum("rd,rf->df", normed_two_low, expanded_grad, preferred_element_type=single),
        jnp.einsum("er,rd->ed", attended_low, branch_low, preferred_element_type=single),
        jnp.einsum("rd,cr->dc", normed_low, projected_grad, preferred_element_type=single),
    ]
    arrays[1:] = [a.reshape(tiles + (share, a.shape[1])) for a in arrays[1:]]
    units = [(0, u, 0) for u in range(arrays[0].shape[2])]
    for a in (1, 2, 3):
        units += [(a, None, c) for c in range(0, arrays[a].shape[3], model_width)]
    chunks = [(a, lead, row, col) for a, lead, col in units for row in range(0, share, rows)]
    if rows % (8 * lines) == 0:
        direct, halved = (chunks[0::2], chunks[1::2])
    else:
        direct, halved = (chunks, [])
    totals = reduce_all(
        arrays, direct + halved, (len(direct), len(halved)), rows, count, lines, 3
    )
    totals = [totals[3], totals[2], totals[1], totals[0].reshape(-1, model_width)]
    project_bias_grad = jnp.sum(projected_grad.astype(single), axis=1)
    output_bias_grad = jnp.sum(branch_low.astype(single), axis=0)
    expand_bias_grad = jnp.sum(expanded_grad.astype(single), axis=0)
    contract_bias_grad = jnp.sum(grad_wide, axis=0)
    small_sums = lax.psum(
        (
            gain_one_grad, bias_one_grad, project_bias_grad, query_map_grad, key_map_grad,
            output_bias_grad, gain_two_grad, bias_two_grad, expand_bias_grad, contract_bias_grad,
        ),
        ("seq", "batch"),
    )
    return (
        block_output, input_grad, small_sums[0], small_sums[1], totals[0], small_sums[2],
        small_sums[3], small_sums[4], totals[1], small_sums[5], small_sums[6], small_sums[7],
        totals[2], small_sums[8], totals[3], small_sums[9],
    )


def solution(mesh):
    rows = P("batch", "seq", None)
    placed = (rows,) + (P(),) * 14 + (P("batch", None), rows)
    shard = P("seq", None)
    return jax.shard_map(
        per_device,
        mesh=mesh,
        in_specs=placed,
        out_specs=(
            rows, rows, P(), P(), shard, P(), P(), P(), shard, P(), P(), P(), shard, P(), shard, P(),
        ),
        check_vma=False,
    )
```

```python
from functools import partial

import jax
import jax.numpy as jnp
from jax import lax
from jax.experimental import pallas as pl
from jax.experimental.pallas import tpu as pltpu
from jax.sharding import PartitionSpec as P

epsilon = 1e-05
bfloat = jnp.bfloat16
single = jnp.float32
MESH = pl.DeviceIdType.MESH
VMEM_LIMIT = 56 * 1024 * 1024
BACKWARD_LIMIT = 63 * 1024 * 1024


def matmul(a, b, contract):
    return lax.dot_general(
        a, b, (((contract[0],), (contract[1],)), ((), ())), preferred_element_type=single
    )


def norm_forward(values, gain_vector, shift_vector):
    centered = values - jnp.mean(values, axis=-1, keepdims=True)
    inverse = lax.rsqrt(jnp.mean(centered * centered, axis=-1, keepdims=True) + epsilon)
    unit_rows = centered * inverse
    return (unit_rows * gain_vector + shift_vector, unit_rows, inverse)


def norm_backward(gradient, unit_rows, inverse, gain_vector):
    inner = gradient * gain_vector
    result = inverse * (
        inner
        - jnp.mean(inner, axis=-1, keepdims=True)
        - unit_rows * jnp.mean(inner * unit_rows, axis=-1, keepdims=True)
    )
    return (result, jnp.sum(gradient * unit_rows, axis=0), jnp.sum(gradient, axis=0))


def two_softmaxes(mapped):
    up = jnp.exp(mapped - jnp.max(mapped, axis=0, keepdims=True))
    down = jnp.exp(jnp.min(mapped, axis=0, keepdims=True) - mapped)
    return (
        up / jnp.sum(up, axis=0, keepdims=True),
        down / jnp.sum(down, axis=0, keepdims=True),
    )


def flat(vector):
    return vector.astype(single).reshape(1, -1)


def with_ones(rows):
    return jnp.concatenate([rows, jnp.ones((16, rows.shape[1]), rows.dtype)], axis=0)


def state_rows(state, micro, micro_count, head_width):
    low = state[micro * head_width : (micro + 1) * head_width, :]
    row = micro_count * head_width + micro
    total = state[row : row + 1, :]
    return jnp.concatenate([low, jnp.broadcast_to(total, (16, low.shape[1]))], axis=0)


def score_grads(grad, attended, denom):
    inverse = 1.0 / denom
    numer_grad = grad * inverse
    denom_grad = -jnp.sum(grad * attended, axis=0, keepdims=True) * inverse
    pad = jnp.zeros((15, grad.shape[1]), single)
    return jnp.concatenate([numer_grad, denom_grad, pad], axis=0)


def feature_backward(feat_grad, source, weights):
    head_width = source.shape[0]
    up, down = two_softmaxes(matmul(weights, source, (0, 0)))
    grad_up, grad_down = (feat_grad[:head_width], feat_grad[head_width:])
    mapped = up * (grad_up - jnp.sum(up * grad_up, axis=0, keepdims=True)) - down * (
        grad_down - jnp.sum(down * grad_down, axis=0, keepdims=True)
    )
    low = mapped.astype(bfloat)
    return (matmul(weights, low, (1, 0)), matmul(source, low, (1, 1)))


def document(position, bounds_ref, m):
    return jnp.where(position >= bounds_ref[0, m], 1, 0) + jnp.where(
        position >= bounds_ref[1, m], 1, 0
    )


def token_masks(bounds_ref, first_row, rows, micro_count, mask_ref, use_ref, last_ref):
    low_shape, line_shape = ((rows, rows), (1, rows))
    source = first_row + lax.broadcasted_iota(jnp.int32, low_shape, 0)
    target = first_row + lax.broadcasted_iota(jnp.int32, low_shape, 1)
    line = first_row + lax.broadcasted_iota(jnp.int32, line_shape, 1)
    for m in range(micro_count):
        part = slice(m * rows, (m + 1) * rows)
        same = document(source, bounds_ref, m) == document(target, bounds_ref, m)
        mask_ref[m] = jnp.where((source <= target) & same, 1.0, 0.0)
        own = document(line, bounds_ref, m)
        use_ref[:, part] = jnp.where(own == document(first_row - 1, bounds_ref, m), 1.0, 0.0)
        last_ref[:, part] = jnp.where(
            own == document(first_row + rows - 1, bounds_ref, m), 1.0, 0.0
        )


def chain_masks(bounds_ref, first_row, low, rows, micro_count, head_width, reverse, mask_ref):
    base = first_row - low * rows
    step = 2 * rows
    height, wide = mask_ref.shape[1:]
    for m in range(micro_count):
        def doc(position, m=m):
            return document(position, bounds_ref, m)

        inner = doc(base + rows - 1)
        if reverse:
            lead = 1 - low
            own_edge, pair, ahead = (doc(first_row - 1), doc(base + step - 1), doc(base - 1))
        else:
            lead = low
            own_edge, pair, ahead = (
                doc(first_row + rows - 1), doc(base - 1), doc(base + step - 1),
            )
        keep = jnp.where(pair == inner, 1.0, 0.0)
        values = [
            jnp.where(pair == ahead, 1.0, 0.0),
            jnp.where(own_edge == ahead, 1.0, 0.0),
            jnp.where(lead == 0, keep, 1.0),
            jnp.where(lead == 0, 1.0, 0.0),
            jnp.where(lead == 0, 1.0, keep),
        ]
        for i, value in enumerate(values):
            mask_ref[i, m * head_width : (m + 1) * head_width, :] = jnp.full(
                (head_width, wide), value
            )
            tail = slice(micro_count * head_width, height)
            row = lax.broadcasted_iota(jnp.int32, (height - tail.start, wide), 0)
            before = jnp.zeros(row.shape, single) if m == 0 else mask_ref[i, tail, :]
            mask_ref[i, tail, :] = jnp.where(lax.rem(row, micro_count) == m, value, before)


CHAIN_RING = 4


class Chain:
    def __init__(self, reverse, count, carry, onward, aside, beside, mask, sems):
        self.carry, self.onward, self.aside, self.beside = carry, onward, aside, beside
        self.mask, self.sems = mask, sems
        place, self.column = (lax.axis_index("seq"), lax.axis_index("batch"))
        high, low = (place // 2, lax.rem(place, 2))
        length = count // 2
        self.lap = length - 1 - high if reverse else high
        self.ahead, self.behind = (place - 2, place + 2) if reverse else (place + 2, place - 2)
        self.partner = place + 1 - 2 * low
        self.first, self.final = (self.lap == 0, self.lap == length - 1)

    def greet(self, barrier):
        def signal(place):
            pl.semaphore_signal(
                barrier, inc=1, device_id=(place, self.column), device_id_type=MESH
            )

        signal(self.partner)

        @pl.when(jnp.logical_not(self.final))
        def _():
            signal(self.ahead)

        @pl.when(jnp.logical_not(self.first))
        def _():
            signal(self.behind)

        return 1 + jnp.where(self.first, 0, 1) + jnp.where(self.final, 0, 1)

    def along(self, i):
        return pltpu.make_async_remote_copy(
            src_ref=self.onward.at[lax.rem(i, CHAIN_RING)], dst_ref=self.carry.at[i], send_sem=self.sems[0].at[i],
            recv_sem=self.sems[1].at[i], device_id=(self.ahead, self.column), device_id_type=MESH,
        )

    def across(self, i):
        return pltpu.make_async_remote_copy(
            src_ref=self.aside.at[lax.rem(i, CHAIN_RING)], dst_ref=self.beside.at[i], send_sem=self.sems[2].at[i],
            recv_sem=self.sems[3].at[i], device_id=(self.partner, self.column),
            device_id_type=MESH,
        )

    def start(self):
        @pl.when(self.first)
        def _():
            self.carry[...] = jnp.zeros_like(self.carry)

    def step(self, i, local):
        @pl.when(jnp.logical_not(self.first))
        def _():
            self.along(i).wait_recv()

        @pl.when(i >= CHAIN_RING)
        def _():
            self.sent(i - CHAIN_RING)

        state, slot = (self.carry[i], lax.rem(i, CHAIN_RING))

        @pl.when(jnp.logical_not(self.final))
        def _():
            self.onward[slot] = self.mask[0] * state + self.mask[1] * local
            self.along(i).start()

        self.aside[slot] = self.mask[2] * state + self.mask[3] * local
        self.across(i).start()

    def sent(self, i):
        self.across(i).wait_send()

        @pl.when(jnp.logical_not(self.final))
        def _():
            self.along(i).wait_send()

    def result(self, i):
        self.across(i).wait_recv()
        return self.mask[4] * self.carry[i] + self.beside[i]

    def drain(self, chunks):
        def one(i, _):
            self.sent(i)
            return 0

        lax.fori_loop(max(chunks - CHAIN_RING, 0), chunks, one, 0)


def local_state(wide, other, micro_count, head_width, target):
    rows = wide.shape[1] // micro_count
    sums = []
    for m in range(micro_count):
        part = slice(m * rows, (m + 1) * rows)
        local = matmul(wide[:, part], other[:, part], (1, 1))
        target[m * head_width : (m + 1) * head_width, :] = local[:head_width]
        sums.append(local[head_width : head_width + 1])
    target[micro_count * head_width :, :] = jnp.concatenate(sums + sums, axis=0)


def forward_kernel(
    count, micro_count, x_ref, gain_ref, shift_ref, weight_ref, bias_ref, qm_ref, km_ref,
    bounds_ref, proj_ref, fq_ref, fk_ref, state_ref, att_ref, low_ref, den_ref, norm_ref, turned_ref,
    normed, bias_row, mask, use, last, chain_mask, local, carry, onward, aside, beside, *sems,
):
    heads, head_width = qm_ref.shape[:2]
    total_rows = x_ref.shape[0]
    rows = total_rows // micro_count
    model_width = x_ref.shape[1]
    pair = 2 * head_width
    place = lax.axis_index("seq")
    first_row = place * rows
    chain = Chain(False, count, carry, onward, aside, beside, chain_mask, sems)
    barrier = pltpu.get_barrier_semaphore()
    greeted = chain.greet(barrier)
    token_masks(bounds_ref, first_row, rows, micro_count, mask, use, last)
    chain_masks(
        bounds_ref, first_row, lax.rem(place, 2), rows, micro_count, head_width, False, chain_mask
    )
    chain.start()
    bias_row[...] = flat(bias_ref[...])
    normed[...] = norm_forward(
        x_ref[...].astype(single), flat(gain_ref[...]), flat(shift_ref[...])
    )[0].astype(bfloat)
    pl.semaphore_wait(barrier, greeted)
    norm_ref[...] = normed[...].T
    turned_ref[...] = x_ref[...].T

    def project(p):
        for part in range(3):
            columns = pl.ds(pl.multiple_of(part * model_width + p * pair, pair), pair)
            value = matmul(normed[...], weight_ref[:, columns], (1, 0))
            value = (value + bias_row[:, columns]).astype(bfloat).T
            proj_ref[part * heads + 2 * p] = value[:head_width]
            proj_ref[part * heads + 2 * p + 1] = value[head_width:]

    def features(h):
        for offset, weights, target in ((0, qm_ref, fq_ref), (heads, km_ref, fk_ref)):
            mapped = matmul(weights[h], proj_ref[offset + h], (0, 0))
            up, down = two_softmaxes(mapped)
            target[h] = jnp.concatenate([up, down], axis=0).astype(bfloat)
        wide = with_ones(proj_ref[2 * heads + h]) * last[...].astype(bfloat)
        local_state(wide, fk_ref.at[h], micro_count, head_width, local.at[h])

    def attend(h):
        state_ref[h] = chain.result(h)
        wide = with_ones(proj_ref[2 * heads + h])
        used = fq_ref[h] * use[...].astype(bfloat)
        for m in range(micro_count):
            part = slice(m * rows, (m + 1) * rows)
            scores = matmul(fk_ref[h, :, part], fq_ref[h, :, part], (0, 0)) * mask[m]
            state = state_rows(state_ref.at[h], m, micro_count, head_width).astype(bfloat)
            numer = matmul(wide[:, part], scores.astype(bfloat), (1, 0)) + matmul(
                state, used[:, part], (1, 0)
            )
            denom = numer[head_width : head_width + 1]
            attended = numer[:head_width] / denom
            att_ref[h, :, part] = attended
            low_ref[h, :, part] = attended.astype(bfloat)
            den_ref[h, :, part] = denom

    def one_round(r, _):
        @pl.when((r < heads) & (lax.rem(r, 2) == 0))
        def _():
            project(r // 2)

        @pl.when(r < heads)
        def _():
            features(r)

        @pl.when((r >= chain.lap) & (r < heads + chain.lap))
        def _():
            chain.step(r - chain.lap, local[r - chain.lap])

        @pl.when(r >= chain.lap + 1)
        def _():
            attend(r - chain.lap - 1)

        return 0

    lax.fori_loop(0, heads + chain.lap + 1, one_round, 0)
    chain.drain(heads)


def forward_attention(x, gain, shift, weight, bias, query_map, key_map, bounds, count):
    total_rows, model_width = x.shape
    heads, head_width = query_map.shape[:2]
    micro_count = bounds.shape[0]
    rows = total_rows // micro_count
    height = micro_count * (head_width + 2)
    chunk = (heads, height, 2 * head_width)
    whole = pl.BlockSpec(memory_space=pltpu.VMEM)
    head = (heads, head_width, total_rows)
    feat = (heads, 2 * head_width, total_rows)
    shape = jax.ShapeDtypeStruct
    return pl.pallas_call(
        partial(forward_kernel, count, micro_count),
        out_shape=[
            shape((3 * heads,) + head[1:], bfloat), shape(feat, bfloat), shape(feat, bfloat),
            shape(chunk, single), shape(head, single), shape(head, bfloat),
            shape((heads, 1, total_rows), single), shape((model_width, total_rows), bfloat),
            shape((model_width, total_rows), bfloat),
        ],
        in_specs=[whole] * 7 + [pl.BlockSpec(memory_space=pltpu.SMEM)],
        out_specs=[whole] * 9,
        scratch_shapes=[
            pltpu.VMEM((total_rows, model_width), bfloat),
            pltpu.VMEM((1, 3 * model_width), single),
            pltpu.VMEM((micro_count, rows, rows), single),
            pltpu.VMEM((1, total_rows), single),
            pltpu.VMEM((1, total_rows), single),
            pltpu.VMEM((5,) + chunk[1:], single),
        ]
        + [pltpu.VMEM(chunk, single)] * 2
        + [pltpu.VMEM((CHAIN_RING,) + chunk[1:], single)] * 2
        + [pltpu.VMEM(chunk, single)]
        + [pltpu.SemaphoreType.DMA((heads,))] * 4,
        compiler_params=pltpu.CompilerParams(
            collective_id=1, has_side_effects=True, vmem_limit_bytes=VMEM_LIMIT
        ),
    )(
        x, gain, shift, weight, bias, query_map, key_map, bounds.T,
    )


def remote(src, dst, send, recv, device):
    return pltpu.make_async_remote_copy(
        src_ref=src, dst_ref=dst, send_sem=send, recv_sem=recv, device_id=device,
        device_id_type=MESH,
    )


FIRST, FIRST_ROWS, SECOND_ROWS = (8, 32, 32)


class Spot:
    def __init__(self, count, lines):
        self.place, self.column = (lax.axis_index("seq"), lax.axis_index("batch"))
        self.high, self.low = (self.place // 2, lax.rem(self.place, 2))
        self.across, self.core = (self.column // 2, lax.rem(self.column, 2))
        self.length, self.lines = (count // 2, lines)
        self.at_core = (self.place, self.column + 1 - 2 * self.core)
        self.at_y = (self.place + 1 - 2 * self.low, self.column)
        self.at_right, self.at_left = ((self.place + 2, self.column), (self.place - 2, self.column))
        self.not_first, self.not_last = (self.high > 0, self.high < self.length - 1)

    def line(self, d):
        other = lax.rem(self.across + d, self.lines)
        return other, (self.place, other * 2 + self.core)

    def along(self, d):
        count = 2 * self.length
        other = lax.rem(self.place + d, count)
        return other, (other, self.column)

    def greet(self, barrier):
        devices = [self.at_core]
        devices += [self.line(d)[1] for d in range(1, self.lines)]
        devices += [self.along(d)[1] for d in range(1, 2 * self.length)]
        other = self.at_core[1]
        devices += [(self.along(d)[0], other) for d in range(1, 2 * self.length)]
        for device in devices:
            pl.semaphore_signal(barrier, inc=1, device_id=device, device_id_type=MESH)
        return len(devices)


class Track:
    def __init__(
        self, spot, base, halved, rows, offset, ring, out, own, got, y_got, z_got, x_got, sems
    ):
        self.base = base
        self.spot, self.halved, self.rows, self.offset, self.ring = spot, halved, rows, offset, ring
        self.out, self.own, self.got, self.y_got, self.z_got, self.x_got = (
            out, own, got, y_got, z_got, x_got,
        )
        (
            self.load_sem, self.core_send, self.core_recv, self.y_send, self.y_recv, self.zr_send,
            self.zr_recv, self.zl_send, self.zl_recv, self.x_send, self.x_recv, self.back_send,
            self.back_recv,
        ) = sems
        half = own.shape[-1]
        self.mine = pl.ds(pl.multiple_of(spot.core * half, 128), half)
        self.theirs = pl.ds(pl.multiple_of((1 - spot.core) * half, 128), half)
        self.part = rows // spot.lines if halved else rows
        self.strip = self.window(spot.across) if halved else slice(None)

    def window(self, line, base=0):
        return pl.ds(pl.multiple_of(base + line * self.part, 8), self.part)

    def source(self, ref, col, columns):
        half = self.own.shape[-1]
        cols = pl.ds(pl.multiple_of(col + columns * half, 128), half)
        return ref.at[:, :, pl.ds(self.offset, self.rows), cols]

    def give(self, u, source):
        return remote(
            source, self.got.at[lax.rem(u, self.ring)], self.core_send.at[u],
            self.core_recv.at[u], self.spot.at_core,
        )

    def begin(self, u, ref, col):
        self.give(u, self.source(ref, col, 1 - self.spot.core)).start()
        pltpu.make_async_copy(
            self.source(ref, col, self.spot.core), self.own.at[u], self.load_sem.at[u]
        ).start()

    def settle(self, u):
        pltpu.make_async_copy(self.own.at[u], self.own.at[u], self.load_sem.at[u]).wait()
        self.give(u, self.own.at[u]).wait_recv()
        self.own[u] = self.own[u] + self.got[lax.rem(u, self.ring)]

    def given(self, u):
        self.give(u, self.own.at[u]).wait_send()

    def cut(self, u, d):
        other, device = self.spot.line(d)
        return remote(
            self.own.at[u, :, :, self.window(other)], self.x_got.at[u, d - 1],
            self.x_send.at[u, 0, d - 1], self.x_recv.at[u, 0, d - 1], device,
        )

    def first(self, u):
        self.settle(u)
        if self.halved:
            for d in range(1, self.spot.lines):
                self.cut(u, d).start()
        else:
            self.y_copy(u).start()

    def cut_taken(self, u):
        for d in range(1, self.spot.lines):
            self.cut(u, d).wait_recv()
            target = self.own.at[u, :, :, self.strip]
            target[...] = target[...] + self.x_got[u, d - 1]
        self.y_copy(u).start()

    def y_copy(self, u):
        return remote(
            self.own.at[u, :, 1 - self.spot.low, self.strip], self.y_got.at[u],
            self.y_send.at[u], self.y_recv.at[u], self.spot.at_y,
        )

    def y_taken(self, u):
        self.y_copy(u).wait_recv()
        target = self.own.at[u, :, self.spot.low, self.strip]
        target[...] = target[...] + self.y_got[u]
        self.z_step(u, 1)

    def block(self, u, h):
        return self.own.at[u, h, self.spot.low, self.strip]

    def right(self, u, k):
        return remote(
            self.block(u, k), self.z_got.at[u, k], self.zr_send.at[u, k], self.zr_recv.at[u, k],
            self.spot.at_right,
        )

    def left(self, u, k, taker):
        slot = jnp.where(k == taker, self.spot.length, k)
        return remote(
            self.block(u, k), self.z_got.at[u, slot], self.zl_send.at[u, k], self.zl_recv.at[u, k],
            self.spot.at_left,
        )

    def take_right(self, u, k):
        self.right(u, k).wait_recv()
        target = self.block(u, k)
        target[...] = target[...] + self.z_got[u, k]

    def take_left(self, u, k):
        high = self.spot.high
        self.left(u, k, high).wait_recv()
        target = self.block(u, k)
        target[...] = target[...] + self.z_got[u, jnp.where(k == high, self.spot.length, k)]

    def z_step(self, u, t):
        spot = self.spot
        k = spot.high + spot.length - t

        @pl.when(spot.high <= t - 1)
        def _():
            if t > 1:
                @pl.when(spot.not_first)
                def _():
                    self.take_right(u, k)

            self.right(u, k).start()

        j = spot.high - spot.length + t

        @pl.when(spot.high >= spot.length - t)
        def _():
            if t > 1:
                @pl.when(spot.not_last)
                def _():
                    self.take_left(u, j)

            self.left(u, j, spot.high - 1).start()

    def z_end(self, u):
        @pl.when(self.spot.not_first)
        def _():
            self.take_right(u, self.spot.high)

        @pl.when(self.spot.not_last)
        def _():
            self.take_left(u, self.spot.high)

    def x_copy(self, u, d):
        return remote(
            self.block(u, self.spot.high), self.x_got.at[u, d - 1], self.x_send.at[u, 0, d - 1],
            self.x_recv.at[u, 0, d - 1], self.spot.line(d)[1],
        )

    def x_back(self, u, d):
        rows = self.window(self.spot.across, self.offset)
        return remote(
            self.block(u, self.spot.high), self.out.at[self.base + u, rows, self.mine],
            self.x_send.at[u, 1, d - 1], self.x_recv.at[u, 1, d - 1], self.spot.line(d)[1],
        )

    def keep(self, u):
        rows = (
            self.window(self.spot.across, self.offset)
            if self.halved
            else pl.ds(self.offset, self.rows)
        )
        return pltpu.make_async_copy(
            self.block(u, self.spot.high), self.out.at[self.base + u, rows, self.mine], self.load_sem.at[u]
        )

    def reduced(self, u):
        self.z_end(u)
        if self.halved:
            self.keep(u).start()
        for d in range(1, self.spot.lines):
            (self.x_back if self.halved else self.x_copy)(u, d).start()

    def back(self, u):
        block = self.out.at[self.base + u, pl.ds(self.offset, self.rows), self.mine]
        source = block if self.halved else self.block(u, self.spot.high)
        return remote(source, block, self.back_send.at[u], self.back_recv.at[u], self.spot.at_core)

    def total(self, u):
        spot = self.spot
        for d in range(1, spot.lines):
            self.x_copy(u, d).wait()
        value = self.block(u, spot.high)[...]
        if spot.lines == 2:
            value = value + self.x_got[u, 0]
        else:
            parts = []
            for x in range(spot.lines):
                slot = lax.rem(spot.across - x + spot.lines - 1, spot.lines)
                slot = jnp.minimum(slot, spot.lines - 2)
                parts.append(jnp.where(x == spot.across, value, self.x_got[u, slot]))
            value = sum(parts[1:], parts[0])
        self.block(u, spot.high)[...] = value

    def done(self, u):
        if self.halved:
            for d in range(1, self.spot.lines):
                self.x_back(u, d).wait_recv()
            self.keep(u).wait()
        else:
            self.total(u)
            self.keep(u).start()
        self.back(u).start()

    def finish(self, u):
        self.back(u).wait()
        if not self.halved:
            self.keep(u).wait()

    def steps(self):
        z_steps = [partial(self.z_step, t=t) for t in range(2, self.spot.length)]
        cut = [self.cut_taken] if self.halved else []
        return [self.first] + cut + [self.y_taken] + z_steps + [self.reduced, self.done]

    def drain(self, u):
        self.y_copy(u).wait_send()
        for d in range(1, self.spot.lines):
            if self.halved:
                self.cut(u, d).wait_send()
                self.x_back(u, d).wait_send()

        def right_one(k, _):
            self.right(u, k).wait_send()
            return 0

        def left_one(k, _):
            self.left(u, k, self.spot.high - 1).wait_send()
            return 0

        lax.fori_loop(self.spot.high + 1, self.spot.length, right_one, 0)
        lax.fori_loop(0, self.spot.high, left_one, 0)


def bands(units, share, lines):
    groups = []
    for low, high, direct in ((0, FIRST, FIRST_ROWS), (FIRST, units, SECOND_ROWS)):
        direct = direct * share // 96
        if direct % 8 or (share - direct) % (8 * lines):
            return [(0, units, share, 0)]
        groups.append((low, high, direct, share - direct))
    return groups


def track_scratch(units, length, lines, rows, halved, ring, half):
    part = rows // lines if halved else rows
    DMA = pltpu.SemaphoreType.DMA
    others = lines - 1
    buffers = [
        pltpu.VMEM((units, length, 2, rows, half), single),
        pltpu.VMEM((ring, length, 2, rows, half), single),
        pltpu.VMEM((units, length, part, half), single),
        pltpu.VMEM((units, length + 1, part, half), single),
        pltpu.VMEM((units, others) + ((length, 2) if halved else ()) + (part, half), single),
    ]
    line = DMA((units, length))
    ends = DMA((units, 2, others))
    one = DMA((units,))
    return buffers + [one] * 5 + [line] * 4 + [ends] * 2 + [one] * 2


BEAT = 2


def unit_order(early, late, gap, length):
    order, starts, left = ([], [], list(range(early)))
    ready = {length + 2 + gap * g: early + g for g in range(late)}
    t = 0
    while len(order) < early + late:
        if t in ready or left:
            order.append(ready[t] if t in ready else left.pop(0))
            starts.append(t)
        t += 1
    return order, starts


def backward_kernel(
    count, lines, micro_count, early, proj_hbm, fq_hbm, fk_hbm, state_hbm, att_hbm, den_hbm,
    grad_hbm, qm_ref, km_ref, norm_ref, weight_ref, x_ref, mid_ref, gain_ref, vector_ref,
    bounds_ref, contract_ref, expand_ref, output_ref, out, in_grad_ref, qm_out, km_out, rows_out, bias_out, expand_bias_out,
    proj, fq_buf, fk_buf, state_buf, att_buf, den_buf, grad_buf, load_sem, pg_ref,
    mask, use, last, chain_mask, local, carry, onward, aside, beside, fqg, fkg, product, small,
    small_sum, small_out, gather_send, gather_recv, gather_keep, credit, *rest,
):
    heads, head_width = qm_ref.shape[:2]
    total_rows = pg_ref.shape[-1]
    rows = total_rows // micro_count
    model_width = heads * head_width
    sources = (contract_ref, expand_ref, output_ref)
    share, wide = out.shape[1:]
    group = wide // (3 * head_width)
    late = heads // group
    units = len(early) + late
    spot = Spot(count, lines)
    length = spot.length
    order, starts = unit_order(len(early), late, group // BEAT, length)
    chain_sems, rest = (rest[:4], rest[4:])
    chain = Chain(True, count, carry, onward, aside, beside, chain_mask, chain_sems)
    ring, half = (2, wide // 2)
    little = Track(spot, 0, False, small.shape[2], 0, 1, small_sum, *rest[:5], rest[5:18])
    rest = rest[18:]
    groups = []
    for low, high, direct, halved in bands(units, share, lines):
        group_tracks = []
        for kind, band, offset in ((False, direct, 0), (True, halved, direct)):
            if band:
                group_tracks.append(
                    Track(spot, low, kind, band, offset, ring, out, *rest[:5], rest[5:18])
                )
                rest = rest[18:]
        groups.append((low, high, group_tracks))
    slots = proj.shape[0]

    def loads(h):
        slot = lax.rem(h, slots)
        pairs = [(proj_hbm.at[:, h], proj.at[slot])]
        for source, target in (
            (fq_hbm, fq_buf), (fk_hbm, fk_buf), (state_hbm, state_buf), (att_hbm, att_buf),
            (den_hbm, den_buf), (grad_hbm, grad_buf),
        ):
            pairs.append((source.at[h], target.at[slot]))
        return [
            pltpu.make_async_copy(source, target, load_sem.at[slot, i])
            for i, (source, target) in enumerate(pairs)
        ]

    for h in range(BEAT):
        for copy in loads(h):
            copy.start()
    barrier = pltpu.get_barrier_semaphore()
    greeted = spot.greet(barrier)
    pl.semaphore_wait(barrier, greeted)

    def tracks_of(u):
        return [t for low, high, tracks in groups for t in tracks if low <= u < high]

    def begin(u):
        if u >= ring:
            pl.semaphore_wait(credit, 1)
        if order[u] < len(early):
            array, lead, col = early[order[u]]
            ref = sources[array]
            ref = ref if lead is None else ref.at[:, :, lead]
        else:
            ref, col = (product, 0)
        for track in tracks_of(u):
            track.begin(u - track.base, ref, col)

    def settled(u):
        @pl.when(u + ring < units)
        def _():
            pl.semaphore_signal(credit, inc=1, device_id=spot.at_core, device_id_type=MESH)

    def state_grad(h):
        for copy in loads(h):
            copy.wait()
        slot = lax.rem(h, slots)
        wide_grad = score_grads(grad_buf[slot], att_buf[slot], den_buf[slot]) * use[...]
        local_state(wide_grad.astype(bfloat), fq_buf.at[slot], micro_count, head_width, local)

    def attend_back(h):
        slot = lax.rem(h, slots)
        beside[h] = chain.result(h)
        grads = score_grads(grad_buf[slot], att_buf[slot], den_buf[slot])
        low_grads = grads.astype(bfloat)
        used_grads = (grads * use[...]).astype(bfloat)
        last_low = last[...].astype(bfloat)
        wide_value = with_ones(proj[slot, 2])
        wide_last = wide_value * last_low
        for m in range(micro_count):
            part = slice(m * rows, (m + 1) * rows)
            fq, fk = (fq_buf[slot, :, part], fk_buf[slot, :, part])
            scores = (matmul(fk, fq, (0, 0)) * mask[m]).astype(bfloat)
            grad_scores = (
                matmul(wide_value[:, part], low_grads[:, part], (0, 0)) * mask[m]
            ).astype(bfloat)
            state = state_rows(state_buf.at[slot], m, micro_count, head_width).astype(bfloat)
            out_grad = state_rows(beside.at[h], m, micro_count, head_width)
            row = lax.broadcasted_iota(jnp.int32, out_grad.shape, 0)
            out_grad = jnp.where(row <= head_width, out_grad, 0.0).astype(bfloat)
            fqg[:, part] = matmul(fk, grad_scores, (1, 0)) + matmul(
                state, used_grads[:, part], (0, 0)
            )
            fkg[:, part] = matmul(fq, grad_scores, (1, 1)) + matmul(
                out_grad, wide_last[:, part], (0, 0)
            )
            value_grad = matmul(low_grads[:head_width, part], scores, (1, 1)) + matmul(
                out_grad[:head_width], fk * last_low[:, part], (1, 0)
            )
            pg_ref[2, h, :, part] = value_grad.astype(bfloat)
        q_grad, qmg = feature_backward(fqg[...], proj[slot, 0], qm_ref[h])
        pg_ref[0, h] = q_grad.astype(bfloat)
        qm_out[h] = qmg
        k_grad, kmg = feature_backward(fkg[...], proj[slot, 1], km_ref[h])
        pg_ref[1, h] = k_grad.astype(bfloat)
        km_out[h] = kmg

    def late_begin(g):
        if g > 0:
            u = order.index(len(early) + g - 1)
            for track in tracks_of(u):
                track.given(u - track.base)
        columns = group * head_width
        for p in range(3):
            low = pg_ref[p, g * group : (g + 1) * group].reshape(columns, -1)
            value = matmul(norm_ref[...], low, (1, 1))
            product[:, :, :, p * columns : (p + 1) * columns] = value.reshape(
                product.shape[:3] + (columns,)
            )
        begin(order.index(len(early) + g))

    def input_back():
        gain_sum, bias_sum = (0.0, 0.0)
        gain = jnp.broadcast_to(flat(gain_ref[...]), (128, model_width)).T[:, :1]
        step = 2 * rows
        for start in range(0, total_rows, step):
            part = slice(start, start + step)
            grad = sum(
                matmul(
                    weight_ref[:, p * model_width : (p + 1) * model_width],
                    pg_ref[p, :, :, part].reshape(model_width, step), (1, 0),
                )
                for p in range(3)
            )
            value = x_ref[:, part].astype(single)
            value = value - jnp.mean(value, axis=0, keepdims=True)
            inverse = lax.rsqrt(jnp.mean(value * value, axis=0, keepdims=True) + epsilon)
            value = value * inverse
            inner = grad * gain
            result = mid_ref[:, part] + inverse * (
                inner
                - jnp.mean(inner, axis=0, keepdims=True)
                - value * jnp.mean(inner * value, axis=0, keepdims=True)
            )
            in_grad_ref[part, :] = result.T.astype(bfloat)
            gain_sum += jnp.sum((grad * value).T, axis=0, keepdims=True)
            bias_sum += jnp.sum(grad.T, axis=0, keepdims=True)
        ones = jnp.ones((16, total_rows), bfloat)
        sums = [
            matmul(ones, pg_ref[p].reshape(model_width, total_rows), (1, 1))[:1] for p in range(3)
        ]
        blank = jnp.zeros((4, model_width), single)
        vectors = vector_ref[...] + jnp.concatenate(
            [gain_sum, bias_sum, blank] + sums + [blank, blank[:3]], axis=0
        )
        maps = [
            jnp.concatenate([ref[h] for h in range(heads)], axis=1) for ref in (qm_out, km_out)
        ]
        size = small.shape[0] * small.shape[1] * small.shape[2]
        used = 2 * head_width + vectors.shape[0]
        pad = [jnp.zeros((size - used, model_width), single)] if size > used else []
        small[...] = jnp.concatenate(maps + [vectors] + pad, axis=0).reshape(small.shape)
        little.begin(0, small, 0)

    others = [(d, 0) for d in range(1, count)] + [(d, 1) for d in range(count)]

    def spread(k, incoming):
        d, other_core = others[k]
        here, there = (spot.place, lax.rem(spot.place + d, count))
        core = lax.rem(spot.core + other_core, 2)
        device = (there, 2 * spot.across + core)
        side = pl.ds(pl.multiple_of((core if incoming else spot.core) * half, 128), half)
        place, its_core = (there, core) if incoming else (here, spot.core)
        return remote(
            little.block(0, spot.high), small_out.at[place, :, side], gather_send.at[k],
            gather_recv.at[place, its_core], device,
        )

    def spread_keep():
        return pltpu.make_async_copy(
            little.block(0, spot.high), small_out.at[spot.place, :, little.mine],
            gather_keep.at[0],
        )

    def little_done(u):
        little.total(u)
        spread_keep().start()
        for k in range(len(others)):
            spread(k, False).start()

    little_steps = little.steps()[:-1] + [little_done]
    stages = [
        (s, f, low, high)
        for low, high, tracks in groups
        for track in tracks
        for s, f in enumerate(track.steps())
    ]
    stages.sort(key=lambda s: (s[0], s[2]))
    ahead = 1
    for u in range(ahead):
        begin(u)
    first_row = spot.place * rows
    token_masks(bounds_ref, first_row, rows, micro_count, mask, use, last)
    chain_masks(
        bounds_ref, first_row, spot.low, rows, micro_count, head_width, True, chain_mask
    )
    chain.start()

    def unit_at(t):
        if starts == list(range(units)):
            return t, (t >= 0) & (t < units)
        u, valid = (0, False)
        for start in starts:
            u = u + jnp.where(t > start, 1, 0)
            valid = valid | (t == start)
        return u, valid

    beats = heads // BEAT

    def one_round(r, _):
        c = r - chain.lap

        @pl.when((c >= 0) & (c < beats))
        def _():
            for i in range(BEAT):
                h = c * BEAT + i
                state_grad(h)
                chain.step(h, local[...])

        for u in range(ahead, units):
            if order[u] < len(early):
                @pl.when(r == starts[u] - ahead)
                def _(u=u):
                    begin(u)

        for lag, step, low, high in stages:
            u, valid = unit_at(r - lag)

            @pl.when(valid & (u >= low) & (u < high))
            def _(u=u, step=step, low=low):
                step(u - low)

        u, valid = unit_at(r)

        @pl.when(valid)
        def _():
            settled(u)

        for s, step in enumerate(little_steps):
            @pl.when(r == beats + length + 1 + s)
            def _(step=step):
                step(0)

        @pl.when((c >= 1) & (c <= beats))
        def _():
            for i in range(BEAT):
                attend_back((c - 1) * BEAT + i)

        @pl.when((c >= 0) & (c + 1 < beats))
        def _():
            for i in range(BEAT):
                for copy in loads((c + 1) * BEAT + i):
                    copy.start()

        for g in range(late):
            u = order.index(len(early) + g)

            @pl.when(r == starts[u] - 1)
            def _(g=g):
                late_begin(g)

        @pl.when(r == beats + length)
        def _():
            input_back()

        return 0

    rounds = max(starts[-1] + stages[-1][0] + 1, beats + length + 1 + len(little_steps))
    lax.fori_loop(0, rounds, one_round, 0)

    for u in range(units):
        for track in tracks_of(u):
            track.finish(u - track.base)
    chain.drain(heads)
    little.drain(0)
    little.given(0)
    spread_keep().wait()
    for k in range(len(others)):
        spread(k, False).wait_send()
        spread(k, True).wait_recv()

    sums = small_out[...].reshape(-1, model_width)
    for h in range(heads):
        part = slice(h * head_width, (h + 1) * head_width)
        qm_out[h] = sums[:head_width, part]
        km_out[h] = sums[head_width : 2 * head_width, part]
    row = 2 * head_width
    rows_out[...] = sums[row : row + 8]
    row += 6
    for target in (bias_out, expand_bias_out):
        for start in range(0, target.shape[0], model_width):
            target[start : start + model_width] = sums[row]
            row += 1

    for low, high, tracks in groups:
        def drain(v, _, tracks=tracks):
            for track in tracks:
                track.drain(v)
            return 0

        lax.fori_loop(0, high - low, drain, 0)
    for u in range(units):
        if order[u] < len(early) or order[u] == units - 1:
            for track in tracks_of(u):
                track.given(u - track.base)


def backward_attention(
    projected, feat_query, feat_key, state_in, attended, denominator, attended_grad, query_map,
    key_map, normed_rows, weight, input_rows, middle_grad_rows, gain, vectors, bounds,
    contract_grad, expand_grad, output_grad, count, lines,
):
    heads, head_width = query_map.shape[:2]
    model_width, total_rows = normed_rows.shape
    micro_count = bounds.shape[0]
    rows = total_rows // micro_count
    length = count // 2
    share = model_width // count
    chunk = state_in.shape
    early = [(0, u, 0) for u in range(contract_grad.shape[2])]
    early += [(1, None, c) for c in range(0, expand_grad.shape[3], model_width)]
    early += [(2, None, 0)]
    units = len(early) + 3
    shape = jax.ShapeDtypeStruct
    whole = pl.BlockSpec(memory_space=pltpu.VMEM)
    anywhere = pl.BlockSpec(memory_space=pl.ANY)
    DMA = pltpu.SemaphoreType.DMA
    half = model_width // 2
    used = 2 * head_width + vectors.shape[0]
    little = -(-used // (8 * count)) * 8
    tracks = track_scratch(1, length, lines, little, False, 1, half)
    for low, high, direct, halved in bands(units, share, lines):
        for kind, band in ((False, direct), (True, halved)):
            if band:
                tracks += track_scratch(high - low, length, lines, band, kind, 2, half)
    slots = 2 * BEAT
    head, feat = ((slots, head_width, total_rows), (slots, 2 * head_width, total_rows))
    return pl.pallas_call(
        partial(backward_kernel, count, lines, micro_count, early),
        out_shape=[
            shape((units, share, model_width), single), shape((total_rows, model_width), bfloat),
            shape(query_map.shape, single), shape(key_map.shape, single),
        ]
        + [shape((8, model_width), single)]
        + [shape((3 * model_width,), single), shape((expand_grad.shape[3],), single)],
        in_specs=[anywhere] * 7
        + [whole] * 8
        + [pl.BlockSpec(memory_space=pltpu.SMEM)]
        + [anywhere] * 3,
        out_specs=[anywhere] + [whole] * 6,
        scratch_shapes=[
            pltpu.VMEM((slots, 3) + head[1:], bfloat),
            pltpu.VMEM(feat, bfloat),
            pltpu.VMEM(feat, bfloat),
            pltpu.VMEM((slots,) + chunk[1:], single),
            pltpu.VMEM(head, single),
            pltpu.VMEM((slots, 1, total_rows), single),
            pltpu.VMEM(head, single),
            DMA((slots, 7)),
            pltpu.VMEM((3, heads, head_width, total_rows), bfloat),
            pltpu.VMEM((micro_count, rows, rows), single),
            pltpu.VMEM((1, total_rows), single),
            pltpu.VMEM((1, total_rows), single),
            pltpu.VMEM((5,) + chunk[1:], single),
            pltpu.VMEM(chunk[1:], single),
        ]
        + [pltpu.VMEM(chunk, single)]
        + [pltpu.VMEM((CHAIN_RING,) + chunk[1:], single)] * 2
        + [pltpu.VMEM(chunk, single)]
        + [pltpu.VMEM(feat[1:], single)] * 2
        + [
            pltpu.VMEM((length, 2, share, model_width), single),
            pltpu.VMEM((length, 2, little, model_width), single),
            pltpu.VMEM((1, little, model_width), single),
            pltpu.VMEM((count, little, model_width), single),
            DMA((2 * count - 1,)),
            DMA((count, 2)),
            DMA((1,)),
            pltpu.SemaphoreType.REGULAR,
        ]
        + [DMA((heads,))] * 4
        + tracks,
        compiler_params=pltpu.CompilerParams(
            collective_id=2, has_side_effects=True, vmem_limit_bytes=BACKWARD_LIMIT
        ),
    )(
        projected, feat_query, feat_key, state_in, attended, denominator, attended_grad, query_map,
        key_map, normed_rows, weight, input_rows, middle_grad_rows,
        gain, vectors, bounds.T, contract_grad, expand_grad,
        output_grad,
    )


def feed_kernel(
    att_ref, x_ref, grad_ref, out_weight_ref, out_bias_ref, gain_ref, shift_ref, contract_bias_ref,
    expand_ref, expand_bias_ref, contract_ref,
    result_ref, contract_grad_ref, expand_grad_ref, output_grad_ref, att_grad_ref, mid_grad_ref,
    vector_ref, unit, inverse, low, turned, total, back,
):
    step, steps = (pl.program_id(0), pl.num_programs(0))
    out_bias, gain, shift, contract_bias = (
        flat(ref[...]) for ref in (out_bias_ref, gain_ref, shift_ref, contract_bias_ref)
    )
    wide = x_ref.shape[1]
    columns = pl.ds(pl.multiple_of(step * wide, wide), wide)

    @pl.when(step == 0)
    def _():
        branch = matmul(att_ref[...], out_weight_ref[...], (0, 0)) + out_bias
        middle = x_ref[...].astype(single) + branch
        normed, unit_rows, factor = norm_forward(middle, gain, shift)
        unit[...] = unit_rows
        inverse[...] = factor
        low[...] = normed.astype(bfloat)
        turned[...] = normed.astype(bfloat).T
        total[...] = middle + contract_bias
        back[...] = jnp.zeros_like(back)
        vector_ref[...] = jnp.zeros_like(vector_ref)

    expanded = matmul(low[...], expand_ref[...], (1, 0)) + flat(expand_bias_ref[columns])
    slope = 0.7978845608028654
    square = expanded * expanded
    bend = jnp.tanh(slope * expanded * (1.0 + 0.044715 * square))
    half = 0.5 * (1.0 + bend)
    hidden = (expanded * half).astype(bfloat)
    derivative = half + expanded * (0.5 * slope) * (1.0 - bend * bend) * (
        1.0 + 3.0 * 0.044715 * square
    )
    hidden_grad = matmul(grad_ref[...], contract_ref[...], (1, 1)) * derivative
    low_grad = hidden_grad.astype(bfloat)
    total[...] += matmul(hidden, contract_ref[...], (1, 0))
    back[...] += matmul(low_grad, expand_ref[...], (1, 1))
    expand_grad_ref[...] = matmul(turned[...], low_grad, (1, 0))
    contract_grad_ref[...] = matmul(hidden, grad_ref[...], (0, 0))
    bias_sum = jnp.sum(low_grad.astype(single), axis=0, keepdims=True)
    row = lax.broadcasted_iota(jnp.int32, vector_ref.shape, 0)
    vector_ref[...] = jnp.where(row == 9 + step, bias_sum, vector_ref[...])

    @pl.when(step == steps - 1)
    def _():
        result_ref[...] = total[...].astype(bfloat)
        wide_grad = grad_ref[...].astype(single)
        mid, gain_sum, shift_sum = norm_backward(back[...], unit[...], inverse[...], gain)
        mid = wide_grad + mid
        branch = mid.astype(bfloat)
        mid_grad_ref[...] = mid.T
        att_grad_ref[...] = matmul(out_weight_ref[...], branch, (1, 1))
        output_grad_ref[...] = matmul(att_ref[...], branch, (1, 0))
        sums = [
            gain_sum[None],
            shift_sum[None],
            jnp.sum(branch.astype(single), axis=0, keepdims=True),
            jnp.sum(wide_grad, axis=0, keepdims=True),
        ]
        height, wide = vector_ref.shape
        vector_ref[...] += jnp.concatenate(
            [jnp.zeros((2, wide), single)] + sums + [jnp.zeros((height - 6, wide), single)], axis=0
        )


def feed_forward(
    att, x, grad, output_weight, output_bias, gain, shift, expand_weight, expand_bias,
    contract_weight, contract_bias,
):
    total_rows, wide = x.shape
    steps = expand_weight.shape[1] // wide
    shape = jax.ShapeDtypeStruct
    whole = pl.BlockSpec(memory_space=pltpu.VMEM)
    square = (wide, wide)
    by_row, by_column = (lambda i: (i, 0), lambda i: (0, i))
    return pl.pallas_call(
        feed_kernel,
        grid=(steps,),
        out_shape=[
            shape((total_rows, wide), bfloat), shape((steps * wide, wide), single),
            shape((wide, steps * wide), single), shape(square, single),
            shape((wide, total_rows), single), shape((wide, total_rows), single),
            shape((16, wide), single),
        ],
        in_specs=[whole] * 8
        + [pl.BlockSpec(square, by_column), whole, pl.BlockSpec(square, by_row)],
        out_specs=[
            whole, pl.BlockSpec(square, by_row), pl.BlockSpec(square, by_column), whole, whole,
            whole, whole,
        ],
        scratch_shapes=[
            pltpu.VMEM((total_rows, wide), single),
            pltpu.VMEM((total_rows, 1), single),
            pltpu.VMEM((total_rows, wide), bfloat),
            pltpu.VMEM((wide, total_rows), bfloat),
            pltpu.VMEM((total_rows, wide), single),
            pltpu.VMEM((total_rows, wide), single),
        ],
        compiler_params=pltpu.CompilerParams(vmem_limit_bytes=VMEM_LIMIT),
    )(
        att, x, grad, output_weight, output_bias, gain, shift, contract_bias, expand_weight,
        expand_bias, contract_weight,
    )


def per_device(
    inputs, gain_one, bias_one, project_weight, project_bias, query_map, key_map, output_weight,
    output_bias, gain_two, bias_two, expand_weight, expand_bias, contract_weight, contract_bias,
    bounds, cotangent,
):
    micro_count, row_count, model_width = inputs.shape
    head_count, head_width = (query_map.shape[0], query_map.shape[1])
    total_rows = micro_count * row_count
    count = lax.axis_size("seq")
    flat_input = inputs.reshape(total_rows, model_width)
    (
        projected, feat_query, feat_key, state_in, attended, attended_low, denominator,
        normed_rows, input_rows,
    ) = forward_attention(
        flat_input, gain_one, bias_one, project_weight,
        project_bias, query_map, key_map, bounds, count,
    )
    attended_low = attended_low.reshape(model_width, total_rows)

    lines = lax.axis_size("batch") // 2
    share = model_width // count
    tiles = (count // 2, 2)
    (
        block_output, contract_grad, expand_grad, output_grad, attended_grad, middle_grad_rows,
        vectors,
    ) = feed_forward(
        attended_low, flat_input, cotangent.reshape(total_rows, model_width), output_weight,
        output_bias, gain_two, bias_two, expand_weight, expand_bias, contract_weight,
        contract_bias,
    )
    contract_grad = contract_grad.reshape(
        tiles + (expand_weight.shape[1] // model_width, share, model_width)
    )
    expand_grad = expand_grad.reshape(tiles + (share, -1))
    output_grad = output_grad.reshape(tiles + (share, model_width))
    (
        totals, input_grad, query_map_grad, key_map_grad, sums, project_bias_grad,
        expand_bias_grad,
    ) = backward_attention(
        projected.reshape(3, head_count, head_width, total_rows), feat_query, feat_key, state_in,
        attended, denominator, attended_grad.reshape(head_count, head_width, total_rows),
        query_map, key_map, normed_rows, project_weight, input_rows, middle_grad_rows, gain_one,
        vectors, bounds, contract_grad, expand_grad, output_grad, count, lines,
    )
    depth = contract_grad.shape[2]
    wide = expand_weight.shape[1] // model_width
    order, _ = unit_order(depth + wide + 1, 3, head_count // 3 // BEAT, count // 2)
    at = [order.index(i) for i in range(len(order))]
    contract_total = jnp.concatenate([totals[i] for i in at[:depth]])
    expand_total = jnp.concatenate([totals[i] for i in at[depth : depth + wide]], axis=1)
    output_total = totals[at[depth + wide]]
    late = [totals[i].reshape(share, 3, -1) for i in at[depth + wide + 1 :]]
    project_total = jnp.stack(late, axis=2).reshape(share, -1)
    return (
        block_output.reshape(inputs.shape), input_grad.reshape(inputs.shape), sums[0], sums[1],
        project_total, project_bias_grad, query_map_grad, key_map_grad, output_total, sums[4],
        sums[2], sums[3], expand_total, expand_bias_grad,
        contract_total, sums[5],
    )


def solution(mesh):
    rows = P("batch", "seq", None)
    placed = (rows,) + (P(),) * 14 + (P("batch", None), rows)
    shard = P("seq", None)
    return jax.shard_map(
        per_device,
        mesh=mesh,
        in_specs=placed,
        out_specs=(
            rows, rows, P(), P(), shard, P(), P(), P(), shard, P(), P(), P(), shard, P(), shard, P(),
        ),
        check_vma=False,
    )
```

```python
from functools import partial

import jax
import jax.numpy as jnp
from jax import lax
from jax.experimental import pallas as pl
from jax.experimental.pallas import tpu as pltpu
from jax.sharding import PartitionSpec as P

epsilon = 1e-05
bfloat = jnp.bfloat16
single = jnp.float32
MESH = pl.DeviceIdType.MESH
VMEM_LIMIT = 56 * 1024 * 1024
BACKWARD_LIMIT = 63 * 1024 * 1024


def matmul(a, b, contract):
    return lax.dot_general(
        a, b, (((contract[0],), (contract[1],)), ((), ())), preferred_element_type=single
    )


def norm_forward(values, gain_vector, shift_vector):
    centered = values - jnp.mean(values, axis=-1, keepdims=True)
    inverse = lax.rsqrt(jnp.mean(centered * centered, axis=-1, keepdims=True) + epsilon)
    unit_rows = centered * inverse
    return (unit_rows * gain_vector + shift_vector, unit_rows, inverse)


def norm_backward(gradient, unit_rows, inverse, gain_vector):
    inner = gradient * gain_vector
    result = inverse * (
        inner
        - jnp.mean(inner, axis=-1, keepdims=True)
        - unit_rows * jnp.mean(inner * unit_rows, axis=-1, keepdims=True)
    )
    return (result, jnp.sum(gradient * unit_rows, axis=0), jnp.sum(gradient, axis=0))


def two_softmaxes(mapped):
    up = jnp.exp(mapped - jnp.max(mapped, axis=0, keepdims=True))
    down = jnp.exp(jnp.min(mapped, axis=0, keepdims=True) - mapped)
    return (
        up / jnp.sum(up, axis=0, keepdims=True),
        down / jnp.sum(down, axis=0, keepdims=True),
    )


def flat(vector):
    return vector.astype(single).reshape(1, -1)


def with_ones(rows):
    return jnp.concatenate([rows, jnp.ones((16, rows.shape[1]), rows.dtype)], axis=0)


def state_rows(state, micro, micro_count, head_width):
    low = state[micro * head_width : (micro + 1) * head_width, :]
    row = micro_count * head_width + micro
    total = state[row : row + 1, :]
    return jnp.concatenate([low, jnp.broadcast_to(total, (16, low.shape[1]))], axis=0)


def score_grads(grad, attended, denom):
    inverse = 1.0 / denom
    numer_grad = grad * inverse
    denom_grad = -jnp.sum(grad * attended, axis=0, keepdims=True) * inverse
    pad = jnp.zeros((15, grad.shape[1]), single)
    return jnp.concatenate([numer_grad, denom_grad, pad], axis=0)


def feature_backward(feat_grad, source, weights):
    head_width = source.shape[0]
    up, down = two_softmaxes(matmul(weights, source, (0, 0)))
    grad_up, grad_down = (feat_grad[:head_width], feat_grad[head_width:])
    mapped = up * (grad_up - jnp.sum(up * grad_up, axis=0, keepdims=True)) - down * (
        grad_down - jnp.sum(down * grad_down, axis=0, keepdims=True)
    )
    low = mapped.astype(bfloat)
    return (matmul(weights, low, (1, 0)), matmul(source, low, (1, 1)))


def document(position, bounds_ref, m):
    return jnp.where(position >= bounds_ref[0, m], 1, 0) + jnp.where(
        position >= bounds_ref[1, m], 1, 0
    )


def token_masks(bounds_ref, first_row, rows, micro_count, mask_ref, use_ref, last_ref):
    low_shape, line_shape = ((rows, rows), (1, rows))
    source = first_row + lax.broadcasted_iota(jnp.int32, low_shape, 0)
    target = first_row + lax.broadcasted_iota(jnp.int32, low_shape, 1)
    line = first_row + lax.broadcasted_iota(jnp.int32, line_shape, 1)
    for m in range(micro_count):
        part = slice(m * rows, (m + 1) * rows)
        same = document(source, bounds_ref, m) == document(target, bounds_ref, m)
        mask_ref[m] = jnp.where((source <= target) & same, 1.0, 0.0)
        own = document(line, bounds_ref, m)
        use_ref[:, part] = jnp.where(own == document(first_row - 1, bounds_ref, m), 1.0, 0.0)
        last_ref[:, part] = jnp.where(
            own == document(first_row + rows - 1, bounds_ref, m), 1.0, 0.0
        )


def chain_masks(bounds_ref, first_row, low, rows, micro_count, head_width, reverse, mask_ref):
    base = first_row - low * rows
    step = 2 * rows
    height, wide = mask_ref.shape[1:]
    for m in range(micro_count):
        def doc(position, m=m):
            return document(position, bounds_ref, m)

        inner = doc(base + rows - 1)
        if reverse:
            lead = 1 - low
            own_edge, pair, ahead = (doc(first_row - 1), doc(base + step - 1), doc(base - 1))
        else:
            lead = low
            own_edge, pair, ahead = (
                doc(first_row + rows - 1), doc(base - 1), doc(base + step - 1),
            )
        keep = jnp.where(pair == inner, 1.0, 0.0)
        values = [
            jnp.where(pair == ahead, 1.0, 0.0),
            jnp.where(own_edge == ahead, 1.0, 0.0),
            jnp.where(lead == 0, keep, 1.0),
            jnp.where(lead == 0, 1.0, 0.0),
            jnp.where(lead == 0, 1.0, keep),
        ]
        for i, value in enumerate(values):
            mask_ref[i, m * head_width : (m + 1) * head_width, :] = jnp.full(
                (head_width, wide), value
            )
            tail = slice(micro_count * head_width, height)
            row = lax.broadcasted_iota(jnp.int32, (height - tail.start, wide), 0)
            before = jnp.zeros(row.shape, single) if m == 0 else mask_ref[i, tail, :]
            mask_ref[i, tail, :] = jnp.where(lax.rem(row, micro_count) == m, value, before)


CHAIN_RING = 4
LATER = 2


class Chain:
    def __init__(self, reverse, count, carry, onward, aside, beside, mask, sems):
        self.carry, self.onward, self.aside, self.beside = carry, onward, aside, beside
        self.mask, self.sems = mask, sems
        place, self.column = (lax.axis_index("seq"), lax.axis_index("batch"))
        high, low = (place // 2, lax.rem(place, 2))
        length = count // 2
        self.lap = length - 1 - high if reverse else high
        self.ahead, self.behind = (place - 2, place + 2) if reverse else (place + 2, place - 2)
        self.partner = place + 1 - 2 * low
        self.first, self.final = (self.lap == 0, self.lap == length - 1)

    def greet(self, barrier):
        def signal(place):
            pl.semaphore_signal(
                barrier, inc=1, device_id=(place, self.column), device_id_type=MESH
            )

        signal(self.partner)

        @pl.when(jnp.logical_not(self.final))
        def _():
            signal(self.ahead)

        @pl.when(jnp.logical_not(self.first))
        def _():
            signal(self.behind)

        return 1 + jnp.where(self.first, 0, 1) + jnp.where(self.final, 0, 1)

    def along(self, i):
        return pltpu.make_async_remote_copy(
            src_ref=self.onward.at[lax.rem(i, CHAIN_RING)], dst_ref=self.carry.at[i], send_sem=self.sems[0].at[i],
            recv_sem=self.sems[1].at[i], device_id=(self.ahead, self.column), device_id_type=MESH,
        )

    def across(self, i):
        return pltpu.make_async_remote_copy(
            src_ref=self.aside.at[lax.rem(i, CHAIN_RING)], dst_ref=self.beside.at[i], send_sem=self.sems[2].at[i],
            recv_sem=self.sems[3].at[i], device_id=(self.partner, self.column),
            device_id_type=MESH,
        )

    def start(self):
        @pl.when(self.first)
        def _():
            self.carry[...] = jnp.zeros_like(self.carry)

    def step(self, i, local):
        @pl.when(jnp.logical_not(self.first))
        def _():
            self.along(i).wait_recv()

        @pl.when(i >= CHAIN_RING)
        def _():
            self.sent(i - CHAIN_RING)

        state, slot = (self.carry[i], lax.rem(i, CHAIN_RING))

        @pl.when(jnp.logical_not(self.final))
        def _():
            self.onward[slot] = self.mask[0] * state + self.mask[1] * local
            self.along(i).start()

        self.aside[slot] = self.mask[2] * state + self.mask[3] * local
        self.across(i).start()

    def sent(self, i):
        self.across(i).wait_send()

        @pl.when(jnp.logical_not(self.final))
        def _():
            self.along(i).wait_send()

    def result(self, i):
        self.across(i).wait_recv()
        return self.mask[4] * self.carry[i] + self.beside[i]

    def drain(self, chunks):
        def one(i, _):
            self.sent(i)
            return 0

        lax.fori_loop(max(chunks - CHAIN_RING, 0), chunks, one, 0)


def local_state(wide, other, micro_count, head_width, target):
    rows = wide.shape[1] // micro_count
    sums = []
    for m in range(micro_count):
        part = slice(m * rows, (m + 1) * rows)
        local = matmul(wide[:, part], other[:, part], (1, 1))
        target[m * head_width : (m + 1) * head_width, :] = local[:head_width]
        sums.append(local[head_width : head_width + 1])
    target[micro_count * head_width :, :] = jnp.concatenate(sums + sums, axis=0)


def forward_kernel(
    count, micro_count, x_ref, gain_ref, shift_ref, weight_hbm, bias_ref, qm_ref, km_ref,
    bounds_ref, proj_out, fq_out, fk_out, state_out, att_out, low_out, den_out, norm_out,
    turned_out, weight_ref, proj_ref, fq_ref, fk_ref, state_ref, att_ref, low_ref, den_ref,
    norm_ref, turned_ref, out_sem, whole_sem, normed, bias_row, mask, use, last, chain_mask, local, carry, onward, aside, beside, *sems,
):
    heads, head_width = qm_ref.shape[:2]
    total_rows = x_ref.shape[0]
    rows = total_rows // micro_count
    model_width = x_ref.shape[1]
    pair = 2 * head_width
    place = lax.axis_index("seq")
    first_row = place * rows
    chain = Chain(False, count, carry, onward, aside, beside, chain_mask, sems)
    weight_copy = pltpu.make_async_copy(weight_hbm, weight_ref, whole_sem.at[0])
    weight_copy.start()
    turned_copies = [
        pltpu.make_async_copy(norm_ref, norm_out, whole_sem.at[1]),
        pltpu.make_async_copy(turned_ref, turned_out, whole_sem.at[2]),
    ]

    def outward(h):
        pairs = [(proj_ref.at[p * heads + h], proj_out.at[p * heads + h]) for p in range(3)]
        for source, target in (
            (fq_ref, fq_out), (fk_ref, fk_out), (state_ref, state_out), (att_ref, att_out),
            (low_ref, low_out), (den_ref, den_out),
        ):
            pairs.append((source.at[h], target.at[h]))
        return [
            pltpu.make_async_copy(source, target, out_sem.at[h, i])
            for i, (source, target) in enumerate(pairs)
        ]

    barrier = pltpu.get_barrier_semaphore()
    greeted = chain.greet(barrier)
    token_masks(bounds_ref, first_row, rows, micro_count, mask, use, last)
    chain_masks(
        bounds_ref, first_row, lax.rem(place, 2), rows, micro_count, head_width, False, chain_mask
    )
    chain.start()
    bias_row[...] = flat(bias_ref[...])
    normed[...] = norm_forward(
        x_ref[...].astype(single), flat(gain_ref[...]), flat(shift_ref[...])
    )[0].astype(bfloat)
    pl.semaphore_wait(barrier, greeted)
    norm_ref[...] = normed[...].T
    turned_ref[...] = x_ref[...].T
    for copy in turned_copies:
        copy.start()
    weight_copy.wait()

    def project(p):
        for part in range(3):
            columns = pl.ds(pl.multiple_of(part * model_width + p * pair, pair), pair)
            value = matmul(normed[...], weight_ref[:, columns], (1, 0))
            value = (value + bias_row[:, columns]).astype(bfloat).T
            proj_ref[part * heads + 2 * p] = value[:head_width]
            proj_ref[part * heads + 2 * p + 1] = value[head_width:]

    def features(h):
        for offset, weights, target in ((0, qm_ref, fq_ref), (heads, km_ref, fk_ref)):
            mapped = matmul(weights[h], proj_ref[offset + h], (0, 0))
            up, down = two_softmaxes(mapped)
            target[h] = jnp.concatenate([up, down], axis=0).astype(bfloat)
        wide = with_ones(proj_ref[2 * heads + h]) * last[...].astype(bfloat)
        local_state(wide, fk_ref.at[h], micro_count, head_width, local.at[h])

    def attend(h):
        state_ref[h] = chain.result(h)
        wide = with_ones(proj_ref[2 * heads + h])
        used = fq_ref[h] * use[...].astype(bfloat)
        for m in range(micro_count):
            part = slice(m * rows, (m + 1) * rows)
            scores = matmul(fk_ref[h, :, part], fq_ref[h, :, part], (0, 0)) * mask[m]
            state = state_rows(state_ref.at[h], m, micro_count, head_width).astype(bfloat)
            numer = matmul(wide[:, part], scores.astype(bfloat), (1, 0)) + matmul(
                state, used[:, part], (1, 0)
            )
            denom = numer[head_width : head_width + 1]
            attended = numer[:head_width] / denom
            att_ref[h, :, part] = attended
            low_ref[h, :, part] = attended.astype(bfloat)
            den_ref[h, :, part] = denom

    def one_round(r, _):
        @pl.when((r < heads) & (lax.rem(r, 2) == 0))
        def _():
            project(r // 2)

        @pl.when(r < heads)
        def _():
            features(r)

        @pl.when((r >= chain.lap) & (r < heads + chain.lap))
        def _():
            chain.step(r - chain.lap, local[r - chain.lap])

        @pl.when(r >= chain.lap + 1)
        def _():
            attend(r - chain.lap - 1)
            for copy in outward(r - chain.lap - 1):
                copy.start()

        @pl.when(r >= chain.lap + 1 + LATER)
        def _():
            for copy in outward(r - chain.lap - 1 - LATER):
                copy.wait()

        return 0

    lax.fori_loop(0, heads + chain.lap + 1, one_round, 0)
    chain.drain(heads)

    def arrived(h, _):
        for copy in outward(h):
            copy.wait()
        return 0

    lax.fori_loop(heads - LATER, heads, arrived, 0)
    for copy in turned_copies:
        copy.wait()


def forward_attention(x, gain, shift, weight, bias, query_map, key_map, bounds, count):
    total_rows, model_width = x.shape
    heads, head_width = query_map.shape[:2]
    micro_count = bounds.shape[0]
    rows = total_rows // micro_count
    height = micro_count * (head_width + 2)
    chunk = (heads, height, 2 * head_width)
    whole = pl.BlockSpec(memory_space=pltpu.VMEM)
    head = (heads, head_width, total_rows)
    feat = (heads, 2 * head_width, total_rows)
    shape = jax.ShapeDtypeStruct
    results = [
        shape((3 * heads,) + head[1:], bfloat), shape(feat, bfloat), shape(feat, bfloat),
        shape(chunk, single), shape(head, single), shape(head, bfloat),
        shape((heads, 1, total_rows), single), shape((model_width, total_rows), bfloat),
        shape((model_width, total_rows), bfloat),
    ]
    anywhere = pl.BlockSpec(memory_space=pl.ANY)
    DMA = pltpu.SemaphoreType.DMA
    return pl.pallas_call(
        partial(forward_kernel, count, micro_count),
        out_shape=results,
        in_specs=[whole] * 3
        + [anywhere]
        + [whole] * 3
        + [pl.BlockSpec(memory_space=pltpu.SMEM)],
        out_specs=[anywhere] * 9,
        scratch_shapes=[pltpu.VMEM(weight.shape, bfloat)]
        + [pltpu.VMEM(result.shape, result.dtype) for result in results]
        + [
            DMA((heads, 9)),
            DMA((3,)),
            pltpu.VMEM((total_rows, model_width), bfloat),
            pltpu.VMEM((1, 3 * model_width), single),
            pltpu.VMEM((micro_count, rows, rows), single),
            pltpu.VMEM((1, total_rows), single),
            pltpu.VMEM((1, total_rows), single),
            pltpu.VMEM((5,) + chunk[1:], single),
        ]
        + [pltpu.VMEM(chunk, single)] * 2
        + [pltpu.VMEM((CHAIN_RING,) + chunk[1:], single)] * 2
        + [pltpu.VMEM(chunk, single)]
        + [DMA((heads,))] * 4,
        compiler_params=pltpu.CompilerParams(
            collective_id=1, has_side_effects=True, vmem_limit_bytes=VMEM_LIMIT
        ),
    )(
        x, gain, shift, weight, bias, query_map, key_map, bounds.T,
    )


def remote(src, dst, send, recv, device):
    return pltpu.make_async_remote_copy(
        src_ref=src, dst_ref=dst, send_sem=send, recv_sem=recv, device_id=device,
        device_id_type=MESH,
    )


PIECES, PIECE_ROWS = (2, (1, 2))


class Spot:
    def __init__(self, count, lines):
        self.place, self.column = (lax.axis_index("seq"), lax.axis_index("batch"))
        self.high, self.low = (self.place // 2, lax.rem(self.place, 2))
        self.across, self.core = (self.column // 2, lax.rem(self.column, 2))
        self.length, self.lines = (count // 2, lines)
        self.at_core = (self.place, self.column + 1 - 2 * self.core)
        self.at_y = (self.place + 1 - 2 * self.low, self.column)
        self.at_right, self.at_left = ((self.place + 2, self.column), (self.place - 2, self.column))
        self.not_first, self.not_last = (self.high > 0, self.high < self.length - 1)

    def line(self, d):
        other = lax.rem(self.across + d, self.lines)
        return other, (self.place, other * 2 + self.core)

    def along(self, d):
        count = 2 * self.length
        other = lax.rem(self.place + d, count)
        return other, (other, self.column)

    def greet(self, barrier):
        devices = [self.at_core]
        devices += [self.line(d)[1] for d in range(1, self.lines)]
        devices += [self.along(d)[1] for d in range(1, 2 * self.length)]
        for device in devices:
            pl.semaphore_signal(barrier, inc=1, device_id=device, device_id_type=MESH)
        return len(devices)


class Track:
    def __init__(
        self, spot, base, halved, rows, offset, stride, ring, out, own, got, y_got, z_got, x_got,
        sems,
    ):
        self.base, self.stride = (base, stride)
        self.spot, self.halved, self.rows, self.offset, self.ring = spot, halved, rows, offset, ring
        self.out, self.own, self.got, self.y_got, self.z_got, self.x_got = (
            out, own, got, y_got, z_got, x_got,
        )
        (
            self.load_sem, self.core_send, self.core_recv, self.y_send, self.y_recv, self.zr_send,
            self.zr_recv, self.zl_send, self.zl_recv, self.x_send, self.x_recv, self.back_send,
            self.back_recv,
        ) = sems
        half = own.shape[-1]
        self.mine = pl.ds(pl.multiple_of(spot.core * half, 128), half)
        self.theirs = pl.ds(pl.multiple_of((1 - spot.core) * half, 128), half)
        self.part = rows // spot.lines if halved else rows
        self.strip = self.window(spot.across) if halved else slice(None)

    def row(self, u):
        return pl.multiple_of(self.offset + u * self.stride, 8) if self.stride else self.offset

    def seat(self, u):
        return self.base if self.stride else self.base + u

    def window(self, line, base=0):
        return pl.ds(pl.multiple_of(base + line * self.part, 8), self.part)

    def source(self, u, ref, col, columns):
        half = self.own.shape[-1]
        cols = pl.ds(pl.multiple_of(col + columns * half, 128), half)
        return ref.at[:, :, pl.ds(self.row(u), self.rows), cols]

    def give(self, u, source):
        return remote(
            source, self.got.at[lax.rem(u, self.ring)], self.core_send.at[u],
            self.core_recv.at[u], self.spot.at_core,
        )

    def begin(self, u, ref, col):
        self.give(u, self.source(u, ref, col, 1 - self.spot.core)).start()
        pltpu.make_async_copy(
            self.source(u, ref, col, self.spot.core), self.own.at[u], self.load_sem.at[u]
        ).start()

    def settle(self, u):
        pltpu.make_async_copy(self.own.at[u], self.own.at[u], self.load_sem.at[u]).wait()
        self.give(u, self.own.at[u]).wait_recv()
        self.own[u] = self.own[u] + self.got[lax.rem(u, self.ring)]

    def given(self, u):
        self.give(u, self.own.at[u]).wait_send()

    def cut(self, u, d):
        other, device = self.spot.line(d)
        return remote(
            self.own.at[u, :, :, self.window(other)], self.x_got.at[u, d - 1],
            self.x_send.at[u, 0, d - 1], self.x_recv.at[u, 0, d - 1], device,
        )

    def first(self, u):
        self.settle(u)
        if self.halved:
            for d in range(1, self.spot.lines):
                self.cut(u, d).start()
        else:
            self.y_copy(u).start()

    def cut_taken(self, u):
        for d in range(1, self.spot.lines):
            self.cut(u, d).wait_recv()
            target = self.own.at[u, :, :, self.strip]
            target[...] = target[...] + self.x_got[u, d - 1]
        self.y_copy(u).start()

    def y_copy(self, u):
        return remote(
            self.own.at[u, :, 1 - self.spot.low, self.strip], self.y_got.at[u],
            self.y_send.at[u], self.y_recv.at[u], self.spot.at_y,
        )

    def y_taken(self, u):
        self.y_copy(u).wait_recv()
        target = self.own.at[u, :, self.spot.low, self.strip]
        target[...] = target[...] + self.y_got[u]
        self.z_step(u, 1)

    def block(self, u, h):
        return self.own.at[u, h, self.spot.low, self.strip]

    def right(self, u, k):
        return remote(
            self.block(u, k), self.z_got.at[u, k], self.zr_send.at[u, k], self.zr_recv.at[u, k],
            self.spot.at_right,
        )

    def left(self, u, k, taker):
        slot = jnp.where(k == taker, self.spot.length, k)
        return remote(
            self.block(u, k), self.z_got.at[u, slot], self.zl_send.at[u, k], self.zl_recv.at[u, k],
            self.spot.at_left,
        )

    def take_right(self, u, k):
        self.right(u, k).wait_recv()
        target = self.block(u, k)
        target[...] = target[...] + self.z_got[u, k]

    def take_left(self, u, k):
        high = self.spot.high
        self.left(u, k, high).wait_recv()
        target = self.block(u, k)
        target[...] = target[...] + self.z_got[u, jnp.where(k == high, self.spot.length, k)]

    def z_step(self, u, t):
        spot = self.spot
        k = spot.high + spot.length - t

        @pl.when(spot.high <= t - 1)
        def _():
            if t > 1:
                @pl.when(spot.not_first)
                def _():
                    self.take_right(u, k)

            self.right(u, k).start()

        j = spot.high - spot.length + t

        @pl.when(spot.high >= spot.length - t)
        def _():
            if t > 1:
                @pl.when(spot.not_last)
                def _():
                    self.take_left(u, j)

            self.left(u, j, spot.high - 1).start()

    def z_end(self, u):
        @pl.when(self.spot.not_first)
        def _():
            self.take_right(u, self.spot.high)

        @pl.when(self.spot.not_last)
        def _():
            self.take_left(u, self.spot.high)

    def x_copy(self, u, d):
        return remote(
            self.block(u, self.spot.high), self.x_got.at[u, d - 1], self.x_send.at[u, 0, d - 1],
            self.x_recv.at[u, 0, d - 1], self.spot.line(d)[1],
        )

    def x_back(self, u, d):
        rows = self.window(self.spot.across, self.row(u))
        return remote(
            self.block(u, self.spot.high), self.out.at[self.seat(u), rows, self.mine],
            self.x_send.at[u, 1, d - 1], self.x_recv.at[u, 1, d - 1], self.spot.line(d)[1],
        )

    def keep(self, u):
        rows = (
            self.window(self.spot.across, self.row(u))
            if self.halved
            else pl.ds(self.row(u), self.rows)
        )
        return pltpu.make_async_copy(
            self.block(u, self.spot.high), self.out.at[self.seat(u), rows, self.mine], self.load_sem.at[u]
        )

    def reduced(self, u):
        self.z_end(u)
        if self.halved:
            self.keep(u).start()
        for d in range(1, self.spot.lines):
            (self.x_back if self.halved else self.x_copy)(u, d).start()

    def back(self, u):
        block = self.out.at[self.seat(u), pl.ds(self.row(u), self.rows), self.mine]
        source = block if self.halved else self.block(u, self.spot.high)
        return remote(source, block, self.back_send.at[u], self.back_recv.at[u], self.spot.at_core)

    def total(self, u):
        spot = self.spot
        for d in range(1, spot.lines):
            self.x_copy(u, d).wait()
        value = self.block(u, spot.high)[...]
        if spot.lines == 2:
            value = value + self.x_got[u, 0]
        else:
            parts = []
            for x in range(spot.lines):
                slot = lax.rem(spot.across - x + spot.lines - 1, spot.lines)
                slot = jnp.minimum(slot, spot.lines - 2)
                parts.append(jnp.where(x == spot.across, value, self.x_got[u, slot]))
            value = sum(parts[1:], parts[0])
        self.block(u, spot.high)[...] = value

    def done(self, u):
        if self.halved:
            for d in range(1, self.spot.lines):
                self.x_back(u, d).wait_recv()
            self.keep(u).wait()
        else:
            self.total(u)
            self.keep(u).start()
        self.back(u).start()

    def finish(self, u):
        self.back(u).wait()
        if not self.halved:
            self.keep(u).wait()

    def steps(self):
        z_steps = [partial(self.z_step, t=t) for t in range(2, self.spot.length)]
        cut = [self.cut_taken] if self.halved else []
        return [self.first] + cut + [self.y_taken] + z_steps + [self.reduced, self.done]

    def drain(self, u):
        self.y_copy(u).wait_send()
        for d in range(1, self.spot.lines):
            if self.halved:
                self.cut(u, d).wait_send()
                self.x_back(u, d).wait_send()

        def right_one(k, _):
            self.right(u, k).wait_send()
            return 0

        def left_one(k, _):
            self.left(u, k, self.spot.high - 1).wait_send()
            return 0

        lax.fori_loop(self.spot.high + 1, self.spot.length, right_one, 0)
        lax.fori_loop(0, self.spot.high, left_one, 0)


def bands(units, share, lines):
    third, rows = (share // 3, share // PIECES)
    fits = [third % 8, 2 * third % (8 * lines), share % 3, share % PIECES]
    direct = rows * PIECE_ROWS[0] // sum(PIECE_ROWS)
    fits += [direct % 8, (rows - direct) % (8 * lines)]
    if any(fits):
        return [(0, units, share, 0, 0)]
    return [
        (0, units - 1, third, 2 * third, 0),
        (units - 1, units - 1 + PIECES, direct, rows - direct, rows),
    ]


def track_scratch(units, length, lines, rows, halved, ring, half):
    part = rows // lines if halved else rows
    DMA = pltpu.SemaphoreType.DMA
    others = lines - 1
    buffers = [
        pltpu.VMEM((units, length, 2, rows, half), single),
        pltpu.VMEM((ring, length, 2, rows, half), single),
        pltpu.VMEM((units, length, part, half), single),
        pltpu.VMEM((units, length + 1, part, half), single),
        pltpu.VMEM((units, others) + ((length, 2) if halved else ()) + (part, half), single),
    ]
    line = DMA((units, length))
    ends = DMA((units, 2, others))
    one = DMA((units,))
    return buffers + [one] * 5 + [line] * 4 + [ends] * 2 + [one] * 2


BEAT = 2


def unit_order(early, late, gap, length):
    order, starts, left = ([], [], list(range(early)))
    ready = {length + 2 + gap * g: early + g for g in range(late)}
    t = 0
    while len(order) < early + late:
        if t in ready or left:
            order.append(ready[t] if t in ready else left.pop(0))
            starts.append(t)
        t += 1
    return order, starts


def backward_kernel(
    count, lines, micro_count, early, proj_hbm, fq_hbm, fk_hbm, state_hbm, att_hbm, den_hbm,
    grad_hbm, qm_ref, km_ref, norm_hbm, weight_hbm, x_hbm, mid_hbm, gain_ref, vector_ref,
    bounds_ref, contract_ref, expand_ref, output_ref, out, in_grad_ref, qm_out, km_out, rows_out, bias_out, expand_bias_out,
    norm_ref, weight_ref, x_ref, mid_ref, whole_sem, proj, fq_buf, fk_buf, state_buf, att_buf, den_buf, grad_buf, load_sem, pg_ref,
    mask, use, last, chain_mask, local, carry, onward, aside, beside, fqg, fkg, product, small,
    small_sum, small_out, gather_send, gather_recv, gather_keep, credit, *rest,
):
    heads, head_width = qm_ref.shape[:2]
    total_rows = pg_ref.shape[-1]
    rows = total_rows // micro_count
    model_width = heads * head_width
    sources = (contract_ref, expand_ref, output_ref)
    share, wide = out.shape[1:]
    group = wide // (3 * head_width)
    late = heads // group
    units = len(early) + late
    spot = Spot(count, lines)
    length = spot.length
    order, starts = unit_order(len(early), late, group // BEAT, length)
    plan = bands(units, share, lines)
    order = order + order[-1:] * (plan[-1][1] - units)
    starts = starts + [starts[-1] + 1 + i for i in range(plan[-1][1] - units)]
    units = len(order)
    chain_sems, rest = (rest[:4], rest[4:])
    chain = Chain(True, count, carry, onward, aside, beside, chain_mask, chain_sems)
    ring, half = (2, wide // 2)
    little = Track(spot, 0, False, small.shape[2], 0, 0, 1, small_sum, *rest[:5], rest[5:18])
    rest = rest[18:]
    groups = []
    for low, high, direct, halved, stride in plan:
        group_tracks = []
        for kind, band, offset in ((False, direct, 0), (True, halved, direct)):
            if band:
                group_tracks.append(
                    Track(spot, low, kind, band, offset, stride, ring, out, *rest[:5], rest[5:18])
                )
                rest = rest[18:]
        groups.append((low, high, group_tracks))
    slots = proj.shape[0]

    def loads(h):
        slot = lax.rem(h, slots)
        pairs = [(proj_hbm.at[:, h], proj.at[slot])]
        for source, target in (
            (fq_hbm, fq_buf), (fk_hbm, fk_buf), (state_hbm, state_buf), (att_hbm, att_buf),
            (den_hbm, den_buf), (grad_hbm, grad_buf),
        ):
            pairs.append((source.at[h], target.at[slot]))
        return [
            pltpu.make_async_copy(source, target, load_sem.at[slot, i])
            for i, (source, target) in enumerate(pairs)
        ]

    for h in range(BEAT):
        for copy in loads(h):
            copy.start()
    whole_copies = [
        pltpu.make_async_copy(source, target, whole_sem.at[i])
        for i, (source, target) in enumerate(
            ((norm_hbm, norm_ref), (weight_hbm, weight_ref), (x_hbm, x_ref), (mid_hbm, mid_ref))
        )
    ]
    for copy in whole_copies:
        copy.start()
    barrier = pltpu.get_barrier_semaphore()
    greeted = spot.greet(barrier)
    pl.semaphore_wait(barrier, greeted)

    def tracks_of(u):
        return [t for low, high, tracks in groups for t in tracks if low <= u < high]

    def begin(u):
        if u >= ring:
            pl.semaphore_wait(credit, 1)
        if order[u] < len(early):
            array, lead, col = early[order[u]]
            ref = sources[array]
            ref = ref if lead is None else ref.at[:, :, lead]
        else:
            ref, col = (product, 0)
        for track in tracks_of(u):
            track.begin(u - track.base, ref, col)

    def settled(u):
        @pl.when(u + ring < units)
        def _():
            pl.semaphore_signal(credit, inc=1, device_id=spot.at_core, device_id_type=MESH)

    def state_grad(h):
        for copy in loads(h):
            copy.wait()
        slot = lax.rem(h, slots)
        wide_grad = score_grads(grad_buf[slot], att_buf[slot], den_buf[slot]) * use[...]
        local_state(wide_grad.astype(bfloat), fq_buf.at[slot], micro_count, head_width, local)

    def attend_back(h):
        slot = lax.rem(h, slots)
        beside[h] = chain.result(h)
        grads = score_grads(grad_buf[slot], att_buf[slot], den_buf[slot])
        low_grads = grads.astype(bfloat)
        used_grads = (grads * use[...]).astype(bfloat)
        last_low = last[...].astype(bfloat)
        wide_value = with_ones(proj[slot, 2])
        wide_last = wide_value * last_low
        for m in range(micro_count):
            part = slice(m * rows, (m + 1) * rows)
            fq, fk = (fq_buf[slot, :, part], fk_buf[slot, :, part])
            scores = (matmul(fk, fq, (0, 0)) * mask[m]).astype(bfloat)
            grad_scores = (
                matmul(wide_value[:, part], low_grads[:, part], (0, 0)) * mask[m]
            ).astype(bfloat)
            state = state_rows(state_buf.at[slot], m, micro_count, head_width).astype(bfloat)
            out_grad = state_rows(beside.at[h], m, micro_count, head_width)
            row = lax.broadcasted_iota(jnp.int32, out_grad.shape, 0)
            out_grad = jnp.where(row <= head_width, out_grad, 0.0).astype(bfloat)
            fqg[:, part] = matmul(fk, grad_scores, (1, 0)) + matmul(
                state, used_grads[:, part], (0, 0)
            )
            fkg[:, part] = matmul(fq, grad_scores, (1, 1)) + matmul(
                out_grad, wide_last[:, part], (0, 0)
            )
            value_grad = matmul(low_grads[:head_width, part], scores, (1, 1)) + matmul(
                out_grad[:head_width], fk * last_low[:, part], (1, 0)
            )
            pg_ref[2, h, :, part] = value_grad.astype(bfloat)
        q_grad, qmg = feature_backward(fqg[...], proj[slot, 0], qm_ref[h])
        pg_ref[0, h] = q_grad.astype(bfloat)
        qm_out[h] = qmg
        k_grad, kmg = feature_backward(fkg[...], proj[slot, 1], km_ref[h])
        pg_ref[1, h] = k_grad.astype(bfloat)
        km_out[h] = kmg

    def late_begin(g):
        if g > 0:
            u = order.index(len(early) + g - 1)
            for track in tracks_of(u):
                track.given(u - track.base)
        columns = group * head_width
        for p in range(3):
            low = pg_ref[p, g * group : (g + 1) * group].reshape(columns, -1)
            value = matmul(norm_ref[...], low, (1, 1))
            product[:, :, :, p * columns : (p + 1) * columns] = value.reshape(
                product.shape[:3] + (columns,)
            )
        begin(order.index(len(early) + g))

    def input_back():
        gain_sum, bias_sum = (0.0, 0.0)
        gain = jnp.broadcast_to(flat(gain_ref[...]), (128, model_width)).T[:, :1]
        step = 2 * rows
        for start in range(0, total_rows, step):
            part = slice(start, start + step)
            grad = sum(
                matmul(
                    weight_ref[:, p * model_width : (p + 1) * model_width],
                    pg_ref[p, :, :, part].reshape(model_width, step), (1, 0),
                )
                for p in range(3)
            )
            value = x_ref[:, part].astype(single)
            value = value - jnp.mean(value, axis=0, keepdims=True)
            inverse = lax.rsqrt(jnp.mean(value * value, axis=0, keepdims=True) + epsilon)
            value = value * inverse
            inner = grad * gain
            result = mid_ref[:, part] + inverse * (
                inner
                - jnp.mean(inner, axis=0, keepdims=True)
                - value * jnp.mean(inner * value, axis=0, keepdims=True)
            )
            in_grad_ref[part, :] = result.T.astype(bfloat)
            gain_sum += jnp.sum((grad * value).T, axis=0, keepdims=True)
            bias_sum += jnp.sum(grad.T, axis=0, keepdims=True)
        ones = jnp.ones((16, total_rows), bfloat)
        sums = [
            matmul(ones, pg_ref[p].reshape(model_width, total_rows), (1, 1))[:1] for p in range(3)
        ]
        blank = jnp.zeros((4, model_width), single)
        vectors = vector_ref[...] + jnp.concatenate(
            [gain_sum, bias_sum, blank] + sums + [blank, blank[:3]], axis=0
        )
        maps = [
            jnp.concatenate([ref[h] for h in range(heads)], axis=1) for ref in (qm_out, km_out)
        ]
        size = small.shape[0] * small.shape[1] * small.shape[2]
        used = 2 * head_width + vectors.shape[0]
        pad = [jnp.zeros((size - used, model_width), single)] if size > used else []
        small[...] = jnp.concatenate(maps + [vectors] + pad, axis=0).reshape(small.shape)
        little.begin(0, small, 0)

    def spread(d, incoming):
        there, device = spot.along(d)
        place = there if incoming else spot.place
        return remote(
            little.block(0, spot.high), small_out.at[place, :, little.mine],
            gather_send.at[d - 1], gather_recv.at[place], device,
        )

    def spread_core():
        block = small_out.at[:, :, little.mine]
        return remote(block, block, gather_keep.at[1], gather_keep.at[2], spot.at_core)

    def spread_keep():
        return pltpu.make_async_copy(
            little.block(0, spot.high), small_out.at[spot.place, :, little.mine],
            gather_keep.at[0],
        )

    def little_done(u):
        little.total(u)
        spread_keep().start()
        for d in range(1, count):
            spread(d, False).start()

    def little_gather(u):
        spread_keep().wait()
        for d in range(1, count):
            spread(d, True).wait_recv()
        spread_core().start()

    little_steps = little.steps()[:-1] + [little_done, little_gather]
    lent = [order.index(len(early) + g) for g in range(late - 1)]

    def settle_all(track, v):
        track.finish(v)
        track.drain(v)
        u = v + track.base
        waited = False
        for k in lent:
            waited = waited | (u == k)

        @pl.when(jnp.logical_not(waited))
        def _():
            track.given(v)

    stages = [
        (s, f, low, high)
        for low, high, tracks in groups
        for track in tracks
        for s, f in enumerate(track.steps() + [partial(settle_all, track)])
    ]
    stages.sort(key=lambda s: (s[0], s[2]))
    ahead = 1
    for u in range(ahead):
        begin(u)
    first_row = spot.place * rows
    token_masks(bounds_ref, first_row, rows, micro_count, mask, use, last)
    chain_masks(
        bounds_ref, first_row, spot.low, rows, micro_count, head_width, True, chain_mask
    )
    chain.start()

    def unit_at(t):
        if starts == list(range(units)):
            return t, (t >= 0) & (t < units)
        u, valid = (0, False)
        for start in starts:
            u = u + jnp.where(t > start, 1, 0)
            valid = valid | (t == start)
        return u, valid

    beats = heads // BEAT

    for copy in whole_copies:
        copy.wait()

    def one_round(r, _):
        c = r - chain.lap

        @pl.when((c >= 0) & (c < beats))
        def _():
            for i in range(BEAT):
                h = c * BEAT + i
                state_grad(h)
                chain.step(h, local[...])

        for u in range(ahead, units):
            if order[u] < len(early):
                @pl.when(r == starts[u] - ahead)
                def _(u=u):
                    begin(u)

        for lag, step, low, high in stages:
            u, valid = unit_at(r - lag)

            @pl.when(valid & (u >= low) & (u < high))
            def _(u=u, step=step, low=low):
                step(u - low)

        u, valid = unit_at(r)

        @pl.when(valid)
        def _():
            settled(u)

        for s, step in enumerate(little_steps):
            @pl.when(r == beats + length + 1 + s)
            def _(step=step):
                step(0)

        @pl.when((c >= 1) & (c <= beats))
        def _():
            for i in range(BEAT):
                attend_back((c - 1) * BEAT + i)

        @pl.when((c >= 0) & (c + 1 < beats))
        def _():
            for i in range(BEAT):
                for copy in loads((c + 1) * BEAT + i):
                    copy.start()

        for g in range(late):
            u = order.index(len(early) + g)

            @pl.when(r == starts[u] - 1)
            def _(g=g):
                late_begin(g)

        @pl.when(r == beats + length)
        def _():
            input_back()

        return 0

    rounds = max(starts[-1] + stages[-1][0] + 1, beats + length + 1 + len(little_steps))
    lax.fori_loop(0, rounds, one_round, 0)

    chain.drain(heads)
    little.drain(0)
    little.given(0)
    for d in range(1, count):
        spread(d, False).wait_send()
    spread_core().wait()

    sums = small_out[...].reshape(-1, model_width)
    for h in range(heads):
        part = slice(h * head_width, (h + 1) * head_width)
        qm_out[h] = sums[:head_width, part]
        km_out[h] = sums[head_width : 2 * head_width, part]
    row = 2 * head_width
    rows_out[...] = sums[row : row + 8]
    row += 6
    for target in (bias_out, expand_bias_out):
        for start in range(0, target.shape[0], model_width):
            target[start : start + model_width] = sums[row]
            row += 1


def backward_attention(
    projected, feat_query, feat_key, state_in, attended, denominator, attended_grad, query_map,
    key_map, normed_rows, weight, input_rows, middle_grad_rows, gain, vectors, bounds,
    contract_grad, expand_grad, output_grad, count, lines,
):
    heads, head_width = query_map.shape[:2]
    model_width, total_rows = normed_rows.shape
    micro_count = bounds.shape[0]
    rows = total_rows // micro_count
    length = count // 2
    share = model_width // count
    chunk = state_in.shape
    early = [(0, u, 0) for u in range(contract_grad.shape[2])]
    early += [(1, None, c) for c in range(0, expand_grad.shape[3], model_width)]
    early += [(2, None, 0)]
    units = len(early) + 3
    shape = jax.ShapeDtypeStruct
    whole = pl.BlockSpec(memory_space=pltpu.VMEM)
    anywhere = pl.BlockSpec(memory_space=pl.ANY)
    DMA = pltpu.SemaphoreType.DMA
    half = model_width // 2
    used = 2 * head_width + vectors.shape[0]
    little = -(-used // (8 * count)) * 8
    tracks = track_scratch(1, length, lines, little, False, 1, half)
    for low, high, direct, halved, _ in bands(units, share, lines):
        for kind, band in ((False, direct), (True, halved)):
            if band:
                tracks += track_scratch(high - low, length, lines, band, kind, 2, half)
    slots = 2 * BEAT
    head, feat = ((slots, head_width, total_rows), (slots, 2 * head_width, total_rows))
    return pl.pallas_call(
        partial(backward_kernel, count, lines, micro_count, early),
        out_shape=[
            shape((units, share, model_width), single), shape((total_rows, model_width), bfloat),
            shape(query_map.shape, single), shape(key_map.shape, single),
        ]
        + [shape((8, model_width), single)]
        + [shape((3 * model_width,), single), shape((expand_grad.shape[3],), single)],
        in_specs=[anywhere] * 7
        + [whole] * 2
        + [anywhere] * 4
        + [whole] * 2
        + [pl.BlockSpec(memory_space=pltpu.SMEM)]
        + [anywhere] * 3,
        out_specs=[anywhere] + [whole] * 6,
        scratch_shapes=[
            pltpu.VMEM(normed_rows.shape, bfloat),
            pltpu.VMEM(weight.shape, bfloat),
            pltpu.VMEM(input_rows.shape, bfloat),
            pltpu.VMEM(middle_grad_rows.shape, single),
            DMA((4,)),
            pltpu.VMEM((slots, 3) + head[1:], bfloat),
            pltpu.VMEM(feat, bfloat),
            pltpu.VMEM(feat, bfloat),
            pltpu.VMEM((slots,) + chunk[1:], single),
            pltpu.VMEM(head, single),
            pltpu.VMEM((slots, 1, total_rows), single),
            pltpu.VMEM(head, single),
            DMA((slots, 7)),
            pltpu.VMEM((3, heads, head_width, total_rows), bfloat),
            pltpu.VMEM((micro_count, rows, rows), single),
            pltpu.VMEM((1, total_rows), single),
            pltpu.VMEM((1, total_rows), single),
            pltpu.VMEM((5,) + chunk[1:], single),
            pltpu.VMEM(chunk[1:], single),
        ]
        + [pltpu.VMEM(chunk, single)]
        + [pltpu.VMEM((CHAIN_RING,) + chunk[1:], single)] * 2
        + [pltpu.VMEM(chunk, single)]
        + [pltpu.VMEM(feat[1:], single)] * 2
        + [
            pltpu.VMEM((length, 2, share, model_width), single),
            pltpu.VMEM((length, 2, little, model_width), single),
            pltpu.VMEM((1, little, model_width), single),
            pltpu.VMEM((count, little, model_width), single),
            DMA((count - 1,)),
            DMA((count,)),
            DMA((3,)),
            pltpu.SemaphoreType.REGULAR,
        ]
        + [DMA((heads,))] * 4
        + tracks,
        compiler_params=pltpu.CompilerParams(
            collective_id=2, has_side_effects=True, vmem_limit_bytes=BACKWARD_LIMIT
        ),
    )(
        projected, feat_query, feat_key, state_in, attended, denominator, attended_grad, query_map,
        key_map, normed_rows, weight, input_rows, middle_grad_rows,
        gain, vectors, bounds.T, contract_grad, expand_grad,
        output_grad,
    )


def feed_kernel(
    att_ref, x_ref, grad_ref, out_weight_ref, out_bias_ref, gain_ref, shift_ref, contract_bias_ref,
    expand_ref, expand_bias_ref, contract_ref,
    result_ref, contract_grad_ref, expand_grad_ref, output_grad_ref, att_grad_ref, mid_grad_ref,
    vector_ref, unit, inverse, low, turned, total, back,
):
    step, steps = (pl.program_id(0), pl.num_programs(0))
    out_bias, gain, shift, contract_bias = (
        flat(ref[...]) for ref in (out_bias_ref, gain_ref, shift_ref, contract_bias_ref)
    )
    wide = x_ref.shape[1]
    columns = pl.ds(pl.multiple_of(step * wide, wide), wide)

    @pl.when(step == 0)
    def _():
        branch = matmul(att_ref[...], out_weight_ref[...], (0, 0)) + out_bias
        middle = x_ref[...].astype(single) + branch
        normed, unit_rows, factor = norm_forward(middle, gain, shift)
        unit[...] = unit_rows
        inverse[...] = factor
        low[...] = normed.astype(bfloat)
        turned[...] = normed.astype(bfloat).T
        total[...] = middle + contract_bias
        back[...] = jnp.zeros_like(back)
        vector_ref[...] = jnp.zeros_like(vector_ref)

    expanded = matmul(low[...], expand_ref[...], (1, 0)) + flat(expand_bias_ref[columns])
    slope = 0.7978845608028654
    square = expanded * expanded
    bend = jnp.tanh(slope * expanded * (1.0 + 0.044715 * square))
    half = 0.5 * (1.0 + bend)
    hidden = (expanded * half).astype(bfloat)
    derivative = half + expanded * (0.5 * slope) * (1.0 - bend * bend) * (
        1.0 + 3.0 * 0.044715 * square
    )
    hidden_grad = matmul(grad_ref[...], contract_ref[...], (1, 1)) * derivative
    low_grad = hidden_grad.astype(bfloat)
    total[...] += matmul(hidden, contract_ref[...], (1, 0))
    back[...] += matmul(low_grad, expand_ref[...], (1, 1))
    expand_grad_ref[...] = matmul(turned[...], low_grad, (1, 0))
    contract_grad_ref[...] = matmul(hidden, grad_ref[...], (0, 0))
    bias_sum = jnp.sum(low_grad.astype(single), axis=0, keepdims=True)
    row = lax.broadcasted_iota(jnp.int32, vector_ref.shape, 0)
    vector_ref[...] = jnp.where(row == 9 + step, bias_sum, vector_ref[...])

    @pl.when(step == steps - 1)
    def _():
        result_ref[...] = total[...].astype(bfloat)
        wide_grad = grad_ref[...].astype(single)
        mid, gain_sum, shift_sum = norm_backward(back[...], unit[...], inverse[...], gain)
        mid = wide_grad + mid
        branch = mid.astype(bfloat)
        mid_grad_ref[...] = mid.T
        att_grad_ref[...] = matmul(out_weight_ref[...], branch, (1, 1))
        output_grad_ref[...] = matmul(att_ref[...], branch, (1, 0))
        sums = [
            gain_sum[None],
            shift_sum[None],
            jnp.sum(branch.astype(single), axis=0, keepdims=True),
            jnp.sum(wide_grad, axis=0, keepdims=True),
        ]
        height, wide = vector_ref.shape
        vector_ref[...] += jnp.concatenate(
            [jnp.zeros((2, wide), single)] + sums + [jnp.zeros((height - 6, wide), single)], axis=0
        )


def feed_forward(
    att, x, grad, output_weight, output_bias, gain, shift, expand_weight, expand_bias,
    contract_weight, contract_bias,
):
    total_rows, wide = x.shape
    steps = expand_weight.shape[1] // wide
    shape = jax.ShapeDtypeStruct
    whole = pl.BlockSpec(memory_space=pltpu.VMEM)
    square = (wide, wide)
    by_row, by_column = (lambda i: (i, 0), lambda i: (0, i))
    return pl.pallas_call(
        feed_kernel,
        grid=(steps,),
        out_shape=[
            shape((total_rows, wide), bfloat), shape((steps * wide, wide), single),
            shape((wide, steps * wide), single), shape(square, single),
            shape((wide, total_rows), single), shape((wide, total_rows), single),
            shape((16, wide), single),
        ],
        in_specs=[whole] * 8
        + [pl.BlockSpec(square, by_column), whole, pl.BlockSpec(square, by_row)],
        out_specs=[
            whole, pl.BlockSpec(square, by_row), pl.BlockSpec(square, by_column), whole, whole,
            whole, whole,
        ],
        scratch_shapes=[
            pltpu.VMEM((total_rows, wide), single),
            pltpu.VMEM((total_rows, 1), single),
            pltpu.VMEM((total_rows, wide), bfloat),
            pltpu.VMEM((wide, total_rows), bfloat),
            pltpu.VMEM((total_rows, wide), single),
            pltpu.VMEM((total_rows, wide), single),
        ],
        compiler_params=pltpu.CompilerParams(vmem_limit_bytes=VMEM_LIMIT),
    )(
        att, x, grad, output_weight, output_bias, gain, shift, contract_bias, expand_weight,
        expand_bias, contract_weight,
    )


def per_device(
    inputs, gain_one, bias_one, project_weight, project_bias, query_map, key_map, output_weight,
    output_bias, gain_two, bias_two, expand_weight, expand_bias, contract_weight, contract_bias,
    bounds, cotangent,
):
    micro_count, row_count, model_width = inputs.shape
    head_count, head_width = (query_map.shape[0], query_map.shape[1])
    total_rows = micro_count * row_count
    count = lax.axis_size("seq")
    flat_input = inputs.reshape(total_rows, model_width)
    (
        projected, feat_query, feat_key, state_in, attended, attended_low, denominator,
        normed_rows, input_rows,
    ) = forward_attention(
        flat_input, gain_one, bias_one, project_weight,
        project_bias, query_map, key_map, bounds, count,
    )
    attended_low = attended_low.reshape(model_width, total_rows)

    lines = lax.axis_size("batch") // 2
    share = model_width // count
    tiles = (count // 2, 2)
    (
        block_output, contract_grad, expand_grad, output_grad, attended_grad, middle_grad_rows,
        vectors,
    ) = feed_forward(
        attended_low, flat_input, cotangent.reshape(total_rows, model_width), output_weight,
        output_bias, gain_two, bias_two, expand_weight, expand_bias, contract_weight,
        contract_bias,
    )
    contract_grad = contract_grad.reshape(
        tiles + (expand_weight.shape[1] // model_width, share, model_width)
    )
    expand_grad = expand_grad.reshape(tiles + (share, -1))
    output_grad = output_grad.reshape(tiles + (share, model_width))
    (
        totals, input_grad, query_map_grad, key_map_grad, sums, project_bias_grad,
        expand_bias_grad,
    ) = backward_attention(
        projected.reshape(3, head_count, head_width, total_rows), feat_query, feat_key, state_in,
        attended, denominator, attended_grad.reshape(head_count, head_width, total_rows),
        query_map, key_map, normed_rows, project_weight, input_rows, middle_grad_rows, gain_one,
        vectors, bounds, contract_grad, expand_grad, output_grad, count, lines,
    )
    depth = contract_grad.shape[2]
    wide = expand_weight.shape[1] // model_width
    order, _ = unit_order(depth + wide + 1, 3, head_count // 3 // BEAT, count // 2)
    at = [order.index(i) for i in range(len(order))]
    contract_total = jnp.concatenate([totals[i] for i in at[:depth]])
    expand_total = jnp.concatenate([totals[i] for i in at[depth : depth + wide]], axis=1)
    output_total = totals[at[depth + wide]]
    late = [totals[i].reshape(share, 3, -1) for i in at[depth + wide + 1 :]]
    project_total = jnp.stack(late, axis=2).reshape(share, -1)
    return (
        block_output.reshape(inputs.shape), input_grad.reshape(inputs.shape), sums[0], sums[1],
        project_total, project_bias_grad, query_map_grad, key_map_grad, output_total, sums[4],
        sums[2], sums[3], expand_total, expand_bias_grad,
        contract_total, sums[5],
    )


def solution(mesh):
    rows = P("batch", "seq", None)
    placed = (rows,) + (P(),) * 14 + (P("batch", None), rows)
    shard = P("seq", None)
    return jax.shard_map(
        per_device,
        mesh=mesh,
        in_specs=placed,
        out_specs=(
            rows, rows, P(), P(), shard, P(), P(), P(), shard, P(), P(), P(), shard, P(), shard, P(),
        ),
        check_vma=False,
    )
```

```python
from functools import partial

import jax
import jax.numpy as jnp
from jax import lax
from jax.experimental import pallas as pl
from jax.experimental.pallas import tpu as pltpu
from jax.sharding import PartitionSpec as P

epsilon = 1e-05
bfloat = jnp.bfloat16
single = jnp.float32
MESH = pl.DeviceIdType.MESH
VMEM_LIMIT = 56 * 1024 * 1024
BACKWARD_LIMIT = 63 * 1024 * 1024


def matmul(a, b, contract):
    return lax.dot_general(
        a, b, (((contract[0],), (contract[1],)), ((), ())), preferred_element_type=single
    )


def norm_forward(values, gain_vector, shift_vector):
    centered = values - jnp.mean(values, axis=-1, keepdims=True)
    inverse = lax.rsqrt(jnp.mean(centered * centered, axis=-1, keepdims=True) + epsilon)
    unit_rows = centered * inverse
    return (unit_rows * gain_vector + shift_vector, unit_rows, inverse)


def norm_backward(gradient, unit_rows, inverse, gain_vector):
    inner = gradient * gain_vector
    result = inverse * (
        inner
        - jnp.mean(inner, axis=-1, keepdims=True)
        - unit_rows * jnp.mean(inner * unit_rows, axis=-1, keepdims=True)
    )
    return (result, jnp.sum(gradient * unit_rows, axis=0), jnp.sum(gradient, axis=0))


def two_softmaxes(mapped):
    up = jnp.exp(mapped - jnp.max(mapped, axis=0, keepdims=True))
    down = jnp.exp(jnp.min(mapped, axis=0, keepdims=True) - mapped)
    return (
        up / jnp.sum(up, axis=0, keepdims=True),
        down / jnp.sum(down, axis=0, keepdims=True),
    )


def flat(vector):
    return vector.astype(single).reshape(1, -1)


def with_ones(rows):
    return jnp.concatenate([rows, jnp.ones((16, rows.shape[1]), rows.dtype)], axis=0)


def state_rows(state, micro, micro_count, head_width):
    low = state[micro * head_width : (micro + 1) * head_width, :]
    row = micro_count * head_width + micro
    total = state[row : row + 1, :]
    return jnp.concatenate([low, jnp.broadcast_to(total, (16, low.shape[1]))], axis=0)


def score_grads(grad, attended, denom):
    inverse = 1.0 / denom
    numer_grad = grad * inverse
    denom_grad = -jnp.sum(grad * attended, axis=0, keepdims=True) * inverse
    pad = jnp.zeros((15, grad.shape[1]), single)
    return jnp.concatenate([numer_grad, denom_grad, pad], axis=0)


def feature_backward(feat_grad, source, weights):
    head_width = source.shape[0]
    up, down = two_softmaxes(matmul(weights, source, (0, 0)))
    grad_up, grad_down = (feat_grad[:head_width], feat_grad[head_width:])
    mapped = up * (grad_up - jnp.sum(up * grad_up, axis=0, keepdims=True)) - down * (
        grad_down - jnp.sum(down * grad_down, axis=0, keepdims=True)
    )
    low = mapped.astype(bfloat)
    return (matmul(weights, low, (1, 0)), matmul(source, low, (1, 1)))


def document(position, bounds_ref, m):
    return jnp.where(position >= bounds_ref[0, m], 1, 0) + jnp.where(
        position >= bounds_ref[1, m], 1, 0
    )


def token_masks(bounds_ref, first_row, rows, micro_count, mask_ref, use_ref, last_ref):
    low_shape, line_shape = ((rows, rows), (1, rows))
    source = first_row + lax.broadcasted_iota(jnp.int32, low_shape, 0)
    target = first_row + lax.broadcasted_iota(jnp.int32, low_shape, 1)
    line = first_row + lax.broadcasted_iota(jnp.int32, line_shape, 1)
    for m in range(micro_count):
        part = slice(m * rows, (m + 1) * rows)
        same = document(source, bounds_ref, m) == document(target, bounds_ref, m)
        mask_ref[m] = jnp.where((source <= target) & same, 1.0, 0.0)
        own = document(line, bounds_ref, m)
        use_ref[:, part] = jnp.where(own == document(first_row - 1, bounds_ref, m), 1.0, 0.0)
        last_ref[:, part] = jnp.where(
            own == document(first_row + rows - 1, bounds_ref, m), 1.0, 0.0
        )


def chain_masks(bounds_ref, first_row, low, rows, micro_count, head_width, reverse, mask_ref):
    base = first_row - low * rows
    step = 2 * rows
    height, wide = mask_ref.shape[1:]
    for m in range(micro_count):
        def doc(position, m=m):
            return document(position, bounds_ref, m)

        inner = doc(base + rows - 1)
        if reverse:
            lead = 1 - low
            own_edge, pair, ahead = (doc(first_row - 1), doc(base + step - 1), doc(base - 1))
        else:
            lead = low
            own_edge, pair, ahead = (
                doc(first_row + rows - 1), doc(base - 1), doc(base + step - 1),
            )
        keep = jnp.where(pair == inner, 1.0, 0.0)
        values = [
            jnp.where(pair == ahead, 1.0, 0.0),
            jnp.where(own_edge == ahead, 1.0, 0.0),
            jnp.where(lead == 0, keep, 1.0),
            jnp.where(lead == 0, 1.0, 0.0),
            jnp.where(lead == 0, 1.0, keep),
        ]
        for i, value in enumerate(values):
            mask_ref[i, m * head_width : (m + 1) * head_width, :] = jnp.full(
                (head_width, wide), value
            )
            tail = slice(micro_count * head_width, height)
            row = lax.broadcasted_iota(jnp.int32, (height - tail.start, wide), 0)
            before = jnp.zeros(row.shape, single) if m == 0 else mask_ref[i, tail, :]
            mask_ref[i, tail, :] = jnp.where(lax.rem(row, micro_count) == m, value, before)


CHAIN_RING = 4
LATER = 2


class Chain:
    def __init__(self, reverse, count, carry, onward, aside, beside, mask, sems):
        self.carry, self.onward, self.aside, self.beside = carry, onward, aside, beside
        self.mask, self.sems = mask, sems
        place, self.column = (lax.axis_index("seq"), lax.axis_index("batch"))
        high, low = (place // 2, lax.rem(place, 2))
        length = count // 2
        self.lap = length - 1 - high if reverse else high
        self.ahead, self.behind = (place - 2, place + 2) if reverse else (place + 2, place - 2)
        self.partner = place + 1 - 2 * low
        self.first, self.final = (self.lap == 0, self.lap == length - 1)

    def greet(self, barrier):
        def signal(place):
            pl.semaphore_signal(
                barrier, inc=1, device_id=(place, self.column), device_id_type=MESH
            )

        signal(self.partner)

        @pl.when(jnp.logical_not(self.final))
        def _():
            signal(self.ahead)

        @pl.when(jnp.logical_not(self.first))
        def _():
            signal(self.behind)

        return 1 + jnp.where(self.first, 0, 1) + jnp.where(self.final, 0, 1)

    def along(self, i):
        return pltpu.make_async_remote_copy(
            src_ref=self.onward.at[lax.rem(i, CHAIN_RING)], dst_ref=self.carry.at[i], send_sem=self.sems[0].at[i],
            recv_sem=self.sems[1].at[i], device_id=(self.ahead, self.column), device_id_type=MESH,
        )

    def across(self, i):
        return pltpu.make_async_remote_copy(
            src_ref=self.aside.at[lax.rem(i, CHAIN_RING)], dst_ref=self.beside.at[i], send_sem=self.sems[2].at[i],
            recv_sem=self.sems[3].at[i], device_id=(self.partner, self.column),
            device_id_type=MESH,
        )

    def start(self):
        @pl.when(self.first)
        def _():
            self.carry[...] = jnp.zeros_like(self.carry)

    def step(self, i, local):
        @pl.when(jnp.logical_not(self.first))
        def _():
            self.along(i).wait_recv()

        @pl.when(i >= CHAIN_RING)
        def _():
            self.sent(i - CHAIN_RING)

        state, slot = (self.carry[i], lax.rem(i, CHAIN_RING))

        @pl.when(jnp.logical_not(self.final))
        def _():
            self.onward[slot] = self.mask[0] * state + self.mask[1] * local
            self.along(i).start()

        self.aside[slot] = self.mask[2] * state + self.mask[3] * local
        self.across(i).start()

    def sent(self, i):
        self.across(i).wait_send()

        @pl.when(jnp.logical_not(self.final))
        def _():
            self.along(i).wait_send()

    def result(self, i):
        self.across(i).wait_recv()
        return self.mask[4] * self.carry[i] + self.beside[i]

    def drain(self, chunks):
        def one(i, _):
            self.sent(i)
            return 0

        lax.fori_loop(max(chunks - CHAIN_RING, 0), chunks, one, 0)


def local_state(wide, other, micro_count, head_width, target):
    rows = wide.shape[1] // micro_count
    sums = []
    for m in range(micro_count):
        part = slice(m * rows, (m + 1) * rows)
        local = matmul(wide[:, part], other[:, part], (1, 1))
        target[m * head_width : (m + 1) * head_width, :] = local[:head_width]
        sums.append(local[head_width : head_width + 1])
    target[micro_count * head_width :, :] = jnp.concatenate(sums + sums, axis=0)


def forward_kernel(
    count, micro_count, x_ref, gain_ref, shift_ref, weight_hbm, bias_ref, qm_ref, km_ref,
    bounds_ref, proj_out, fq_out, fk_out, state_out, att_out, low_out, den_out, norm_out,
    turned_out, weight_ref, proj_ref, fq_ref, fk_ref, state_ref, att_ref, low_ref, den_ref,
    norm_ref, turned_ref, out_sem, whole_sem, normed, bias_row, mask, use, last, chain_mask, local, carry, onward, aside, beside, *sems,
):
    heads, head_width = qm_ref.shape[:2]
    total_rows = x_ref.shape[0]
    rows = total_rows // micro_count
    model_width = x_ref.shape[1]
    pair = 2 * head_width
    place = lax.axis_index("seq")
    first_row = place * rows
    chain = Chain(False, count, carry, onward, aside, beside, chain_mask, sems)
    weight_copy = pltpu.make_async_copy(weight_hbm, weight_ref, whole_sem.at[0])
    weight_copy.start()
    turned_copies = [
        pltpu.make_async_copy(norm_ref, norm_out, whole_sem.at[1]),
        pltpu.make_async_copy(turned_ref, turned_out, whole_sem.at[2]),
    ]

    def outward(h):
        pairs = [(proj_ref.at[p * heads + h], proj_out.at[p * heads + h]) for p in range(3)]
        for source, target in (
            (fq_ref, fq_out), (fk_ref, fk_out), (state_ref, state_out), (att_ref, att_out),
            (low_ref, low_out), (den_ref, den_out),
        ):
            pairs.append((source.at[h], target.at[h]))
        return [
            pltpu.make_async_copy(source, target, out_sem.at[h, i])
            for i, (source, target) in enumerate(pairs)
        ]

    barrier = pltpu.get_barrier_semaphore()
    greeted = chain.greet(barrier)
    token_masks(bounds_ref, first_row, rows, micro_count, mask, use, last)
    chain_masks(
        bounds_ref, first_row, lax.rem(place, 2), rows, micro_count, head_width, False, chain_mask
    )
    chain.start()
    bias_row[...] = flat(bias_ref[...])
    normed[...] = norm_forward(
        x_ref[...].astype(single), flat(gain_ref[...]), flat(shift_ref[...])
    )[0].astype(bfloat)
    pl.semaphore_wait(barrier, greeted)
    norm_ref[...] = normed[...].T
    turned_ref[...] = x_ref[...].T
    for copy in turned_copies:
        copy.start()
    weight_copy.wait()

    def project(p):
        for part in range(3):
            columns = pl.ds(pl.multiple_of(part * model_width + p * pair, pair), pair)
            value = matmul(normed[...], weight_ref[:, columns], (1, 0))
            value = (value + bias_row[:, columns]).astype(bfloat).T
            proj_ref[part * heads + 2 * p] = value[:head_width]
            proj_ref[part * heads + 2 * p + 1] = value[head_width:]

    def features(h):
        for offset, weights, target in ((0, qm_ref, fq_ref), (heads, km_ref, fk_ref)):
            mapped = matmul(weights[h], proj_ref[offset + h], (0, 0))
            up, down = two_softmaxes(mapped)
            target[h] = jnp.concatenate([up, down], axis=0).astype(bfloat)
        wide = with_ones(proj_ref[2 * heads + h]) * last[...].astype(bfloat)
        local_state(wide, fk_ref.at[h], micro_count, head_width, local.at[h])

    def attend(h):
        state_ref[h] = chain.result(h)
        wide = with_ones(proj_ref[2 * heads + h])
        used = fq_ref[h] * use[...].astype(bfloat)
        for m in range(micro_count):
            part = slice(m * rows, (m + 1) * rows)
            scores = matmul(fk_ref[h, :, part], fq_ref[h, :, part], (0, 0)) * mask[m]
            state = state_rows(state_ref.at[h], m, micro_count, head_width).astype(bfloat)
            numer = matmul(wide[:, part], scores.astype(bfloat), (1, 0)) + matmul(
                state, used[:, part], (1, 0)
            )
            denom = numer[head_width : head_width + 1]
            attended = numer[:head_width] / denom
            att_ref[h, :, part] = attended
            low_ref[h, :, part] = attended.astype(bfloat)
            den_ref[h, :, part] = denom

    def one_round(r, _):
        @pl.when((r >= chain.lap) & (r < heads + chain.lap) & jnp.logical_not(chain.first))
        def _():
            chain.step(r - chain.lap, local[r - chain.lap])

        @pl.when((r < heads) & (lax.rem(r, 2) == 0))
        def _():
            project(r // 2)

        @pl.when(r < heads)
        def _():
            features(r)

        @pl.when((r >= chain.lap) & (r < heads + chain.lap) & chain.first)
        def _():
            chain.step(r - chain.lap, local[r - chain.lap])

        @pl.when(r >= chain.lap + 1)
        def _():
            attend(r - chain.lap - 1)
            for copy in outward(r - chain.lap - 1):
                copy.start()

        @pl.when(r >= chain.lap + 1 + LATER)
        def _():
            for copy in outward(r - chain.lap - 1 - LATER):
                copy.wait()

        return 0

    lax.fori_loop(0, heads + chain.lap + 1, one_round, 0)
    chain.drain(heads)

    def arrived(h, _):
        for copy in outward(h):
            copy.wait()
        return 0

    lax.fori_loop(heads - LATER, heads, arrived, 0)
    for copy in turned_copies:
        copy.wait()


def forward_attention(x, gain, shift, weight, bias, query_map, key_map, bounds, count):
    total_rows, model_width = x.shape
    heads, head_width = query_map.shape[:2]
    micro_count = bounds.shape[0]
    rows = total_rows // micro_count
    height = micro_count * (head_width + 2)
    chunk = (heads, height, 2 * head_width)
    whole = pl.BlockSpec(memory_space=pltpu.VMEM)
    head = (heads, head_width, total_rows)
    feat = (heads, 2 * head_width, total_rows)
    shape = jax.ShapeDtypeStruct
    results = [
        shape((3 * heads,) + head[1:], bfloat), shape(feat, bfloat), shape(feat, bfloat),
        shape(chunk, single), shape(head, single), shape(head, bfloat),
        shape((heads, 1, total_rows), single), shape((model_width, total_rows), bfloat),
        shape((model_width, total_rows), bfloat),
    ]
    anywhere = pl.BlockSpec(memory_space=pl.ANY)
    DMA = pltpu.SemaphoreType.DMA
    return pl.pallas_call(
        partial(forward_kernel, count, micro_count),
        out_shape=results,
        in_specs=[whole] * 3
        + [anywhere]
        + [whole] * 3
        + [pl.BlockSpec(memory_space=pltpu.SMEM)],
        out_specs=[anywhere] * 9,
        scratch_shapes=[pltpu.VMEM(weight.shape, bfloat)]
        + [pltpu.VMEM(result.shape, result.dtype) for result in results]
        + [
            DMA((heads, 9)),
            DMA((3,)),
            pltpu.VMEM((total_rows, model_width), bfloat),
            pltpu.VMEM((1, 3 * model_width), single),
            pltpu.VMEM((micro_count, rows, rows), single),
            pltpu.VMEM((1, total_rows), single),
            pltpu.VMEM((1, total_rows), single),
            pltpu.VMEM((5,) + chunk[1:], single),
        ]
        + [pltpu.VMEM(chunk, single)] * 2
        + [pltpu.VMEM((CHAIN_RING,) + chunk[1:], single)] * 2
        + [pltpu.VMEM(chunk, single)]
        + [DMA((heads,))] * 4,
        compiler_params=pltpu.CompilerParams(
            collective_id=1, has_side_effects=True, vmem_limit_bytes=VMEM_LIMIT
        ),
    )(
        x, gain, shift, weight, bias, query_map, key_map, bounds.T,
    )


def remote(src, dst, send, recv, device):
    return pltpu.make_async_remote_copy(
        src_ref=src, dst_ref=dst, send_sem=send, recv_sem=recv, device_id=device,
        device_id_type=MESH,
    )


PIECES, PIECE_ROWS = (2, (1, 2))


class Spot:
    def __init__(self, count, lines):
        self.place, self.column = (lax.axis_index("seq"), lax.axis_index("batch"))
        self.high, self.low = (self.place // 2, lax.rem(self.place, 2))
        self.across, self.core = (self.column // 2, lax.rem(self.column, 2))
        self.length, self.lines = (count // 2, lines)
        self.at_core = (self.place, self.column + 1 - 2 * self.core)
        self.at_y = (self.place + 1 - 2 * self.low, self.column)
        self.at_right, self.at_left = ((self.place + 2, self.column), (self.place - 2, self.column))
        self.not_first, self.not_last = (self.high > 0, self.high < self.length - 1)

    def line(self, d):
        other = lax.rem(self.across + d, self.lines)
        return other, (self.place, other * 2 + self.core)

    def along(self, d):
        count = 2 * self.length
        other = lax.rem(self.place + d, count)
        return other, (other, self.column)

    def greet(self, barrier):
        devices = [self.at_core]
        devices += [self.line(d)[1] for d in range(1, self.lines)]
        devices += [self.along(d)[1] for d in range(1, 2 * self.length)]
        for device in devices:
            pl.semaphore_signal(barrier, inc=1, device_id=device, device_id_type=MESH)
        return len(devices)


class Track:
    def __init__(
        self, spot, base, halved, rows, offset, stride, ring, out, own, got, y_got, z_got, x_got,
        sems,
    ):
        self.base, self.stride = (base, stride)
        self.spot, self.halved, self.rows, self.offset, self.ring = spot, halved, rows, offset, ring
        self.out, self.own, self.got, self.y_got, self.z_got, self.x_got = (
            out, own, got, y_got, z_got, x_got,
        )
        (
            self.load_sem, self.core_send, self.core_recv, self.y_send, self.y_recv, self.zr_send,
            self.zr_recv, self.zl_send, self.zl_recv, self.x_send, self.x_recv, self.back_send,
            self.back_recv,
        ) = sems
        half = own.shape[-1]
        self.mine = pl.ds(pl.multiple_of(spot.core * half, 128), half)
        self.theirs = pl.ds(pl.multiple_of((1 - spot.core) * half, 128), half)
        self.part = rows // spot.lines if halved else rows
        self.strip = self.window(spot.across) if halved else slice(None)

    def row(self, u):
        return pl.multiple_of(self.offset + u * self.stride, 8) if self.stride else self.offset

    def seat(self, u):
        return self.base if self.stride else self.base + u

    def window(self, line, base=0):
        return pl.ds(pl.multiple_of(base + line * self.part, 8), self.part)

    def source(self, u, ref, col, columns):
        half = self.own.shape[-1]
        cols = pl.ds(pl.multiple_of(col + columns * half, 128), half)
        return ref.at[:, :, pl.ds(self.row(u), self.rows), cols]

    def give(self, u, source):
        return remote(
            source, self.got.at[lax.rem(u, self.ring)], self.core_send.at[u],
            self.core_recv.at[u], self.spot.at_core,
        )

    def begin(self, u, ref, col):
        self.give(u, self.source(u, ref, col, 1 - self.spot.core)).start()
        pltpu.make_async_copy(
            self.source(u, ref, col, self.spot.core), self.own.at[u], self.load_sem.at[u]
        ).start()

    def settle(self, u):
        pltpu.make_async_copy(self.own.at[u], self.own.at[u], self.load_sem.at[u]).wait()
        self.give(u, self.own.at[u]).wait_recv()
        self.own[u] = self.own[u] + self.got[lax.rem(u, self.ring)]

    def given(self, u):
        self.give(u, self.own.at[u]).wait_send()

    def cut(self, u, d):
        other, device = self.spot.line(d)
        return remote(
            self.own.at[u, :, :, self.window(other)], self.x_got.at[u, d - 1],
            self.x_send.at[u, 0, d - 1], self.x_recv.at[u, 0, d - 1], device,
        )

    def first(self, u):
        self.settle(u)
        if self.halved:
            for d in range(1, self.spot.lines):
                self.cut(u, d).start()
        else:
            self.y_copy(u).start()

    def cut_taken(self, u):
        for d in range(1, self.spot.lines):
            self.cut(u, d).wait_recv()
            target = self.own.at[u, :, :, self.strip]
            target[...] = target[...] + self.x_got[u, d - 1]
        self.y_copy(u).start()

    def y_copy(self, u):
        return remote(
            self.own.at[u, :, 1 - self.spot.low, self.strip], self.y_got.at[u],
            self.y_send.at[u], self.y_recv.at[u], self.spot.at_y,
        )

    def y_taken(self, u):
        self.y_copy(u).wait_recv()
        target = self.own.at[u, :, self.spot.low, self.strip]
        target[...] = target[...] + self.y_got[u]
        self.z_step(u, 1)

    def block(self, u, h):
        return self.own.at[u, h, self.spot.low, self.strip]

    def right(self, u, k):
        return remote(
            self.block(u, k), self.z_got.at[u, k], self.zr_send.at[u, k], self.zr_recv.at[u, k],
            self.spot.at_right,
        )

    def left(self, u, k, taker):
        slot = jnp.where(k == taker, self.spot.length, k)
        return remote(
            self.block(u, k), self.z_got.at[u, slot], self.zl_send.at[u, k], self.zl_recv.at[u, k],
            self.spot.at_left,
        )

    def take_right(self, u, k):
        self.right(u, k).wait_recv()
        target = self.block(u, k)
        target[...] = target[...] + self.z_got[u, k]

    def take_left(self, u, k):
        high = self.spot.high
        self.left(u, k, high).wait_recv()
        target = self.block(u, k)
        target[...] = target[...] + self.z_got[u, jnp.where(k == high, self.spot.length, k)]

    def z_step(self, u, t):
        spot = self.spot
        k = spot.high + spot.length - t

        @pl.when(spot.high <= t - 1)
        def _():
            if t > 1:
                @pl.when(spot.not_first)
                def _():
                    self.take_right(u, k)

            self.right(u, k).start()

        j = spot.high - spot.length + t

        @pl.when(spot.high >= spot.length - t)
        def _():
            if t > 1:
                @pl.when(spot.not_last)
                def _():
                    self.take_left(u, j)

            self.left(u, j, spot.high - 1).start()

    def z_end(self, u):
        @pl.when(self.spot.not_first)
        def _():
            self.take_right(u, self.spot.high)

        @pl.when(self.spot.not_last)
        def _():
            self.take_left(u, self.spot.high)

    def x_copy(self, u, d):
        return remote(
            self.block(u, self.spot.high), self.x_got.at[u, d - 1], self.x_send.at[u, 0, d - 1],
            self.x_recv.at[u, 0, d - 1], self.spot.line(d)[1],
        )

    def x_back(self, u, d):
        rows = self.window(self.spot.across, self.row(u))
        return remote(
            self.block(u, self.spot.high), self.out.at[self.seat(u), rows, self.mine],
            self.x_send.at[u, 1, d - 1], self.x_recv.at[u, 1, d - 1], self.spot.line(d)[1],
        )

    def keep(self, u):
        rows = (
            self.window(self.spot.across, self.row(u))
            if self.halved
            else pl.ds(self.row(u), self.rows)
        )
        return pltpu.make_async_copy(
            self.block(u, self.spot.high), self.out.at[self.seat(u), rows, self.mine], self.load_sem.at[u]
        )

    def reduced(self, u):
        self.z_end(u)
        if self.halved:
            self.keep(u).start()
        for d in range(1, self.spot.lines):
            (self.x_back if self.halved else self.x_copy)(u, d).start()

    def back(self, u):
        block = self.out.at[self.seat(u), pl.ds(self.row(u), self.rows), self.mine]
        source = block if self.halved else self.block(u, self.spot.high)
        return remote(source, block, self.back_send.at[u], self.back_recv.at[u], self.spot.at_core)

    def total(self, u):
        spot = self.spot
        for d in range(1, spot.lines):
            self.x_copy(u, d).wait()
        value = self.block(u, spot.high)[...]
        if spot.lines == 2:
            value = value + self.x_got[u, 0]
        else:
            parts = []
            for x in range(spot.lines):
                slot = lax.rem(spot.across - x + spot.lines - 1, spot.lines)
                slot = jnp.minimum(slot, spot.lines - 2)
                parts.append(jnp.where(x == spot.across, value, self.x_got[u, slot]))
            value = sum(parts[1:], parts[0])
        self.block(u, spot.high)[...] = value

    def done(self, u):
        if self.halved:
            for d in range(1, self.spot.lines):
                self.x_back(u, d).wait_recv()
            self.keep(u).wait()
        else:
            self.total(u)
            self.keep(u).start()
        self.back(u).start()

    def finish(self, u):
        self.back(u).wait()
        if not self.halved:
            self.keep(u).wait()

    def steps(self):
        z_steps = [partial(self.z_step, t=t) for t in range(2, self.spot.length)]
        cut = [self.cut_taken] if self.halved else []
        return [self.first] + cut + [self.y_taken] + z_steps + [self.reduced, self.done]

    def drain(self, u):
        self.y_copy(u).wait_send()
        for d in range(1, self.spot.lines):
            if self.halved:
                self.cut(u, d).wait_send()
                self.x_back(u, d).wait_send()

        def right_one(k, _):
            self.right(u, k).wait_send()
            return 0

        def left_one(k, _):
            self.left(u, k, self.spot.high - 1).wait_send()
            return 0

        lax.fori_loop(self.spot.high + 1, self.spot.length, right_one, 0)
        lax.fori_loop(0, self.spot.high, left_one, 0)


def bands(units, share, lines):
    third, rows = (share // 3, share // PIECES)
    fits = [third % 8, 2 * third % (8 * lines), share % 3, share % PIECES]
    direct = rows * PIECE_ROWS[0] // sum(PIECE_ROWS)
    fits += [direct % 8, (rows - direct) % (8 * lines)]
    if any(fits):
        return [(0, units, share, 0, 0)]
    return [
        (0, units - 1, third, 2 * third, 0),
        (units - 1, units - 1 + PIECES, direct, rows - direct, rows),
    ]


def track_scratch(units, length, lines, rows, halved, ring, half):
    part = rows // lines if halved else rows
    DMA = pltpu.SemaphoreType.DMA
    others = lines - 1
    buffers = [
        pltpu.VMEM((units, length, 2, rows, half), single),
        pltpu.VMEM((ring, length, 2, rows, half), single),
        pltpu.VMEM((units, length, part, half), single),
        pltpu.VMEM((units, length + 1, part, half), single),
        pltpu.VMEM((units, others) + ((length, 2) if halved else ()) + (part, half), single),
    ]
    line = DMA((units, length))
    ends = DMA((units, 2, others))
    one = DMA((units,))
    return buffers + [one] * 5 + [line] * 4 + [ends] * 2 + [one] * 2


BEAT = 2


def unit_order(early, late, gap, length):
    order, starts, left = ([], [], list(range(early)))
    ready = {length + 2 + gap * g: early + g for g in range(late)}
    t = 0
    while len(order) < early + late:
        if t in ready or left:
            order.append(ready[t] if t in ready else left.pop(0))
            starts.append(t)
        t += 1
    return order, starts


def backward_kernel(
    count, lines, micro_count, early, proj_hbm, fq_hbm, fk_hbm, state_hbm, att_hbm, den_hbm,
    grad_hbm, qm_ref, km_ref, norm_hbm, weight_hbm, x_hbm, mid_hbm, gain_ref, vector_ref,
    bounds_ref, contract_ref, expand_ref, output_ref, out, in_grad_ref, qm_out, km_out, rows_out, bias_out, expand_bias_out,
    norm_ref, weight_ref, x_ref, mid_ref, whole_sem, proj, fq_buf, fk_buf, state_buf, att_buf, den_buf, grad_buf, load_sem, pg_ref,
    mask, use, last, chain_mask, local, carry, onward, aside, beside, fqg, fkg, product, small,
    small_sum, small_out, gather_send, gather_recv, gather_keep, credit, *rest,
):
    heads, head_width = qm_ref.shape[:2]
    total_rows = pg_ref.shape[-1]
    rows = total_rows // micro_count
    model_width = heads * head_width
    sources = (contract_ref, expand_ref, output_ref)
    share, wide = out.shape[1:]
    group = wide // (3 * head_width)
    late = heads // group
    units = len(early) + late
    spot = Spot(count, lines)
    length = spot.length
    order, starts = unit_order(len(early), late, group // BEAT, length)
    plan = bands(units, share, lines)
    order = order + order[-1:] * (plan[-1][1] - units)
    starts = starts + [starts[-1] + 1 + i for i in range(plan[-1][1] - units)]
    units = len(order)
    chain_sems, rest = (rest[:4], rest[4:])
    chain = Chain(True, count, carry, onward, aside, beside, chain_mask, chain_sems)
    ring, half = (2, wide // 2)
    little = Track(spot, 0, False, small.shape[2], 0, 0, 1, small_sum, *rest[:5], rest[5:18])
    rest = rest[18:]
    groups = []
    for low, high, direct, halved, stride in plan:
        group_tracks = []
        for kind, band, offset in ((False, direct, 0), (True, halved, direct)):
            if band:
                group_tracks.append(
                    Track(spot, low, kind, band, offset, stride, ring, out, *rest[:5], rest[5:18])
                )
                rest = rest[18:]
        groups.append((low, high, group_tracks))
    slots = proj.shape[0]

    def loads(h):
        slot = lax.rem(h, slots)
        pairs = [(proj_hbm.at[:, h], proj.at[slot])]
        for source, target in (
            (fq_hbm, fq_buf), (fk_hbm, fk_buf), (state_hbm, state_buf), (att_hbm, att_buf),
            (den_hbm, den_buf), (grad_hbm, grad_buf),
        ):
            pairs.append((source.at[h], target.at[slot]))
        return [
            pltpu.make_async_copy(source, target, load_sem.at[slot, i])
            for i, (source, target) in enumerate(pairs)
        ]

    for h in range(BEAT):
        for copy in loads(h):
            copy.start()
    whole_copies = [
        pltpu.make_async_copy(source, target, whole_sem.at[i])
        for i, (source, target) in enumerate(
            ((norm_hbm, norm_ref), (weight_hbm, weight_ref), (x_hbm, x_ref), (mid_hbm, mid_ref))
        )
    ]
    for copy in whole_copies:
        copy.start()
    barrier = pltpu.get_barrier_semaphore()
    greeted = spot.greet(barrier)
    pl.semaphore_wait(barrier, greeted)

    def tracks_of(u):
        return [t for low, high, tracks in groups for t in tracks if low <= u < high]

    def begin(u):
        if u >= ring:
            pl.semaphore_wait(credit, 1)
        if order[u] < len(early):
            array, lead, col = early[order[u]]
            ref = sources[array]
            ref = ref if lead is None else ref.at[:, :, lead]
        else:
            ref, col = (product, 0)
        for track in tracks_of(u):
            track.begin(u - track.base, ref, col)

    def settled(u):
        @pl.when(u + ring < units)
        def _():
            pl.semaphore_signal(credit, inc=1, device_id=spot.at_core, device_id_type=MESH)

    def state_grad(h):
        for copy in loads(h):
            copy.wait()
        slot = lax.rem(h, slots)
        wide_grad = score_grads(grad_buf[slot], att_buf[slot], den_buf[slot]) * use[...]
        local_state(wide_grad.astype(bfloat), fq_buf.at[slot], micro_count, head_width, local)

    def attend_back(h):
        slot = lax.rem(h, slots)
        beside[h] = chain.result(h)
        grads = score_grads(grad_buf[slot], att_buf[slot], den_buf[slot])
        low_grads = grads.astype(bfloat)
        used_grads = (grads * use[...]).astype(bfloat)
        last_low = last[...].astype(bfloat)
        wide_value = with_ones(proj[slot, 2])
        wide_last = wide_value * last_low
        for m in range(micro_count):
            part = slice(m * rows, (m + 1) * rows)
            fq, fk = (fq_buf[slot, :, part], fk_buf[slot, :, part])
            scores = (matmul(fk, fq, (0, 0)) * mask[m]).astype(bfloat)
            grad_scores = (
                matmul(wide_value[:, part], low_grads[:, part], (0, 0)) * mask[m]
            ).astype(bfloat)
            state = state_rows(state_buf.at[slot], m, micro_count, head_width).astype(bfloat)
            out_grad = state_rows(beside.at[h], m, micro_count, head_width)
            row = lax.broadcasted_iota(jnp.int32, out_grad.shape, 0)
            out_grad = jnp.where(row <= head_width, out_grad, 0.0).astype(bfloat)
            fqg[:, part] = matmul(fk, grad_scores, (1, 0)) + matmul(
                state, used_grads[:, part], (0, 0)
            )
            fkg[:, part] = matmul(fq, grad_scores, (1, 1)) + matmul(
                out_grad, wide_last[:, part], (0, 0)
            )
            value_grad = matmul(low_grads[:head_width, part], scores, (1, 1)) + matmul(
                out_grad[:head_width], fk * last_low[:, part], (1, 0)
            )
            pg_ref[2, h, :, part] = value_grad.astype(bfloat)
        q_grad, qmg = feature_backward(fqg[...], proj[slot, 0], qm_ref[h])
        pg_ref[0, h] = q_grad.astype(bfloat)
        qm_out[h] = qmg
        k_grad, kmg = feature_backward(fkg[...], proj[slot, 1], km_ref[h])
        pg_ref[1, h] = k_grad.astype(bfloat)
        km_out[h] = kmg

    def late_begin(g):
        if g > 0:
            u = order.index(len(early) + g - 1)
            for track in tracks_of(u):
                track.given(u - track.base)
        columns = group * head_width
        for p in range(3):
            low = pg_ref[p, g * group : (g + 1) * group].reshape(columns, -1)
            value = matmul(norm_ref[...], low, (1, 1))
            product[:, :, :, p * columns : (p + 1) * columns] = value.reshape(
                product.shape[:3] + (columns,)
            )
        begin(order.index(len(early) + g))

    def input_back():
        gain_sum, bias_sum = (0.0, 0.0)
        gain = jnp.broadcast_to(flat(gain_ref[...]), (128, model_width)).T[:, :1]
        step = 2 * rows
        for start in range(0, total_rows, step):
            part = slice(start, start + step)
            grad = sum(
                matmul(
                    weight_ref[:, p * model_width : (p + 1) * model_width],
                    pg_ref[p, :, :, part].reshape(model_width, step), (1, 0),
                )
                for p in range(3)
            )
            value = x_ref[:, part].astype(single)
            value = value - jnp.mean(value, axis=0, keepdims=True)
            inverse = lax.rsqrt(jnp.mean(value * value, axis=0, keepdims=True) + epsilon)
            value = value * inverse
            inner = grad * gain
            result = mid_ref[:, part] + inverse * (
                inner
                - jnp.mean(inner, axis=0, keepdims=True)
                - value * jnp.mean(inner * value, axis=0, keepdims=True)
            )
            in_grad_ref[part, :] = result.T.astype(bfloat)
            gain_sum += jnp.sum((grad * value).T, axis=0, keepdims=True)
            bias_sum += jnp.sum(grad.T, axis=0, keepdims=True)
        ones = jnp.ones((16, total_rows), bfloat)
        sums = [
            matmul(ones, pg_ref[p].reshape(model_width, total_rows), (1, 1))[:1] for p in range(3)
        ]
        blank = jnp.zeros((4, model_width), single)
        vectors = vector_ref[...] + jnp.concatenate(
            [gain_sum, bias_sum, blank] + sums + [blank, blank[:3]], axis=0
        )
        maps = [
            jnp.concatenate([ref[h] for h in range(heads)], axis=1) for ref in (qm_out, km_out)
        ]
        size = small.shape[0] * small.shape[1] * small.shape[2]
        used = 2 * head_width + vectors.shape[0]
        pad = [jnp.zeros((size - used, model_width), single)] if size > used else []
        small[...] = jnp.concatenate(maps + [vectors] + pad, axis=0).reshape(small.shape)
        little.begin(0, small, 0)

    def spread(d, incoming):
        there, device = spot.along(d)
        place = there if incoming else spot.place
        return remote(
            little.block(0, spot.high), small_out.at[place, :, little.mine],
            gather_send.at[d - 1], gather_recv.at[place], device,
        )

    def spread_core():
        block = small_out.at[:, :, little.mine]
        return remote(block, block, gather_keep.at[1], gather_keep.at[2], spot.at_core)

    def spread_keep():
        return pltpu.make_async_copy(
            little.block(0, spot.high), small_out.at[spot.place, :, little.mine],
            gather_keep.at[0],
        )

    def little_done(u):
        little.total(u)
        spread_keep().start()
        for d in range(1, count):
            spread(d, False).start()

    def little_gather(u):
        spread_keep().wait()
        for d in range(1, count):
            spread(d, True).wait_recv()
        spread_core().start()

    little_steps = little.steps()[:-1] + [little_done, little_gather]
    lent = [order.index(len(early) + g) for g in range(late - 1)]

    def settle_all(track, v):
        track.finish(v)
        track.drain(v)
        u = v + track.base
        waited = False
        for k in lent:
            waited = waited | (u == k)

        @pl.when(jnp.logical_not(waited))
        def _():
            track.given(v)

    stages = [
        (s, f, low, high)
        for low, high, tracks in groups
        for track in tracks
        for s, f in enumerate(track.steps() + [partial(settle_all, track)])
    ]
    stages.sort(key=lambda s: (s[0], s[2]))
    ahead = 1
    for u in range(ahead):
        begin(u)
    first_row = spot.place * rows
    token_masks(bounds_ref, first_row, rows, micro_count, mask, use, last)
    chain_masks(
        bounds_ref, first_row, spot.low, rows, micro_count, head_width, True, chain_mask
    )
    chain.start()

    def unit_at(t):
        if starts == list(range(units)):
            return t, (t >= 0) & (t < units)
        u, valid = (0, False)
        for start in starts:
            u = u + jnp.where(t > start, 1, 0)
            valid = valid | (t == start)
        return u, valid

    beats = heads // BEAT

    for copy in whole_copies:
        copy.wait()

    def one_round(r, _):
        c = r - chain.lap

        @pl.when((c >= 0) & (c < beats))
        def _():
            for i in range(BEAT):
                h = c * BEAT + i
                state_grad(h)
                chain.step(h, local[...])

        for u in range(ahead, units):
            if order[u] < len(early):
                @pl.when(r == starts[u] - ahead)
                def _(u=u):
                    begin(u)

        for lag, step, low, high in stages:
            u, valid = unit_at(r - lag)

            @pl.when(valid & (u >= low) & (u < high))
            def _(u=u, step=step, low=low):
                step(u - low)

        u, valid = unit_at(r)

        @pl.when(valid)
        def _():
            settled(u)

        for s, step in enumerate(little_steps):
            @pl.when(r == beats + length + 1 + s)
            def _(step=step):
                step(0)

        @pl.when((c >= 1) & (c <= beats))
        def _():
            for i in range(BEAT):
                attend_back((c - 1) * BEAT + i)

        @pl.when((c >= 0) & (c + 1 < beats))
        def _():
            for i in range(BEAT):
                for copy in loads((c + 1) * BEAT + i):
                    copy.start()

        for g in range(late):
            u = order.index(len(early) + g)

            @pl.when(r == starts[u] - 1)
            def _(g=g):
                late_begin(g)

        @pl.when(r == beats + length)
        def _():
            input_back()

        return 0

    rounds = max(starts[-1] + stages[-1][0] + 1, beats + length + 1 + len(little_steps))
    lax.fori_loop(0, rounds, one_round, 0)

    chain.drain(heads)
    little.drain(0)
    little.given(0)
    for d in range(1, count):
        spread(d, False).wait_send()
    spread_core().wait()

    sums = small_out[...].reshape(-1, model_width)
    for h in range(heads):
        part = slice(h * head_width, (h + 1) * head_width)
        qm_out[h] = sums[:head_width, part]
        km_out[h] = sums[head_width : 2 * head_width, part]
    row = 2 * head_width
    rows_out[...] = sums[row : row + 8]
    row += 6
    for target in (bias_out, expand_bias_out):
        for start in range(0, target.shape[0], model_width):
            target[start : start + model_width] = sums[row]
            row += 1


def backward_attention(
    projected, feat_query, feat_key, state_in, attended, denominator, attended_grad, query_map,
    key_map, normed_rows, weight, input_rows, middle_grad_rows, gain, vectors, bounds,
    contract_grad, expand_grad, output_grad, count, lines,
):
    heads, head_width = query_map.shape[:2]
    model_width, total_rows = normed_rows.shape
    micro_count = bounds.shape[0]
    rows = total_rows // micro_count
    length = count // 2
    share = model_width // count
    chunk = state_in.shape
    early = [(0, u, 0) for u in range(contract_grad.shape[2])]
    early += [(1, None, c) for c in range(0, expand_grad.shape[3], model_width)]
    early += [(2, None, 0)]
    units = len(early) + 3
    shape = jax.ShapeDtypeStruct
    whole = pl.BlockSpec(memory_space=pltpu.VMEM)
    anywhere = pl.BlockSpec(memory_space=pl.ANY)
    DMA = pltpu.SemaphoreType.DMA
    half = model_width // 2
    used = 2 * head_width + vectors.shape[0]
    little = -(-used // (8 * count)) * 8
    tracks = track_scratch(1, length, lines, little, False, 1, half)
    for low, high, direct, halved, _ in bands(units, share, lines):
        for kind, band in ((False, direct), (True, halved)):
            if band:
                tracks += track_scratch(high - low, length, lines, band, kind, 2, half)
    slots = 2 * BEAT
    head, feat = ((slots, head_width, total_rows), (slots, 2 * head_width, total_rows))
    return pl.pallas_call(
        partial(backward_kernel, count, lines, micro_count, early),
        out_shape=[
            shape((units, share, model_width), single), shape((total_rows, model_width), bfloat),
            shape(query_map.shape, single), shape(key_map.shape, single),
        ]
        + [shape((8, model_width), single)]
        + [shape((3 * model_width,), single), shape((expand_grad.shape[3],), single)],
        in_specs=[anywhere] * 7
        + [whole] * 2
        + [anywhere] * 4
        + [whole] * 2
        + [pl.BlockSpec(memory_space=pltpu.SMEM)]
        + [anywhere] * 3,
        out_specs=[anywhere] + [whole] * 6,
        scratch_shapes=[
            pltpu.VMEM(normed_rows.shape, bfloat),
            pltpu.VMEM(weight.shape, bfloat),
            pltpu.VMEM(input_rows.shape, bfloat),
            pltpu.VMEM(middle_grad_rows.shape, single),
            DMA((4,)),
            pltpu.VMEM((slots, 3) + head[1:], bfloat),
            pltpu.VMEM(feat, bfloat),
            pltpu.VMEM(feat, bfloat),
            pltpu.VMEM((slots,) + chunk[1:], single),
            pltpu.VMEM(head, single),
            pltpu.VMEM((slots, 1, total_rows), single),
            pltpu.VMEM(head, single),
            DMA((slots, 7)),
            pltpu.VMEM((3, heads, head_width, total_rows), bfloat),
            pltpu.VMEM((micro_count, rows, rows), single),
            pltpu.VMEM((1, total_rows), single),
            pltpu.VMEM((1, total_rows), single),
            pltpu.VMEM((5,) + chunk[1:], single),
            pltpu.VMEM(chunk[1:], single),
        ]
        + [pltpu.VMEM(chunk, single)]
        + [pltpu.VMEM((CHAIN_RING,) + chunk[1:], single)] * 2
        + [pltpu.VMEM(chunk, single)]
        + [pltpu.VMEM(feat[1:], single)] * 2
        + [
            pltpu.VMEM((length, 2, share, model_width), single),
            pltpu.VMEM((length, 2, little, model_width), single),
            pltpu.VMEM((1, little, model_width), single),
            pltpu.VMEM((count, little, model_width), single),
            DMA((count - 1,)),
            DMA((count,)),
            DMA((3,)),
            pltpu.SemaphoreType.REGULAR,
        ]
        + [DMA((heads,))] * 4
        + tracks,
        compiler_params=pltpu.CompilerParams(
            collective_id=2, has_side_effects=True, vmem_limit_bytes=BACKWARD_LIMIT
        ),
    )(
        projected, feat_query, feat_key, state_in, attended, denominator, attended_grad, query_map,
        key_map, normed_rows, weight, input_rows, middle_grad_rows,
        gain, vectors, bounds.T, contract_grad, expand_grad,
        output_grad,
    )


def feed_kernel(
    att_ref, x_ref, grad_ref, out_weight_ref, out_bias_ref, gain_ref, shift_ref, contract_bias_ref,
    expand_ref, expand_bias_ref, contract_ref,
    result_ref, contract_grad_ref, expand_grad_ref, output_grad_ref, att_grad_ref, mid_grad_ref,
    vector_ref, unit, inverse, low, turned, total, back,
):
    step, steps = (pl.program_id(0), pl.num_programs(0))
    out_bias, gain, shift, contract_bias = (
        flat(ref[...]) for ref in (out_bias_ref, gain_ref, shift_ref, contract_bias_ref)
    )
    wide = x_ref.shape[1]
    columns = pl.ds(pl.multiple_of(step * wide, wide), wide)

    @pl.when(step == 0)
    def _():
        branch = matmul(att_ref[...], out_weight_ref[...], (0, 0)) + out_bias
        middle = x_ref[...].astype(single) + branch
        normed, unit_rows, factor = norm_forward(middle, gain, shift)
        unit[...] = unit_rows
        inverse[...] = factor
        low[...] = normed.astype(bfloat)
        turned[...] = normed.astype(bfloat).T
        total[...] = middle + contract_bias
        back[...] = jnp.zeros_like(back)
        vector_ref[...] = jnp.zeros_like(vector_ref)

    expanded = matmul(low[...], expand_ref[...], (1, 0)) + flat(expand_bias_ref[columns])
    slope = 0.7978845608028654
    square = expanded * expanded
    bend = jnp.tanh(slope * expanded * (1.0 + 0.044715 * square))
    half = 0.5 * (1.0 + bend)
    hidden = (expanded * half).astype(bfloat)
    derivative = half + expanded * (0.5 * slope) * (1.0 - bend * bend) * (
        1.0 + 3.0 * 0.044715 * square
    )
    hidden_grad = matmul(grad_ref[...], contract_ref[...], (1, 1)) * derivative
    low_grad = hidden_grad.astype(bfloat)
    total[...] += matmul(hidden, contract_ref[...], (1, 0))
    back[...] += matmul(low_grad, expand_ref[...], (1, 1))
    expand_grad_ref[...] = matmul(turned[...], low_grad, (1, 0))
    contract_grad_ref[...] = matmul(hidden, grad_ref[...], (0, 0))
    bias_sum = jnp.sum(low_grad.astype(single), axis=0, keepdims=True)
    row = lax.broadcasted_iota(jnp.int32, vector_ref.shape, 0)
    vector_ref[...] = jnp.where(row == 9 + step, bias_sum, vector_ref[...])

    @pl.when(step == steps - 1)
    def _():
        result_ref[...] = total[...].astype(bfloat)
        wide_grad = grad_ref[...].astype(single)
        mid, gain_sum, shift_sum = norm_backward(back[...], unit[...], inverse[...], gain)
        mid = wide_grad + mid
        branch = mid.astype(bfloat)
        mid_grad_ref[...] = mid.T
        att_grad_ref[...] = matmul(out_weight_ref[...], branch, (1, 1))
        output_grad_ref[...] = matmul(att_ref[...], branch, (1, 0))
        sums = [
            gain_sum[None],
            shift_sum[None],
            jnp.sum(branch.astype(single), axis=0, keepdims=True),
            jnp.sum(wide_grad, axis=0, keepdims=True),
        ]
        height, wide = vector_ref.shape
        vector_ref[...] += jnp.concatenate(
            [jnp.zeros((2, wide), single)] + sums + [jnp.zeros((height - 6, wide), single)], axis=0
        )


def feed_forward(
    att, x, grad, output_weight, output_bias, gain, shift, expand_weight, expand_bias,
    contract_weight, contract_bias,
):
    total_rows, wide = x.shape
    steps = expand_weight.shape[1] // wide
    shape = jax.ShapeDtypeStruct
    whole = pl.BlockSpec(memory_space=pltpu.VMEM)
    square = (wide, wide)
    by_row, by_column = (lambda i: (i, 0), lambda i: (0, i))
    return pl.pallas_call(
        feed_kernel,
        grid=(steps,),
        out_shape=[
            shape((total_rows, wide), bfloat), shape((steps * wide, wide), single),
            shape((wide, steps * wide), single), shape(square, single),
            shape((wide, total_rows), single), shape((wide, total_rows), single),
            shape((16, wide), single),
        ],
        in_specs=[whole] * 8
        + [pl.BlockSpec(square, by_column), whole, pl.BlockSpec(square, by_row)],
        out_specs=[
            whole, pl.BlockSpec(square, by_row), pl.BlockSpec(square, by_column), whole, whole,
            whole, whole,
        ],
        scratch_shapes=[
            pltpu.VMEM((total_rows, wide), single),
            pltpu.VMEM((total_rows, 1), single),
            pltpu.VMEM((total_rows, wide), bfloat),
            pltpu.VMEM((wide, total_rows), bfloat),
            pltpu.VMEM((total_rows, wide), single),
            pltpu.VMEM((total_rows, wide), single),
        ],
        compiler_params=pltpu.CompilerParams(vmem_limit_bytes=VMEM_LIMIT),
    )(
        att, x, grad, output_weight, output_bias, gain, shift, contract_bias, expand_weight,
        expand_bias, contract_weight,
    )


def per_device(
    inputs, gain_one, bias_one, project_weight, project_bias, query_map, key_map, output_weight,
    output_bias, gain_two, bias_two, expand_weight, expand_bias, contract_weight, contract_bias,
    bounds, cotangent,
):
    micro_count, row_count, model_width = inputs.shape
    head_count, head_width = (query_map.shape[0], query_map.shape[1])
    total_rows = micro_count * row_count
    count = lax.axis_size("seq")
    flat_input = inputs.reshape(total_rows, model_width)
    (
        projected, feat_query, feat_key, state_in, attended, attended_low, denominator,
        normed_rows, input_rows,
    ) = forward_attention(
        flat_input, gain_one, bias_one, project_weight,
        project_bias, query_map, key_map, bounds, count,
    )
    attended_low = attended_low.reshape(model_width, total_rows)

    lines = lax.axis_size("batch") // 2
    share = model_width // count
    tiles = (count // 2, 2)
    (
        block_output, contract_grad, expand_grad, output_grad, attended_grad, middle_grad_rows,
        vectors,
    ) = feed_forward(
        attended_low, flat_input, cotangent.reshape(total_rows, model_width), output_weight,
        output_bias, gain_two, bias_two, expand_weight, expand_bias, contract_weight,
        contract_bias,
    )
    contract_grad = contract_grad.reshape(
        tiles + (expand_weight.shape[1] // model_width, share, model_width)
    )
    expand_grad = expand_grad.reshape(tiles + (share, -1))
    output_grad = output_grad.reshape(tiles + (share, model_width))
    (
        totals, input_grad, query_map_grad, key_map_grad, sums, project_bias_grad,
        expand_bias_grad,
    ) = backward_attention(
        projected.reshape(3, head_count, head_width, total_rows), feat_query, feat_key, state_in,
        attended, denominator, attended_grad.reshape(head_count, head_width, total_rows),
        query_map, key_map, normed_rows, project_weight, input_rows, middle_grad_rows, gain_one,
        vectors, bounds, contract_grad, expand_grad, output_grad, count, lines,
    )
    depth = contract_grad.shape[2]
    wide = expand_weight.shape[1] // model_width
    order, _ = unit_order(depth + wide + 1, 3, head_count // 3 // BEAT, count // 2)
    at = [order.index(i) for i in range(len(order))]
    contract_total = jnp.concatenate([totals[i] for i in at[:depth]])
    expand_total = jnp.concatenate([totals[i] for i in at[depth : depth + wide]], axis=1)
    output_total = totals[at[depth + wide]]
    late = [totals[i].reshape(share, 3, -1) for i in at[depth + wide + 1 :]]
    project_total = jnp.stack(late, axis=2).reshape(share, -1)
    return (
        block_output.reshape(inputs.shape), input_grad.reshape(inputs.shape), sums[0], sums[1],
        project_total, project_bias_grad, query_map_grad, key_map_grad, output_total, sums[4],
        sums[2], sums[3], expand_total, expand_bias_grad,
        contract_total, sums[5],
    )


def solution(mesh):
    rows = P("batch", "seq", None)
    placed = (rows,) + (P(),) * 14 + (P("batch", None), rows)
    shard = P("seq", None)
    return jax.shard_map(
        per_device,
        mesh=mesh,
        in_specs=placed,
        out_specs=(
            rows, rows, P(), P(), shard, P(), P(), P(), shard, P(), P(), P(), shard, P(), shard, P(),
        ),
        check_vma=False,
    )
```
